256 devices in a mesh: lat: 4 (over x_hi, core), lon: 64 (over z, y, x_lo).
Axes of the slice: x: 4 (x_hi: 2, x_lo: 2; x = x_hi * 2 + x_lo), y: 4, z: 8, core: 2. Of those that a mesh axis runs over, the one named last changes fastest.
Arguments:
- adjoint_state: float32 [3, 1024, 32768], P(None, 'lat', 'lon'), may hold values from -6 to 6
- face_depth: float32 [2, 1024, 32768], P(None, 'lat', 'lon'), may hold values from 0.1 to 0.45
- innovation: float32 [8192, 128], P(('lat', 'lon')), may hold values from -6 to 6
- interp_weight: float32 [8192, 4, 128], P(('lat', 'lon')), may hold values from 0 to 1
- block_tile: int32 [8192, 1], P(('lat', 'lon')), may hold values from 0 to 63; in each aligned block of 32 rows (0 to 31, 32 to 63, ...) at most 2 rows name the same one
- block_count: int32 [8192, 1], P(('lat', 'lon')), may hold values from 1 to 128
- obs_row: int32 [8192, 128], P(('lat', 'lon')), may hold values from 0 to 254
- obs_col: int32 [8192, 128], P(('lat', 'lon')), may hold values from 0 to 510
Outputs:
- gradient: float32 [3, 1024, 32768], P(None, 'lat', 'lon')
The draws below stay inside these ranges and needn't reach their ends.
Inputs may be any that keep to these rules, and one draw needn't show every extreme that they name: `block_tile`: among the 32 blocks held by one device, no tile is named by more than 2 blocks, a bound that some block reaches.
All inputs are finite; a program needn't handle non-finite values.
Results may differ from the reference program's by a relative error of at most 0.00029.
Values sent between devices are 32-bit elements; how exact they have to be, the bound alone decides.
A program may use at most 64 MiB of HBM per device.

```python
import math
import jax
import jax.numpy as jnp
import numpy as np

CX = 256
CY = 512
WIN = 6
WINDOWS = 4
SLOTS = 128
BLK_DEV = 32
NX = 1024
NY = 32768
BLOCKS = 8192
CAP = 2
N_LON = 64


def with_ends(entries, key, least, high):
    longest = entries.shape.index(max(entries.shape))
    spots = []
    for shift in (0, 1):
        where = [jax.random.randint(jax.random.fold_in(key, axis), (), 0, length) for axis, length in enumerate(entries.shape)]
        where[longest] = (where[longest] + shift) % entries.shape[longest]
        spots.append(tuple(where))
    return entries.at[spots[0]].set(least).at[spots[1]].set(high)


def block_levels(stream_key, extent, split, smallest, high):
    level, own = 1.0, jax.random.fold_in(stream_key, 6)
    for axis_at, parts in split:
        draws = jnp.exp(jax.random.uniform(jax.random.fold_in(own, axis_at), (parts,), jnp.float32, smallest / len(split), high / len(split)))
        level = level * jnp.repeat(draws, extent[axis_at] // parts).reshape([-1 if axis == axis_at else 1 for axis in range(len(extent))])
    return level


def shared_out(key, own, number, rows, number_of, top, bound, slope):
    order = jax.random.permutation(key, number_of)
    packed, usual = portions_of(number_of, rows * top, bound, slope, True), portions_of(number_of, rows * top, bound, slope, False)
    places = jnp.arange(number_of)

    def named(lengths, turn):
        used = int((lengths > 0).sum())
        fixed = max(1, used // 4)
        shifted = fixed + (places - fixed + turn * (used - fixed)) % max(1, number_of - fixed)
        return jnp.zeros((number_of,), jnp.int32).at[order[jnp.where(places < fixed, places, shifted)]].set(jnp.asarray(lengths, jnp.int32))

    lengths = jnp.where(number % 4 == 0, named(packed, number // 4), named(usual, number - number // 4 - 1))
    mixed = jax.random.permutation(jax.random.fold_in(own, 3), number_of)
    giver, receiver = mixed[0:number_of // 2 * 2:2], mixed[1:number_of // 2 * 2:2]
    slack = jnp.minimum(lengths[giver] - 1, bound - lengths[receiver]) // 2
    slack = jnp.where((giver == order[0]) | (receiver == order[0]) | (lengths[receiver] == 0), 0, jnp.maximum(slack, 0))
    shifted = jax.random.randint(jax.random.fold_in(own, 4), (number_of // 2,), 0, 1 << 20) % (slack + 1)
    lengths = lengths.at[giver].add(-shifted).at[receiver].add(shifted)
    labels = jnp.searchsorted(jnp.cumsum(lengths), jnp.arange(rows * top), side="right").astype(jnp.int32)
    table = labels.reshape(top, rows).T
    table = table[jax.random.permutation(jax.random.fold_in(own, 1), rows)]
    turn = jax.random.randint(jax.random.fold_in(own, 2), (rows, 1), 0, top)
    return jnp.take_along_axis(table, (jnp.arange(top)[None, :] + turn) % top, axis=1)


def portions_of(amount, total, reach, slope, full):
    weights = [(1 << 20) // math.isqrt(grade ** slope) + 1 for grade in range(1, amount + 1)]
    largest = reach if full else min(reach, max(-(-total // amount), total * weights[0] // sum(weights)))
    least = 1 if total - largest >= amount - 1 else 0
    holding, spare = [largest] + [least] * (amount - 1), total - largest - least * (amount - 1)
    while spare > 0:
        candidates = [i for i in range(1, amount) if holding[i] < largest] or [i for i in range(1, amount) if holding[i] < reach]
        mass, remaining = sum([weights[i] for i in candidates]), spare
        for i in candidates:
            extra = min(reach - holding[i], max(1, remaining * weights[i] // mass), spare)
            holding[i] = holding[i] + extra
            spare = spare - extra
    return np.array(holding)


def noise(own_key, extent, deviation, limit, shards=(), kind=jnp.bfloat16):
    result = deviation * jax.random.normal(own_key, extent, jnp.float32)
    if shards:
        result = result * block_levels(own_key, extent, shards, -0.22, 0.18)
    return jnp.clip(result, -limit, limit).astype(kind)


def setup_inputs(seed: int = 0) -> dict:
    key_of = jax.random.split(jax.random.key(seed), 9)
    adjoint_state = noise(key_of[0], (3, NX, NY), 1.0, 6.0, ((1, 4), (2, 64)), jnp.float32)
    face_depth = jnp.clip(0.1 + 0.35 * jax.random.uniform(key_of[1], (2, NX, NY), jnp.float32) ** block_levels(key_of[1], (2, NX, NY), ((1, 4), (2, 64)), -0.2, 0.2), 0.1, 0.45)
    innovation = noise(key_of[2], (BLOCKS, SLOTS), 1.0, 6.0, ((0, 256),), jnp.float32)
    interp_weight = jnp.clip(1.0 * jax.random.uniform(key_of[3], (BLOCKS, 4, SLOTS), jnp.float32) ** block_levels(key_of[3], (BLOCKS, 4, SLOTS), ((0, 256),), -0.2, 0.2), 0.0, 1.0)
    block_tile_keys = jax.random.split(jax.random.fold_in(key_of[4], 1), BLOCKS // BLK_DEV)
    block_tile_turns = jax.random.permutation(jax.random.fold_in(key_of[4], 3), BLOCKS // BLK_DEV)
    block_tile = jax.vmap(lambda own, number: shared_out(jax.random.fold_in(key_of[4], 2), own, number, BLK_DEV, N_LON, 1, CAP, 2))(block_tile_keys, block_tile_turns).reshape((BLOCKS, 1))
    block_count = with_ends(jax.random.randint(key_of[5], (BLOCKS, 1), 1, SLOTS + 1), jax.random.fold_in(key_of[5], 1), 1, SLOTS).astype(jnp.int32)
    obs_row = with_ends(jax.random.randint(key_of[6], (BLOCKS, SLOTS), 0, CX - 1), jax.random.fold_in(key_of[6], 1), 0, (CX - 1) - 1).astype(jnp.int32)
    obs_col = with_ends(jax.random.randint(key_of[7], (BLOCKS, SLOTS), 0, CY - 1), jax.random.fold_in(key_of[7], 1), 0, (CY - 1) - 1).astype(jnp.int32)
    return {"adjoint_state": adjoint_state, "face_depth": face_depth, "innovation": innovation, "interp_weight": interp_weight, "block_tile": block_tile, "block_count": block_count, "obs_row": obs_row, "obs_col": obs_col}


def adjoint_step(adj_state, depth_east, depth_north):
    height = adj_state[0]
    east_vel = adj_state[1]
    north_vel = adj_state[2]
    zero_row = jnp.zeros((1, height.shape[1]), jnp.float32)
    height_east = jnp.roll(height, -1, axis=1)
    height_north = jnp.concatenate([height[1:], zero_row], axis=0)
    east_bar = east_vel + depth_east * (height_east - height)
    north_bar = north_vel + depth_north * (height_north - height)
    east_west = jnp.roll(east_bar, 1, axis=1)
    north_south = jnp.concatenate([zero_row, north_bar[:-1]], axis=0)
    height_new = height + east_bar - east_west + north_bar - north_south
    return jnp.stack([height_new, east_bar, north_bar])


def reference(adjoint_state, face_depth, innovation, interp_weight, block_tile, block_count, obs_row, obs_col):
    row_ids = jnp.arange(NX, dtype=jnp.int32)
    depth_east = face_depth[0]
    depth_north = jnp.where((row_ids == NX - 1)[:, None], jnp.float32(0.0), face_depth[1])
    block_ids = jnp.arange(BLOCKS, dtype=jnp.int32)
    lat_tile = (block_ids // (N_LON * BLK_DEV)).astype(jnp.int32)
    global_row = lat_tile[:, None] * CX + obs_row
    global_col = block_tile * CY + obs_col
    usable = jnp.arange(SLOTS, dtype=jnp.int32)[None, :] < block_count
    masked = jnp.where(usable, innovation, jnp.float32(0.0))
    values = interp_weight * masked[:, None, :]
    base_cell = (global_row * NY + global_col).astype(jnp.int32)
    corners = jnp.stack([base_cell, base_cell + 1, base_cell + NY, base_cell + NY + 1], axis=1)
    forcing = jnp.zeros((NX * NY,), jnp.float32).at[corners.reshape(-1)].add(values.reshape(-1)).reshape(NX, NY)
    adj_state = adjoint_state
    for window in range(WINDOWS):
        if window == 2:
            adj_state = adj_state.at[0].add(forcing)
        for step_index in range(WIN):
            adj_state = adjoint_step(adj_state, depth_east, depth_north)
    return adj_state
```

```python
import functools

import jax
import jax.numpy as jnp
from jax import lax
from jax.experimental import pallas as pl
from jax.experimental.pallas import tpu as pltpu
from jax.sharding import PartitionSpec as P

WIN = 6
WINDOWS = 4
CAP = 2
LANES = 128
ROWS8 = 8
HALO = WIN * WINDOWS
HALF = HALO // 2
FRINGE = 16
PIECES = 5
GROUP = 2
MESH = pl.DeviceIdType.MESH
F32 = jnp.float32
BF16 = jnp.bfloat16
I32 = jnp.int32


def lane_ids(shape):
    return lax.broadcasted_iota(I32, shape, len(shape) - 1)


def shift_to(me, index, lon):
    if lon != 64:
        return lax.rem(me + index, lon)
    z = (me // 8 + index % 8) % 8
    y = (me // 2 + index // 8) % 4
    x = (me + index // 32) % 2
    return (z * 4 + y) * 2 + x


def steps(fields, tiles, first, last, number):
    cols = tiles + 1
    lane = lane_ids((ROWS8, LANES))
    sub = lax.broadcasted_iota(I32, (ROWS8, LANES), 0)
    last_lane = lane == LANES - 1
    first_lane = lane == 0
    first_sub = sub == 0

    def group(index, above):
        base = pl.multiple_of(index * ROWS8, ROWS8)
        here = pl.ds(base, ROWS8)
        north = pl.ds(base + 1, ROWS8)
        height = [fields[0, t, here, :] for t in range(cols)]
        height_n = [fields[0, t, north, :] for t in range(cols)]
        turned = [pltpu.roll(x, LANES - 1, 1) for x in height]
        height_e = [jnp.where(last_lane, turned[(t + 1) % cols], turned[t]) for t in range(cols)]
        east = [fields[1, t, here, :] + fields[3, t, here, :] * (height_e[t] - height[t]) for t in range(cols)]
        north_v = [fields[2, t, here, :] + fields[4, t, here, :] * (height_n[t] - height[t]) for t in range(cols)]
        turned = [pltpu.roll(x, 1, 1) for x in east]
        below = [pltpu.roll(x, 1, 0) for x in north_v]
        for t in range(cols):
            west = jnp.where(first_lane, turned[(t - 1) % cols], turned[t])
            south = jnp.where(first_sub, above[t], below[t])
            fields[0, t, here, :] = height[t] + east[t] - west + north_v[t] - south
            fields[1, t, here, :] = east[t]
            fields[2, t, here, :] = north_v[t]
        return tuple(below)

    def step(_, carry):
        lax.fori_loop(first, last, group, tuple(jnp.zeros((ROWS8, LANES), F32) for _ in range(cols)), unroll=2)
        return carry

    lax.fori_loop(0, number, step, 0)


def route_kernel(dims, state, depth, innov, weight, tile, count, obs_row, obs_col, fields_out, recv_out, count_out,
                 fields, send, recv, east_pack, west_pack, east_got, west_got,
                 load_sem, row_sem, pack_sem, corner_sem, a2a_sem, own_sem, store_sem):
    rows, cols, lat, lon, blocks = dims
    tiles = cols // LANES
    ext = rows + 2 * HALO
    total = fields.shape[2]
    my_lat, my_lon = lax.axis_index("lat"), lax.axis_index("lon")
    east, west = lax.rem(my_lon + 1, lon), lax.rem(my_lon + lon - 1, lon)
    has_north, has_south = my_lat < lat - 1, my_lat > 0

    loads = []
    for t in range(tiles):
        span = pl.ds(t * LANES, LANES)
        for source, start, number in ((state, 0, 3), (depth, 3, 2)):
            loads.append(pltpu.make_async_copy(
                source.at[:, :, span], fields.at[pl.ds(start, number), t, pl.ds(HALO, rows), :], load_sem.at[len(loads)]))
    for load in loads:
        load.start()

    barrier = pltpu.get_barrier_semaphore()

    def greet(index, carry):
        pl.semaphore_signal(barrier, inc=1, device_id=(my_lat, shift_to(my_lon, index, lon)), device_id_type=MESH)
        return carry

    for has, where in ((has_north, my_lat + 1), (has_south, my_lat - 1)):
        @pl.when(has)
        def _():
            for column in (west, my_lon, east):
                pl.semaphore_signal(barrier, inc=1, device_id=(where, column), device_id_type=MESH)
    lax.fori_loop(1, lon, greet, 0)

    slots = innov.shape[1]
    live = lane_ids((blocks, slots)) < count[...]
    masked = jnp.where(live, innov[...], 0.0)
    cell = jnp.where(live, obs_row[...] * cols + obs_col[...] + 1, 0).astype(F32)
    data = jnp.concatenate([weight[:, k, :] * masked for k in range(4)] + [cell], axis=0)
    named = jnp.where(tile[...] == lane_ids((blocks, lon)), 1.0, 0.0).astype(F32)
    earlier = (lax.broadcasted_iota(I32, (blocks, blocks), 0) > lane_ids((blocks, blocks))).astype(F32)
    before = jnp.dot(earlier.astype(BF16), named.astype(BF16), preferred_element_type=F32)
    rank = jnp.sum(before * named, axis=1, keepdims=True)
    place = tile[...].astype(F32) * CAP + rank
    wide = (blocks, PIECES * blocks)
    ids = lane_ids(wide)
    row_of = jnp.where(lax.broadcasted_iota(I32, wide, 0) == ids % blocks, place * ROWS8 + (ids // blocks).astype(F32), 0.0)
    row_of = jnp.sum(row_of, axis=0, keepdims=True)
    pick = lax.broadcasted_iota(I32, (CAP * lon * ROWS8, PIECES * blocks), 0).astype(F32) == row_of
    pick = jnp.where(pick, 1.0, 0.0).astype(BF16)
    high = data.astype(BF16)
    rest = data - high.astype(F32)
    mid = rest.astype(BF16)
    low = (rest - mid.astype(F32)).astype(BF16)
    sent = (jnp.dot(pick, high, preferred_element_type=F32) + jnp.dot(pick, mid, preferred_element_type=F32)
            + jnp.dot(pick, low, preferred_element_type=F32))
    send[...] = sent.reshape(CAP * lon, ROWS8, slots)[:, :PIECES, :]

    zero_rows = jnp.zeros((5, tiles, HALO, LANES), F32)
    fields[:, :, pl.ds(ext, total - ext), :] = jnp.zeros((5, tiles + 1, total - ext, LANES), F32)

    @pl.when(jnp.logical_not(has_south))
    def _():
        fields[:, pl.ds(0, tiles), pl.ds(0, HALO), :] = zero_rows
        east_got[pl.ds(0, HALO), :] = zero_rows[0, 0]
        west_got[pl.ds(0, HALO), :] = zero_rows[0, 0]

    @pl.when(jnp.logical_not(has_north))
    def _():
        fields[:, pl.ds(0, tiles), pl.ds(HALO + rows, HALO), :] = zero_rows
        east_got[pl.ds(HALO + rows, HALO), :] = zero_rows[0, 0]
        west_got[pl.ds(HALO + rows, HALO), :] = zero_rows[0, 0]

    for load in loads:
        load.wait()

    @pl.when(jnp.logical_not(has_north))
    def _():
        wall = pl.ds(HALO + rows - ROWS8, ROWS8)
        keep = lax.broadcasted_iota(I32, (tiles, ROWS8, LANES), 1) < ROWS8 - 1
        fields[4, pl.ds(0, tiles), wall, :] = jnp.where(keep, fields[4, pl.ds(0, tiles), wall, :], 0.0)

    lane = lane_ids((ROWS8, LANES))

    def pack(index, carry):
        base = pl.multiple_of(index * ROWS8, ROWS8)
        here = pl.ds(HALO + base, ROWS8)
        to_west = jnp.zeros((ROWS8, LANES), F32)
        to_east = to_west
        for f in range(5):
            first = HALO * f
            inside = jnp.logical_and(lane >= first, lane < first + HALO)
            to_west = jnp.where(inside, pltpu.roll(fields[f, 0, here, :], first, 1) if f else fields[f, 0, here, :], to_west)
            first = (LANES - HALO + HALO * f) % LANES
            inside = jnp.logical_and(lane >= first, lane < first + HALO)
            value = fields[f, tiles - 1, here, :]
            to_east = jnp.where(inside, pltpu.roll(value, HALO * f, 1) if f else value, to_east)
        west_pack[pl.ds(base, ROWS8), :] = to_west
        east_pack[pl.ds(base, ROWS8), :] = to_east
        return carry

    lax.fori_loop(0, rows // ROWS8, pack, 0, unroll=2)

    number = lon - 1 + 3 * has_north.astype(I32) + 3 * has_south.astype(I32)
    pl.semaphore_wait(barrier, number)

    def remote(source, target, sems, where):
        return pltpu.make_async_remote_copy(src_ref=source, dst_ref=target, send_sem=sems.at[0], recv_sem=sems.at[1],
                                            device_id=where, device_id_type=MESH)

    main = pl.ds(HALO, rows)
    low_rows, high_rows = pl.ds(0, HALO), pl.ds(HALO + rows, HALO)
    inner = pl.ds(0, tiles)
    to_north = remote(fields.at[:, inner, pl.ds(rows, HALO), :], fields.at[:, inner, low_rows, :], row_sem.at[0], (my_lat + 1, my_lon))
    to_south = remote(fields.at[:, inner, pl.ds(HALO, HALO), :], fields.at[:, inner, high_rows, :], row_sem.at[1], (my_lat - 1, my_lon))
    to_east = remote(east_pack, west_got.at[main], pack_sem.at[0], (my_lat, east))
    to_west = remote(west_pack, east_got.at[main], pack_sem.at[1], (my_lat, west))
    tail = pl.ds(rows - HALO, HALO)
    north_east = remote(east_pack.at[tail], west_got.at[low_rows], corner_sem.at[0], (my_lat + 1, east))
    north_west = remote(west_pack.at[tail], east_got.at[low_rows], corner_sem.at[1], (my_lat + 1, west))
    south_east = remote(east_pack.at[low_rows], west_got.at[high_rows], corner_sem.at[2], (my_lat - 1, east))
    south_west = remote(west_pack.at[low_rows], east_got.at[high_rows], corner_sem.at[3], (my_lat - 1, west))
    northward, southward = (to_north, north_east, north_west), (to_south, south_east, south_west)

    @pl.when(has_north)
    def _():
        for copy in northward:
            copy.start()

    @pl.when(has_south)
    def _():
        for copy in southward:
            copy.start()

    to_east.start()
    to_west.start()

    def block_copy(index):
        where = shift_to(my_lon, index, lon)
        return remote(send.at[pl.ds(CAP * where, CAP)], recv.at[pl.ds(CAP * my_lon, CAP)], a2a_sem, (my_lat, where))

    def send_blocks(index, carry):
        block_copy(index).start()
        return carry

    lax.fori_loop(1, lon, send_blocks, 0)
    mine = pl.ds(CAP * my_lon, CAP)
    own = pltpu.make_async_copy(send.at[mine], recv.at[mine], own_sem)
    own.start()

    @pl.when(has_south)
    def _():
        for copy in northward:
            copy.wait_recv()

    @pl.when(has_north)
    def _():
        for copy in southward:
            copy.wait_recv()

    to_east.wait_recv()
    to_west.wait_recv()

    def unpack(index, carry):
        here = pl.ds(pl.multiple_of(index * ROWS8, ROWS8), ROWS8)
        from_east, from_west = east_got[here, :], west_got[here, :]
        for f in range(5):
            first = HALO * f
            right = jnp.logical_and(lane >= first, lane < first + HALO)
            first = (LANES - HALO + HALO * f) % LANES
            left = jnp.logical_and(lane >= first, lane < first + HALO)
            both = jnp.where(right, from_east, jnp.where(left, from_west, 0.0))
            fields[f, tiles, here, :] = pltpu.roll(both, LANES - HALO * f, 1) if f else both
        return carry

    lax.fori_loop(0, ext // ROWS8, unpack, 0, unroll=2)

    @pl.when(has_north)
    def _():
        for copy in northward:
            copy.wait_send()

    @pl.when(has_south)
    def _():
        for copy in southward:
            copy.wait_send()

    to_east.wait_send()
    to_west.wait_send()

    steps(fields, tiles, 0, ext // ROWS8, 8)
    steps(fields, tiles, 1, ext // ROWS8 - 1, HALF - 8)
    stores = [pltpu.make_async_copy(fields, fields_out, store_sem.at[0])]
    stores[0].start()

    own.wait()
    others = pl.ds(0, CAP * (lon - 1))
    every = pltpu.make_async_remote_copy(src_ref=send.at[others], dst_ref=recv.at[others], send_sem=a2a_sem.at[0],
                                         recv_sem=a2a_sem.at[1], device_id=(my_lat, east), device_id_type=MESH)
    every.wait_recv()
    stores.append(pltpu.make_async_copy(recv, recv_out, store_sem.at[1]))
    stores[1].start()
    filled = jnp.where(recv[:, PIECES - 1, :] > 0.0, 1.0, 0.0).astype(BF16)
    ones = jnp.ones((ROWS8, slots), BF16)
    live_of = lax.dot_general(ones, filled, (((1,), (1,)), ((), ())), preferred_element_type=F32)
    count_out[...] = live_of.astype(I32)
    every.wait_send()
    for store in stores:
        store.wait()


def spread_kernel(dims, counts, recv, out, packed, total):
    rows, cols, lat, lon, blocks = dims
    tiles = cols // LANES
    segments = CAP * lon
    lane = lane_ids((PIECES, LANES))

    def append(segment, carry):
        fill, current = carry
        number = counts[0, segment]
        chunk = fill // LANES
        shift = fill - chunk * LANES
        turned = pltpu.roll(recv[segment], shift, 1)
        current = jnp.where(lane >= shift, turned, current)
        packed[chunk] = current
        fill = fill + number
        current = jnp.where(fill // LANES > chunk, turned, current)
        return fill, current

    zero = jnp.zeros((PIECES, LANES), F32)
    fill, current = lax.fori_loop(0, segments, append, (jnp.int32(0), zero), unroll=4)
    chunk = fill // LANES
    packed[chunk] = jnp.where(lane < fill - chunk * LANES, current, 0.0)
    for extra in range(1, GROUP):
        packed[chunk + extra] = zero
    total[...] = jnp.zeros_like(total)
    groups = (fill + GROUP * LANES - 1) // (GROUP * LANES)

    depth = GROUP * LANES
    row_ids = lax.broadcasted_iota(I32, (rows, depth), 0)
    col_ids = lax.broadcasted_iota(I32, (cols, depth), 0)

    def add_group(index, carry):
        part = [packed[index * GROUP + j] for j in range(GROUP)]
        both = jnp.concatenate(part, axis=1)
        cell = both[PIECES - 1:, :].astype(I32) - 1
        row_at = cell // cols
        col_at = cell - row_at * cols
        here = row_ids == row_at
        past = row_ids == row_at + 1
        column = jnp.where(col_ids == col_at, 1.0, 0.0).astype(BF16)
        high = both[:4, :].astype(BF16).astype(F32)
        low = both[:4, :] - high

        def side(value, k):
            return jnp.where(here, value[k:k + 1, :], jnp.where(past, value[k + 2:k + 3, :], 0.0)).astype(BF16)

        left = jnp.concatenate([side(high, 0), side(low, 0)], axis=1)
        right = jnp.concatenate([side(high, 1), side(low, 1)], axis=1)
        both_sides = jnp.concatenate([left, right], axis=0)
        columns = jnp.concatenate([column, column], axis=1)
        total[...] += lax.dot_general(both_sides, columns, (((1,), (1,)), ((), ())), preferred_element_type=F32)
        return carry

    lax.fori_loop(0, groups, add_group, 0)

    lane = lane_ids((rows, LANES))
    turned = [pltpu.roll(total[pl.ds(rows, rows), pl.ds(t * LANES, LANES)], 1, 1) for t in range(tiles)]
    for t in range(tiles):
        before = turned[t - 1] if t else jnp.zeros((rows, LANES), F32)
        out[t] = total[pl.ds(0, rows), pl.ds(t * LANES, LANES)] + jnp.where(lane == 0, before, turned[t])


def finish_kernel(dims, fields_in, forcing, out, fields, east_pack, west_pack, east_got, west_got, south_got, north_got,
                  load_sem, row_sem, pack_sem, corner_sem, store_sem):
    rows, cols, lat, lon, blocks = dims
    tiles = cols // LANES
    ext = rows + 2 * HALO
    my_lat, my_lon = lax.axis_index("lat"), lax.axis_index("lon")
    east, west = lax.rem(my_lon + 1, lon), lax.rem(my_lon + lon - 1, lon)
    has_north, has_south = my_lat < lat - 1, my_lat > 0

    load = pltpu.make_async_copy(fields_in, fields, load_sem)
    load.start()
    barrier = pltpu.get_barrier_semaphore()
    for has, where in ((has_north, my_lat + 1), (has_south, my_lat - 1)):
        @pl.when(has)
        def _():
            for column in (west, my_lon, east):
                pl.semaphore_signal(barrier, inc=1, device_id=(where, column), device_id_type=MESH)
    for column in (west, east):
        pl.semaphore_signal(barrier, inc=1, device_id=(my_lat, column), device_id_type=MESH)

    run = rows // 8
    lane = lane_ids((run, LANES))
    to_west = jnp.zeros((run, LANES), F32)
    to_east = to_west
    for g in range(8):
        here = pl.ds(run * g, run)
        inside = lane // FRINGE == g
        value = forcing[0, here, :]
        to_west = jnp.where(inside, pltpu.roll(value, FRINGE * g, 1) if g else value, to_west)
        value = forcing[tiles - 1, here, :]
        to_east = jnp.where(inside, pltpu.roll(value, (FRINGE * (g + 1)) % LANES, 1) if g < 7 else value, to_east)
    west_pack[pl.ds(0, run), :] = to_west
    east_pack[pl.ds(0, run), :] = to_east
    ends = (pl.ds(0, FRINGE), pl.ds(rows - FRINGE, FRINGE))
    for at, here in zip((run, run + FRINGE), ends):
        west_pack[pl.ds(at, FRINGE), :] = forcing[0, here, :]
        east_pack[pl.ds(at, FRINGE), :] = forcing[tiles - 1, here, :]

    number = 2 + 3 * has_north.astype(I32) + 3 * has_south.astype(I32)
    pl.semaphore_wait(barrier, number)

    def remote(source, target, sems, where):
        return pltpu.make_async_remote_copy(src_ref=source, dst_ref=target, send_sem=sems.at[0], recv_sem=sems.at[1],
                                            device_id=where, device_id_type=MESH)

    strip, low_end, high_end = pl.ds(0, run), pl.ds(run, FRINGE), pl.ds(run + FRINGE, FRINGE)
    to_north = remote(forcing.at[:, ends[1], :], south_got, row_sem.at[0], (my_lat + 1, my_lon))
    to_south = remote(forcing.at[:, ends[0], :], north_got, row_sem.at[1], (my_lat - 1, my_lon))
    go_east = remote(east_pack.at[strip], west_got.at[strip], pack_sem.at[0], (my_lat, east))
    go_west = remote(west_pack.at[strip], east_got.at[strip], pack_sem.at[1], (my_lat, west))
    north_east = remote(east_pack.at[high_end], west_got.at[low_end], corner_sem.at[0], (my_lat + 1, east))
    north_west = remote(west_pack.at[high_end], east_got.at[low_end], corner_sem.at[1], (my_lat + 1, west))
    south_east = remote(east_pack.at[low_end], west_got.at[high_end], corner_sem.at[2], (my_lat - 1, east))
    south_west = remote(west_pack.at[low_end], east_got.at[high_end], corner_sem.at[3], (my_lat - 1, west))
    northward, southward = (to_north, north_east, north_west), (to_south, south_east, south_west)

    @pl.when(has_north)
    def _():
        for copy in northward:
            copy.start()

    @pl.when(has_south)
    def _():
        for copy in southward:
            copy.start()

    go_east.start()
    go_west.start()

    load.wait()
    fields[0, pl.ds(0, tiles), pl.ds(HALO, rows), :] += forcing[...]

    @pl.when(has_south)
    def _():
        for copy in northward:
            copy.wait_recv()
        at = pl.ds(HALO - FRINGE, FRINGE)
        fields[0, pl.ds(0, tiles), at, :] += south_got[...]

    @pl.when(has_north)
    def _():
        for copy in southward:
            copy.wait_recv()
        at = pl.ds(HALO + rows, FRINGE)
        fields[0, pl.ds(0, tiles), at, :] += north_got[...]

    go_east.wait_recv()
    go_west.wait_recv()
    right = lane < FRINGE
    left = lane >= LANES - FRINGE
    from_east, from_west = east_got[strip, :], west_got[strip, :]
    for g in range(8):
        here = pl.ds(HALO + run * g, run)
        one = pltpu.roll(from_east, (LANES - FRINGE * g) % LANES, 1) if g else from_east
        two = pltpu.roll(from_west, (LANES - FRINGE * (g + 1)) % LANES, 1) if g < 7 else from_west
        fields[0, tiles, here, :] += jnp.where(right, one, jnp.where(left, two, 0.0))
    lane = lane_ids((FRINGE, LANES))
    right = lane < FRINGE
    left = lane >= LANES - FRINGE
    for has, end, at in ((has_south, low_end, HALO - FRINGE), (has_north, high_end, HALO + rows)):
        @pl.when(has)
        def _():
            fields[0, tiles, pl.ds(at, FRINGE), :] += jnp.where(right, east_got[end, :], jnp.where(left, west_got[end, :], 0.0))

    steps(fields, tiles, 1, ext // ROWS8 - 1, 4)
    steps(fields, tiles, 2, ext // ROWS8 - 2, HALF - 4)
    stores = []
    for t in range(tiles):
        store = pltpu.make_async_copy(fields.at[pl.ds(0, 3), t, pl.ds(HALO, rows), :],
                                      out.at[:, :, pl.ds(t * LANES, LANES)], store_sem.at[t])
        store.start()
        stores.append(store)

    @pl.when(has_north)
    def _():
        for copy in northward:
            copy.wait_send()

    @pl.when(has_south)
    def _():
        for copy in southward:
            copy.wait_send()

    go_east.wait_send()
    go_west.wait_send()
    for store in stores:
        store.wait()


def per_device(lat, lon, adjoint_state, face_depth, innovation, interp_weight, block_tile, block_count, obs_row, obs_col):
    rows, cols = adjoint_state.shape[1:]
    blocks, slots = innovation.shape
    tiles = cols // LANES
    dims = (rows, cols, lat, lon, blocks)
    ext = rows + 2 * HALO
    total = ext + ROWS8
    segments = CAP * lon
    vmem = pl.BlockSpec(memory_space=pltpu.VMEM)
    anywhere = pl.BlockSpec(memory_space=pl.ANY)
    dma = pltpu.SemaphoreType.DMA
    fields_shape = (5, tiles + 1, total, LANES)
    fields, recv, counts = pl.pallas_call(
        functools.partial(route_kernel, dims),
        name="route",
        out_shape=(
            jax.ShapeDtypeStruct(fields_shape, F32),
            jax.ShapeDtypeStruct((segments, PIECES, slots), F32),
            jax.ShapeDtypeStruct((ROWS8, segments), I32),
        ),
        in_specs=[anywhere] * 2 + [vmem] * 6,
        out_specs=(anywhere, anywhere, vmem),
        scratch_shapes=[
            pltpu.VMEM(fields_shape, F32),
            pltpu.VMEM((segments, PIECES, slots), F32),
            pltpu.VMEM((segments, PIECES, slots), F32),
            pltpu.VMEM((rows, LANES), F32),
            pltpu.VMEM((rows, LANES), F32),
            pltpu.VMEM((ext, LANES), F32),
            pltpu.VMEM((ext, LANES), F32),
            dma((2 * tiles,)), dma((2, 2)), dma((2, 2)), dma((4, 2)), dma((2,)), dma, dma((2,)),
        ],
        compiler_params=pltpu.CompilerParams(collective_id=0, has_side_effects=True, vmem_limit_bytes=32 << 20),
    )(adjoint_state, face_depth, innovation, interp_weight, block_tile, block_count, obs_row, obs_col)
    forcing = pl.pallas_call(
        functools.partial(spread_kernel, dims),
        name="spread",
        out_shape=jax.ShapeDtypeStruct((tiles, rows, LANES), F32),
        in_specs=[pl.BlockSpec(memory_space=pltpu.SMEM), vmem],
        out_specs=vmem,
        scratch_shapes=[
            pltpu.VMEM((segments + GROUP, PIECES, LANES), F32),
            pltpu.VMEM((2 * rows, cols), F32),
        ],
        compiler_params=pltpu.CompilerParams(vmem_limit_bytes=32 << 20),
    )(counts, recv)
    run = rows // 8 + 2 * FRINGE
    return pl.pallas_call(
        functools.partial(finish_kernel, dims),
        name="finish",
        out_shape=jax.ShapeDtypeStruct((3, rows, cols), F32),
        in_specs=[anywhere, vmem],
        out_specs=anywhere,
        scratch_shapes=[
            pltpu.VMEM(fields_shape, F32),
            pltpu.VMEM((run, LANES), F32),
            pltpu.VMEM((run, LANES), F32),
            pltpu.VMEM((run, LANES), F32),
            pltpu.VMEM((run, LANES), F32),
            pltpu.VMEM((tiles, FRINGE, LANES), F32),
            pltpu.VMEM((tiles, FRINGE, LANES), F32),
            dma, dma((2, 2)), dma((2, 2)), dma((4, 2)), dma((tiles,)),
        ],
        compiler_params=pltpu.CompilerParams(collective_id=1, has_side_effects=True, vmem_limit_bytes=32 << 20),
    )(fields, forcing)


def solution(mesh):
    return jax.shard_map(
        functools.partial(per_device, mesh.shape["lat"], mesh.shape["lon"]),
        mesh=mesh,
        in_specs=(
            P(None, "lat", "lon"),
            P(None, "lat", "lon"),
            P(("lat", "lon"), None),
            P(("lat", "lon"), None, None),
            P(("lat", "lon"), None),
            P(("lat", "lon"), None),
            P(("lat", "lon"), None),
            P(("lat", "lon"), None),
        ),
        out_specs=P(None, "lat", "lon"),
        check_vma=False,
    )
```

```python
import functools

import jax
import jax.numpy as jnp
from jax import lax
from jax.experimental import pallas as pl
from jax.experimental.pallas import tpu as pltpu
from jax.sharding import PartitionSpec as P

WIN = 6
WINDOWS = 4
CAP = 2
LANES = 128
ROWS8 = 8
HALO = WIN * WINDOWS
HALF = HALO // 2
FRINGE = 16
PIECES = 5
GROUP = 2
MESH = pl.DeviceIdType.MESH
F32 = jnp.float32
BF16 = jnp.bfloat16
I32 = jnp.int32


def lane_ids(shape):
    return lax.broadcasted_iota(I32, shape, len(shape) - 1)


def shift_to(me, index, lon):
    if lon != 64:
        return lax.rem(me + index, lon)
    z = (me // 8 + index % 8) % 8
    y = (me // 2 + index // 8) % 4
    x = (me + index // 32) % 2
    return (z * 4 + y) * 2 + x


def columns_at(width):
    part = LANES // width
    lane = lane_ids((ROWS8, LANES))
    part_of, inside = lane // part, lane % part
    cuts = [(width * part * t - HALO) % LANES for t in range(width)]
    into = [(width * part * t - HALO + LANES + width * inside + (part_of + width - t) % width) % LANES for t in range(width)]
    turn = [part * ((part_of + c) % width) + inside for c in range(width)]
    back = [part * ((part_of + width - c) % width) + inside for c in range(width)]
    out = []
    for t in range(width):
        along = (lane + LANES - cuts[t]) % LANES
        out.append(jnp.minimum(part * ((along + t) % width) + along // width, LANES - 1))
    return lane, part_of, cuts, into, turn, back, out


def take(values, index):
    return jnp.take_along_axis(values, index, axis=1)


def by_part(part_of, choices):
    value = choices[-1]
    for p in range(len(choices) - 1):
        value = jnp.where(part_of == p, choices[p], value)
    return value


def to_runs(maps, values):
    lane, part_of, cuts, into, turn, back, out = maps
    width = len(values)
    sorted_ = [take(jnp.where(lane >= cuts[t], values[t - 1], values[t]), into[t]) for t in range(width)]
    mixed = [by_part(part_of, [sorted_[(p - c) % width] for p in range(width)]) for c in range(width)]
    return [take(mixed[c], turn[c]) if c else mixed[c] for c in range(width)]


def from_runs(maps, values):
    lane, part_of, cuts, into, turn, back, out = maps
    width = len(values)
    mixed = [take(values[c], back[c]) if c else values[c] for c in range(width)]
    sorted_ = [by_part(part_of, [mixed[(p - t) % width] for p in range(width)]) for t in range(width)]
    windows = [take(sorted_[t], out[t]) for t in range(width)]
    return [jnp.where(lane < cuts[t + 1], windows[t], windows[t + 1]) for t in range(width - 1)]


def one_step(old, new, east_vel, north_vel, depth_east, depth_north):
    width, number = east_vel.shape[:2]
    cols = range(width)
    for c in cols:
        old[c, number] = pltpu.roll(old[c, 0], ROWS8 - 1, 0)
    end = number - 1
    south = [pltpu.roll(north_vel[c, end] + depth_north[c, end] * (old[c, number] - old[c, end]), 1, 0) for c in cols]
    for k in range(number):
        height = [old[c, k] for c in cols]
        height_e = height[1:] + [pltpu.roll(height[0], LANES - 1, 1)]
        east = [None] * width
        for c in [width - 1] + list(range(width - 1)):
            east[c] = east_vel[c, k] + depth_east[c, k] * (height_e[c] - height[c])
        west = [pltpu.roll(east[-1], 1, 1)] + east[:-1]
        north = [None] * width
        for c in cols:
            north[c] = north_vel[c, k] + depth_north[c, k] * (old[c, k + 1] - height[c])
            new[c, k] = height[c] + (east[c] - west[c]) + (north[c] - south[c])
            east_vel[c, k] = east[c]
            north_vel[c, k] = north[c]
        south = north


def steps(number, height, other, *rest):
    def two(_, carry):
        one_step(height, other, *rest)
        one_step(other, height, *rest)
        return carry

    lax.fori_loop(0, number // 2, two, 0)


def route_kernel(dims, state, depth, innov_in, weight_in, tile_in, count_in, row_in, col_in, fields_out, recv_out, count_out,
                 fields, height, other, east_vel, north_vel, depth_east, depth_north,
                 innov, weight, tile_row, count_row, obs_row, obs_col, send, recv, east_pack, west_pack, east_got, west_got,
                 load_sem, small_sem, row_sem, pack_sem, corner_sem, a2a_sem, own_sem, store_sem):
    rows, cols, lat, lon, blocks = dims
    tiles = cols // LANES
    ext = rows + 2 * HALO
    number = ext // ROWS8
    my_lat, my_lon = lax.axis_index("lat"), lax.axis_index("lon")
    east, west = lax.rem(my_lon + 1, lon), lax.rem(my_lon + lon - 1, lon)
    has_north, has_south = my_lat < lat - 1, my_lat > 0

    small = [pltpu.make_async_copy(source, target, small_sem.at[i]) for i, (source, target) in enumerate((
        (tile_in, tile_row), (count_in, count_row), (innov_in, innov), (weight_in, weight), (row_in, obs_row), (col_in, obs_col)))]
    for load in small:
        load.start()
    loads = []
    for t in range(tiles):
        span = pl.ds(t * LANES, LANES)
        for source, start, some in ((state, 0, 3), (depth, 3, 2)):
            loads.append(pltpu.make_async_copy(
                source.at[:, :, span], fields.at[pl.ds(start, some), t, pl.ds(HALO, rows), :], load_sem.at[len(loads)]))
    for load in loads:
        load.start()

    barrier = pltpu.get_barrier_semaphore()

    def greet(index, carry):
        pl.semaphore_signal(barrier, inc=1, device_id=(my_lat, shift_to(my_lon, index, lon)), device_id_type=MESH)
        return carry

    for has, where in ((has_north, my_lat + 1), (has_south, my_lat - 1)):
        @pl.when(has)
        def _():
            for column in (west, my_lon, east):
                pl.semaphore_signal(barrier, inc=1, device_id=(where, column), device_id_type=MESH)
    lax.fori_loop(1, lon, greet, 0)

    for load in small:
        load.wait()
    slots = innov.shape[1]
    square = (blocks, blocks)
    diagonal = lax.broadcasted_iota(I32, square, 0) == lane_ids(square)
    tile = jnp.sum(jnp.where(diagonal, tile_row[...].astype(F32), 0.0), axis=1, keepdims=True)
    count = jnp.sum(jnp.where(diagonal, count_row[...].astype(F32), 0.0), axis=1, keepdims=True)
    live = lane_ids((blocks, slots)).astype(F32) < count
    masked = jnp.where(live, innov[...], 0.0)
    cell = jnp.where(live, obs_row[...] * cols + obs_col[...] + 1, 0).astype(F32)
    data = jnp.concatenate([weight[:, k, :] * masked for k in range(4)] + [cell], axis=0)
    named = jnp.where(tile == lane_ids((blocks, lon)).astype(F32), 1.0, 0.0)
    earlier = jnp.where(lax.broadcasted_iota(I32, square, 0) > lane_ids(square), 1.0, 0.0)
    before = jnp.dot(earlier.astype(BF16), named.astype(BF16), preferred_element_type=F32)
    rank = jnp.sum(before * named, axis=1, keepdims=True)
    place = tile * CAP + rank
    wide = (blocks, PIECES * blocks)
    ids = lane_ids(wide)
    row_of = jnp.where(lax.broadcasted_iota(I32, wide, 0) == ids % blocks, place * ROWS8 + (ids // blocks).astype(F32), 0.0)
    row_of = jnp.sum(row_of, axis=0, keepdims=True)
    pick = lax.broadcasted_iota(I32, (CAP * lon * ROWS8, PIECES * blocks), 0).astype(F32) == row_of
    pick = jnp.where(pick, 1.0, 0.0).astype(BF16)
    high = data.astype(BF16)
    rest = data - high.astype(F32)
    mid = rest.astype(BF16)
    low = (rest - mid.astype(F32)).astype(BF16)
    sent = (jnp.dot(pick, high, preferred_element_type=F32) + jnp.dot(pick, mid, preferred_element_type=F32)
            + jnp.dot(pick, low, preferred_element_type=F32))
    send[...] = sent.reshape(CAP * lon, ROWS8, slots)[:, :PIECES, :]

    zero_rows = jnp.zeros((5, tiles, HALO, LANES), F32)

    @pl.when(jnp.logical_not(has_south))
    def _():
        fields[:, pl.ds(0, tiles), pl.ds(0, HALO), :] = zero_rows
        east_got[pl.ds(0, HALO), :] = zero_rows[0, 0]
        west_got[pl.ds(0, HALO), :] = zero_rows[0, 0]

    @pl.when(jnp.logical_not(has_north))
    def _():
        fields[:, pl.ds(0, tiles), pl.ds(HALO + rows, HALO), :] = zero_rows
        east_got[pl.ds(HALO + rows, HALO), :] = zero_rows[0, 0]
        west_got[pl.ds(HALO + rows, HALO), :] = zero_rows[0, 0]

    for load in loads:
        load.wait()

    @pl.when(jnp.logical_not(has_north))
    def _():
        wall = pl.ds(HALO + rows - ROWS8, ROWS8)
        keep = lax.broadcasted_iota(I32, (tiles, ROWS8, LANES), 1) < ROWS8 - 1
        fields[4, pl.ds(0, tiles), wall, :] = jnp.where(keep, fields[4, pl.ds(0, tiles), wall, :], 0.0)

    lane = lane_ids((ROWS8, LANES))

    def pack(index, carry):
        base = pl.multiple_of(index * ROWS8, ROWS8)
        here = pl.ds(HALO + base, ROWS8)
        to_west = jnp.zeros((ROWS8, LANES), F32)
        to_east = to_west
        for f in range(5):
            first = HALO * f
            inside = jnp.logical_and(lane >= first, lane < first + HALO)
            to_west = jnp.where(inside, pltpu.roll(fields[f, 0, here, :], first, 1) if f else fields[f, 0, here, :], to_west)
            first = (LANES - HALO + HALO * f) % LANES
            inside = jnp.logical_and(lane >= first, lane < first + HALO)
            value = fields[f, tiles - 1, here, :]
            to_east = jnp.where(inside, pltpu.roll(value, HALO * f, 1) if f else value, to_east)
        west_pack[pl.ds(base, ROWS8), :] = to_west
        east_pack[pl.ds(base, ROWS8), :] = to_east
        return carry

    lax.fori_loop(0, rows // ROWS8, pack, 0, unroll=2)

    pl.semaphore_wait(barrier, lon - 1 + 3 * has_north.astype(I32) + 3 * has_south.astype(I32))

    def remote(source, target, sems, where):
        return pltpu.make_async_remote_copy(src_ref=source, dst_ref=target, send_sem=sems.at[0], recv_sem=sems.at[1],
                                            device_id=where, device_id_type=MESH)

    main = pl.ds(HALO, rows)
    low_rows, high_rows = pl.ds(0, HALO), pl.ds(HALO + rows, HALO)
    inner = pl.ds(0, tiles)
    to_north = remote(fields.at[:, inner, pl.ds(rows, HALO), :], fields.at[:, inner, low_rows, :], row_sem.at[0], (my_lat + 1, my_lon))
    to_south = remote(fields.at[:, inner, pl.ds(HALO, HALO), :], fields.at[:, inner, high_rows, :], row_sem.at[1], (my_lat - 1, my_lon))
    to_east = remote(east_pack, west_got.at[main], pack_sem.at[0], (my_lat, east))
    to_west = remote(west_pack, east_got.at[main], pack_sem.at[1], (my_lat, west))
    tail = pl.ds(rows - HALO, HALO)
    north_east = remote(east_pack.at[tail], west_got.at[low_rows], corner_sem.at[0], (my_lat + 1, east))
    north_west = remote(west_pack.at[tail], east_got.at[low_rows], corner_sem.at[1], (my_lat + 1, west))
    south_east = remote(east_pack.at[low_rows], west_got.at[high_rows], corner_sem.at[2], (my_lat - 1, east))
    south_west = remote(west_pack.at[low_rows], east_got.at[high_rows], corner_sem.at[3], (my_lat - 1, west))
    northward, southward = (to_north, north_east, north_west), (to_south, south_east, south_west)

    @pl.when(has_north)
    def _():
        for copy in northward:
            copy.start()

    @pl.when(has_south)
    def _():
        for copy in southward:
            copy.start()

    to_east.start()
    to_west.start()

    def block_copy(index):
        where = shift_to(my_lon, index, lon)
        return remote(send.at[pl.ds(CAP * where, CAP)], recv.at[pl.ds(CAP * my_lon, CAP)], a2a_sem, (my_lat, where))

    def send_blocks(index, carry):
        block_copy(index).start()
        return carry

    lax.fori_loop(1, lon, send_blocks, 0)
    mine = pl.ds(CAP * my_lon, CAP)
    own = pltpu.make_async_copy(send.at[mine], recv.at[mine], own_sem)
    own.start()

    @pl.when(has_south)
    def _():
        for copy in northward:
            copy.wait_recv()

    @pl.when(has_north)
    def _():
        for copy in southward:
            copy.wait_recv()

    to_east.wait_recv()
    to_west.wait_recv()

    def unpack(index, carry):
        here = pl.ds(pl.multiple_of(index * ROWS8, ROWS8), ROWS8)
        from_east, from_west = east_got[here, :], west_got[here, :]
        for f in range(5):
            first = HALO * f
            right = jnp.logical_and(lane >= first, lane < first + HALO)
            first = (LANES - HALO + HALO * f) % LANES
            left = jnp.logical_and(lane >= first, lane < first + HALO)
            both = jnp.where(right, from_east, jnp.where(left, from_west, 0.0))
            fields[f, tiles, here, :] = pltpu.roll(both, LANES - HALO * f, 1) if f else both
        return carry

    lax.fori_loop(0, ext // ROWS8, unpack, 0, unroll=2)

    @pl.when(has_north)
    def _():
        for copy in northward:
            copy.wait_send()

    @pl.when(has_south)
    def _():
        for copy in southward:
            copy.wait_send()

    to_east.wait_send()
    to_west.wait_send()

    refs = (height, east_vel, north_vel, depth_east, depth_north)
    maps = columns_at(tiles + 1)

    def arrange(k, carry):
        for f, ref in enumerate(refs):
            values = to_runs(maps, [fields[f, t, pl.ds(k, ROWS8, stride=number), :] for t in range(tiles + 1)])
            for c in range(tiles + 1):
                ref[c, k] = values[c]
        return carry

    lax.fori_loop(0, number, arrange, 0, unroll=2)
    inner = pl.ds(0, number)
    stores = [pltpu.make_async_copy(ref.at[:, inner], fields_out.at[f], store_sem.at[f]) for f, ref in enumerate(refs)]
    for store in stores[3:]:
        store.start()
    steps(HALF, height, other, *refs[1:])
    for store in stores[:3]:
        store.start()

    own.wait()
    others = pl.ds(0, CAP * (lon - 1))
    every = pltpu.make_async_remote_copy(src_ref=send.at[others], dst_ref=recv.at[others], send_sem=a2a_sem.at[0],
                                         recv_sem=a2a_sem.at[1], device_id=(my_lat, east), device_id_type=MESH)
    every.wait_recv()
    stores.append(pltpu.make_async_copy(recv, recv_out, store_sem.at[5]))
    stores[5].start()
    filled = jnp.where(recv[:, PIECES - 1, :] > 0.0, 1.0, 0.0).astype(BF16)
    ones = jnp.ones((ROWS8, slots), BF16)
    live_of = lax.dot_general(ones, filled, (((1,), (1,)), ((), ())), preferred_element_type=F32)
    count_out[...] = live_of.astype(I32)
    every.wait_send()
    for store in stores:
        store.wait()


def spread_kernel(dims, counts, recv, out, packed, total):
    rows, cols, lat, lon, blocks = dims
    tiles = cols // LANES
    segments = CAP * lon
    lane = lane_ids((PIECES, LANES))

    def append(segment, carry):
        fill, current = carry
        number = counts[0, segment]
        chunk = fill // LANES
        shift = fill - chunk * LANES
        turned = pltpu.roll(recv[segment], shift, 1)
        current = jnp.where(lane >= shift, turned, current)
        packed[chunk] = current
        fill = fill + number
        current = jnp.where(fill // LANES > chunk, turned, current)
        return fill, current

    zero = jnp.zeros((PIECES, LANES), F32)
    fill, current = lax.fori_loop(0, segments, append, (jnp.int32(0), zero), unroll=min(32, segments))
    chunk = fill // LANES
    packed[chunk] = jnp.where(lane < fill - chunk * LANES, current, 0.0)
    for extra in range(1, GROUP):
        packed[chunk + extra] = zero
    total[...] = jnp.zeros_like(total)
    groups = (fill + GROUP * LANES - 1) // (GROUP * LANES)

    depth = GROUP * LANES
    row_ids = lax.broadcasted_iota(I32, (rows, depth), 0)
    col_ids = lax.broadcasted_iota(I32, (cols, depth), 0)

    def add_group(index, carry):
        part = [packed[index * GROUP + j] for j in range(GROUP)]
        both = jnp.concatenate(part, axis=1)
        cell = both[PIECES - 1:, :].astype(I32) - 1
        row_at = cell // cols
        col_at = cell - row_at * cols
        here = row_ids == row_at
        past = row_ids == row_at + 1
        column = jnp.where(col_ids == col_at, 1.0, 0.0).astype(BF16)
        high = both[:4, :].astype(BF16).astype(F32)
        low = both[:4, :] - high

        def side(value, k):
            return jnp.where(here, value[k:k + 1, :], jnp.where(past, value[k + 2:k + 3, :], 0.0)).astype(BF16)

        left = jnp.concatenate([side(high, 0), side(low, 0)], axis=1)
        right = jnp.concatenate([side(high, 1), side(low, 1)], axis=1)
        both_sides = jnp.concatenate([left, right], axis=0)
        columns = jnp.concatenate([column, column], axis=1)
        total[...] += lax.dot_general(both_sides, columns, (((1,), (1,)), ((), ())), preferred_element_type=F32)
        return carry

    lax.fori_loop(0, groups, add_group, 0)

    lane = lane_ids((rows, LANES))
    turned = [pltpu.roll(total[pl.ds(rows, rows), pl.ds(t * LANES, LANES)], 1, 1) for t in range(tiles)]
    for t in range(tiles):
        before = turned[t - 1] if t else jnp.zeros((rows, LANES), F32)
        out[t] = total[pl.ds(0, rows), pl.ds(t * LANES, LANES)] + jnp.where(lane == 0, before, turned[t])


def finish_kernel(dims, fields_in, forcing_in, out, forcing, height, other, east_vel, north_vel, depth_east, depth_north, done,
                  east_pack, west_pack, east_got, west_got, load_sem, row_sem, pack_sem, corner_sem, store_sem):
    rows, cols, lat, lon, blocks = dims
    tiles = cols // LANES
    ext = rows + 2 * HALO
    number = ext // ROWS8
    my_lat, my_lon = lax.axis_index("lat"), lax.axis_index("lon")
    east, west = lax.rem(my_lon + 1, lon), lax.rem(my_lon + lon - 1, lon)
    has_north, has_south = my_lat < lat - 1, my_lat > 0
    refs = (height, east_vel, north_vel, depth_east, depth_north)
    inner = pl.ds(0, number)
    loads = [pltpu.make_async_copy(forcing_in, forcing.at[pl.ds(0, tiles), pl.ds(HALO, rows), :], load_sem.at[5])]
    loads += [pltpu.make_async_copy(fields_in.at[f], ref.at[:, inner], load_sem.at[f]) for f, ref in enumerate(refs)]
    for load in loads:
        load.start()
    barrier = pltpu.get_barrier_semaphore()
    for has, where in ((has_north, my_lat + 1), (has_south, my_lat - 1)):
        @pl.when(has)
        def _():
            for column in (west, my_lon, east):
                pl.semaphore_signal(barrier, inc=1, device_id=(where, column), device_id_type=MESH)
    for column in (west, east):
        pl.semaphore_signal(barrier, inc=1, device_id=(my_lat, column), device_id_type=MESH)

    beyond = HALO - FRINGE
    for at in (0, ext - beyond):
        forcing[:, pl.ds(at, beyond), :] = jnp.zeros((tiles + 1, beyond, LANES), F32)
    for has, at in ((has_south, beyond), (has_north, HALO + rows)):
        @pl.when(jnp.logical_not(has))
        def _():
            forcing[:, pl.ds(at, FRINGE), :] = jnp.zeros((tiles + 1, FRINGE, LANES), F32)

    loads[0].wait()
    run = rows // 8
    lane = lane_ids((run, LANES))
    to_west = jnp.zeros((run, LANES), F32)
    to_east = to_west
    for g in range(8):
        here = pl.ds(HALO + run * g, run)
        inside = lane // FRINGE == g
        value = forcing[0, here, :]
        to_west = jnp.where(inside, pltpu.roll(value, FRINGE * g, 1) if g else value, to_west)
        value = forcing[tiles - 1, here, :]
        to_east = jnp.where(inside, pltpu.roll(value, (FRINGE * (g + 1)) % LANES, 1) if g < 7 else value, to_east)
    west_pack[pl.ds(0, run), :] = to_west
    east_pack[pl.ds(0, run), :] = to_east
    ends = (pl.ds(HALO, FRINGE), pl.ds(HALO + rows - FRINGE, FRINGE))
    outer = (pl.ds(HALO - FRINGE, FRINGE), pl.ds(HALO + rows, FRINGE))
    for at, here in zip((run, run + FRINGE), ends):
        west_pack[pl.ds(at, FRINGE), :] = forcing[0, here, :]
        east_pack[pl.ds(at, FRINGE), :] = forcing[tiles - 1, here, :]

    pl.semaphore_wait(barrier, 2 + 3 * has_north.astype(I32) + 3 * has_south.astype(I32))

    def remote(source, target, sems, where):
        return pltpu.make_async_remote_copy(src_ref=source, dst_ref=target, send_sem=sems.at[0], recv_sem=sems.at[1],
                                            device_id=where, device_id_type=MESH)

    main = pl.ds(0, tiles)
    strip, low_end, high_end = pl.ds(0, run), pl.ds(run, FRINGE), pl.ds(run + FRINGE, FRINGE)
    to_north = remote(forcing.at[main, ends[1], :], forcing.at[main, outer[0], :], row_sem.at[0], (my_lat + 1, my_lon))
    to_south = remote(forcing.at[main, ends[0], :], forcing.at[main, outer[1], :], row_sem.at[1], (my_lat - 1, my_lon))
    go_east = remote(east_pack.at[strip], west_got.at[strip], pack_sem.at[0], (my_lat, east))
    go_west = remote(west_pack.at[strip], east_got.at[strip], pack_sem.at[1], (my_lat, west))
    north_east = remote(east_pack.at[high_end], west_got.at[low_end], corner_sem.at[0], (my_lat + 1, east))
    north_west = remote(west_pack.at[high_end], east_got.at[low_end], corner_sem.at[1], (my_lat + 1, west))
    south_east = remote(east_pack.at[low_end], west_got.at[high_end], corner_sem.at[2], (my_lat - 1, east))
    south_west = remote(west_pack.at[low_end], east_got.at[high_end], corner_sem.at[3], (my_lat - 1, west))
    northward, southward = (to_north, north_east, north_west), (to_south, south_east, south_west)

    @pl.when(has_north)
    def _():
        for copy in northward:
            copy.start()

    @pl.when(has_south)
    def _():
        for copy in southward:
            copy.start()

    go_east.start()
    go_west.start()

    for load in loads[1:]:
        load.wait()

    @pl.when(has_south)
    def _():
        for copy in northward:
            copy.wait_recv()

    @pl.when(has_north)
    def _():
        for copy in southward:
            copy.wait_recv()

    go_east.wait_recv()
    go_west.wait_recv()
    right = lane < FRINGE
    left = lane >= LANES - FRINGE
    from_east, from_west = east_got[strip, :], west_got[strip, :]
    for g in range(8):
        here = pl.ds(HALO + run * g, run)
        one = pltpu.roll(from_east, (LANES - FRINGE * g) % LANES, 1) if g else from_east
        two = pltpu.roll(from_west, (LANES - FRINGE * (g + 1)) % LANES, 1) if g < 7 else from_west
        forcing[tiles, here, :] = jnp.where(right, one, jnp.where(left, two, 0.0))
    lane = lane_ids((FRINGE, LANES))
    right = lane < FRINGE
    left = lane >= LANES - FRINGE
    for has, end, at in ((has_south, low_end, HALO - FRINGE), (has_north, high_end, HALO + rows)):
        @pl.when(has)
        def _():
            forcing[tiles, pl.ds(at, FRINGE), :] = jnp.where(right, east_got[end, :], jnp.where(left, west_got[end, :], 0.0))

    maps = columns_at(tiles + 1)

    def add(k, carry):
        values = to_runs(maps, [forcing[t, pl.ds(k, ROWS8, stride=number), :] for t in range(tiles + 1)])
        for c in range(tiles + 1):
            height[c, k] += values[c]
        return carry

    lax.fori_loop(0, number, add, 0, unroll=2)
    steps(HALF, height, other, *refs[1:])
    stores = []
    for f in range(3):
        def leave(k, carry):
            for t, value in enumerate(from_runs(maps, [refs[f][c, k] for c in range(tiles + 1)])):
                done[f, t, pl.ds(k, ROWS8, stride=number), :] = value
            return carry

        lax.fori_loop(0, number, leave, 0, unroll=2)
        for t in range(tiles):
            store = pltpu.make_async_copy(done.at[f, t, pl.ds(HALO, rows), :],
                                          out.at[f, :, pl.ds(t * LANES, LANES)], store_sem.at[f, t])
            store.start()
            stores.append(store)

    @pl.when(has_north)
    def _():
        for copy in northward:
            copy.wait_send()

    @pl.when(has_south)
    def _():
        for copy in southward:
            copy.wait_send()

    go_east.wait_send()
    go_west.wait_send()
    for store in stores:
        store.wait()


def per_device(lat, lon, adjoint_state, face_depth, innovation, interp_weight, block_tile, block_count, obs_row, obs_col):
    rows, cols = adjoint_state.shape[1:]
    blocks, slots = innovation.shape
    tiles = cols // LANES
    dims = (rows, cols, lat, lon, blocks)
    ext = rows + 2 * HALO
    segments = CAP * lon
    vmem = pl.BlockSpec(memory_space=pltpu.VMEM)
    anywhere = pl.BlockSpec(memory_space=pl.ANY)
    dma = pltpu.SemaphoreType.DMA
    number = ext // ROWS8
    natural = pltpu.VMEM((5, tiles + 1, ext, LANES), F32)
    runs = [pltpu.VMEM((tiles + 1, number + 1, ROWS8, LANES), F32)] * 2 + [pltpu.VMEM((tiles + 1, number, ROWS8, LANES), F32)] * 4
    params = functools.partial(pltpu.CompilerParams, has_side_effects=True, vmem_limit_bytes=56 << 20)
    fields, recv, counts = pl.pallas_call(
        functools.partial(route_kernel, dims),
        name="route",
        out_shape=(
            jax.ShapeDtypeStruct((5, tiles + 1, number, ROWS8, LANES), F32),
            jax.ShapeDtypeStruct((segments, PIECES, slots), F32),
            jax.ShapeDtypeStruct((ROWS8, segments), I32),
        ),
        in_specs=[anywhere] * 8,
        out_specs=(anywhere, anywhere, vmem),
        scratch_shapes=[
            natural, *runs,
            pltpu.VMEM((blocks, slots), F32),
            pltpu.VMEM((blocks, 4, slots), F32),
            pltpu.VMEM((1, blocks), I32),
            pltpu.VMEM((1, blocks), I32),
            pltpu.VMEM((blocks, slots), I32),
            pltpu.VMEM((blocks, slots), I32),
            pltpu.VMEM((segments, PIECES, slots), F32),
            pltpu.VMEM((segments, PIECES, slots), F32),
            pltpu.VMEM((rows, LANES), F32),
            pltpu.VMEM((rows, LANES), F32),
            pltpu.VMEM((ext, LANES), F32),
            pltpu.VMEM((ext, LANES), F32),
            dma((2 * tiles,)), dma((6,)), dma((2, 2)), dma((2, 2)), dma((4, 2)), dma((2,)), dma, dma((6,)),
        ],
        compiler_params=params(collective_id=0),
    )(adjoint_state, face_depth, innovation, interp_weight, block_tile.reshape(1, blocks), block_count.reshape(1, blocks),
      obs_row, obs_col)
    forcing = pl.pallas_call(
        functools.partial(spread_kernel, dims),
        name="spread",
        out_shape=jax.ShapeDtypeStruct((tiles, rows, LANES), F32),
        in_specs=[pl.BlockSpec(memory_space=pltpu.SMEM), vmem],
        out_specs=vmem,
        scratch_shapes=[
            pltpu.VMEM((segments + GROUP, PIECES, LANES), F32),
            pltpu.VMEM((2 * rows, cols), F32),
        ],
        compiler_params=pltpu.CompilerParams(vmem_limit_bytes=56 << 20),
    )(counts, recv)
    run = rows // 8 + 2 * FRINGE
    return pl.pallas_call(
        functools.partial(finish_kernel, dims),
        name="finish",
        out_shape=jax.ShapeDtypeStruct((3, rows, cols), F32),
        in_specs=[anywhere] * 2,
        out_specs=anywhere,
        scratch_shapes=[
            pltpu.VMEM((tiles + 1, ext, LANES), F32),
            *runs,
            pltpu.VMEM((3, tiles, ext, LANES), F32),
            pltpu.VMEM((run, LANES), F32),
            pltpu.VMEM((run, LANES), F32),
            pltpu.VMEM((run, LANES), F32),
            pltpu.VMEM((run, LANES), F32),
            dma((6,)), dma((2, 2)), dma((2, 2)), dma((4, 2)), dma((3, tiles)),
        ],
        compiler_params=params(collective_id=1),
    )(fields, forcing)


def solution(mesh):
    return jax.shard_map(
        functools.partial(per_device, mesh.shape["lat"], mesh.shape["lon"]),
        mesh=mesh,
        in_specs=(
            P(None, "lat", "lon"),
            P(None, "lat", "lon"),
            P(("lat", "lon"), None),
            P(("lat", "lon"), None, None),
            P(("lat", "lon"), None),
            P(("lat", "lon"), None),
            P(("lat", "lon"), None),
            P(("lat", "lon"), None),
        ),
        out_specs=P(None, "lat", "lon"),
        check_vma=False,
    )
```

```python
import functools

import jax
import jax.numpy as jnp
from jax import lax
from jax.experimental import pallas as pl
from jax.experimental.pallas import tpu as pltpu
from jax.sharding import PartitionSpec as P

WIN = 6
WINDOWS = 4
CAP = 2
LANES = 128
ROWS8 = 8
HALO = WIN * WINDOWS
HALF = HALO // 2
FRINGE = 16
PIECES = 5
GROUP = 8
ROW_BINS = 1
COL_BINS = 2
BINS = ROW_BINS * COL_BINS
UNROLL = 32
IDS = jnp.int16
MESH = pl.DeviceIdType.MESH
F32 = jnp.float32
BF16 = jnp.bfloat16
I32 = jnp.int32


def lane_ids(shape):
    return lax.broadcasted_iota(I32, shape, len(shape) - 1)


def shift_to(me, index, lon):
    if lon != 64:
        return lax.rem(me + index, lon)
    z = (me // 8 + index % 8) % 8
    y = (me // 2 + index // 8) % 4
    x = (me + index // 32) % 2
    return (z * 4 + y) * 2 + x


def columns_at(width):
    part = LANES // width
    lane = lane_ids((ROWS8, LANES))
    part_of, inside = lane // part, lane % part
    cuts = [(width * part * t - HALO) % LANES for t in range(width)]
    into = [(width * part * t - HALO + LANES + width * inside + (part_of + width - t) % width) % LANES for t in range(width)]
    turn = [part * ((part_of + c) % width) + inside for c in range(width)]
    back = [part * ((part_of + width - c) % width) + inside for c in range(width)]
    out = []
    for t in range(width):
        along = (lane + LANES - cuts[t]) % LANES
        out.append(jnp.minimum(part * ((along + t) % width) + along // width, LANES - 1))
    return lane, part_of, cuts, into, turn, back, out


def take(values, index):
    return jnp.take_along_axis(values, index, axis=1)


def by_part(part_of, choices):
    value = choices[-1]
    for p in range(len(choices) - 1):
        value = jnp.where(part_of == p, choices[p], value)
    return value


def over(number, body):
    unroll = max(d for d in range(1, 20) if number % d == 0)

    def one(k, carry):
        body(k)
        return carry

    lax.fori_loop(0, number, one, 0, unroll=unroll)


def to_runs(maps, natural, temp, number, keep):
    lane, part_of, cuts, into, turn, back, out = maps
    width = len(cuts)
    for t in range(width):
        for f, ref in enumerate(natural):
            def sort(k):
                rows = pl.ds(k, ROWS8, stride=number)
                temp[f, t, k] = take(jnp.where(lane >= cuts[t], ref[(t - 1) % width, rows, :], ref[t, rows, :]), into[t])

            over(number, sort)
    for c in range(width):
        for f in range(len(natural)):
            def mix(k):
                value = by_part(part_of, [temp[f, (p - c) % width, k] for p in range(width)])
                keep(f, c, k, take(value, turn[c]) if c else value)

            over(number, mix)


def from_runs(maps, ref, temp, number, natural):
    lane, part_of, cuts, into, turn, back, out = maps
    width = len(cuts)
    for c in range(1, width):
        def unmix(k):
            temp[0, c, k] = take(ref[c, k], back[c])

        over(number, unmix)
    for t in range(width):
        def unsort(k):
            value = by_part(part_of, [temp[0, (p - t) % width, k] if (p - t) % width else ref[0, k] for p in range(width)])
            temp[1, t, k] = take(value, out[t])

        over(number, unsort)
    for t in range(width - 1):
        def join(k):
            natural[t, pl.ds(k, ROWS8, stride=number), :] = jnp.where(lane < cuts[t + 1], temp[1, t, k], temp[1, t + 1, k])

        over(number, join)


def one_step(old, new, east_vel, north_vel, depth_east, depth_north):
    width, number = east_vel.shape[:2]
    cols = range(width)
    for c in cols:
        old[c, number] = pltpu.roll(old[c, 0], ROWS8 - 1, 0)
    end = number - 1
    south = [pltpu.roll(north_vel[c, end] + depth_north[c, end] * (old[c, number] - old[c, end]), 1, 0) for c in cols]
    for k in range(number):
        height = [old[c, k] for c in cols]
        height_e = height[1:] + [pltpu.roll(height[0], LANES - 1, 1)]
        east = [None] * width
        for c in [width - 1] + list(range(width - 1)):
            east[c] = east_vel[c, k] + depth_east[c, k] * (height_e[c] - height[c])
        west = [pltpu.roll(east[-1], 1, 1)] + east[:-1]
        north = [None] * width
        for c in cols:
            north[c] = north_vel[c, k] + depth_north[c, k] * (old[c, k + 1] - height[c])
            new[c, k] = height[c] + (east[c] - west[c]) + (north[c] - south[c])
            east_vel[c, k] = east[c]
            north_vel[c, k] = north[c]
        south = north


def steps(number, height, other, *rest):
    def two(_, carry):
        one_step(height, other, *rest)
        one_step(other, height, *rest)
        return carry

    lax.fori_loop(0, number // 2, two, 0)


def route_kernel(dims, state, depth, innov_in, weight_in, tile_in, count_in, row_in, col_in, fields_out, recv_out, count_out,
                 fields, height, other, east_vel, north_vel, depth_east, depth_north,
                 innov, weight, tile_row, count_row, obs_row, obs_col, spots, cells, ordered, temp, send, recv, east_pack, west_pack, east_got, west_got,
                 load_sem, small_sem, row_sem, pack_sem, corner_sem, a2a_sem, own_sem, store_sem):
    rows, cols, lat, lon, blocks = dims
    tiles = cols // LANES
    ext = rows + 2 * HALO
    number = ext // ROWS8
    my_lat, my_lon = lax.axis_index("lat"), lax.axis_index("lon")
    east, west = lax.rem(my_lon + 1, lon), lax.rem(my_lon + lon - 1, lon)
    has_north, has_south = my_lat < lat - 1, my_lat > 0

    small = [pltpu.make_async_copy(source, target, small_sem.at[i]) for i, (source, target) in enumerate((
        (tile_in, tile_row), (count_in, count_row), (innov_in, innov), (weight_in, weight), (row_in, obs_row), (col_in, obs_col)))]
    for load in small:
        load.start()
    loads = []
    for t in range(tiles):
        span = pl.ds(t * LANES, LANES)
        for source, start, some in ((state, 0, 3), (depth, 3, 2)):
            loads.append(pltpu.make_async_copy(
                source.at[:, :, span], fields.at[pl.ds(start, some), t, pl.ds(HALO, rows), :], load_sem.at[len(loads)]))
    for load in loads:
        load.start()

    barrier = pltpu.get_barrier_semaphore()

    def greet(index, carry):
        pl.semaphore_signal(barrier, inc=1, device_id=(my_lat, shift_to(my_lon, index, lon)), device_id_type=MESH)
        return carry

    for has, where in ((has_north, my_lat + 1), (has_south, my_lat - 1)):
        @pl.when(has)
        def _():
            for column in (west, my_lon, east):
                pl.semaphore_signal(barrier, inc=1, device_id=(where, column), device_id_type=MESH)
    lax.fori_loop(1, lon, greet, 0)

    for load in small:
        load.wait()
    slots = innov.shape[1]
    square = (blocks, blocks)
    diagonal = lax.broadcasted_iota(I32, square, 0) == lane_ids(square)
    tile = jnp.sum(jnp.where(diagonal, tile_row[...].astype(F32), 0.0), axis=1, keepdims=True)
    count = jnp.sum(jnp.where(diagonal, count_row[...].astype(F32), 0.0), axis=1, keepdims=True)
    live = lane_ids((blocks, slots)).astype(F32) < count
    bin_rows, bin_cols = rows // ROW_BINS, cols // COL_BINS
    row_at, col_at = obs_row[...], obs_col[...]
    bin_at = row_at // bin_rows * COL_BINS + col_at // bin_cols
    cell = (bin_at * bin_rows + row_at % bin_rows) * bin_cols + col_at % bin_cols + 1
    member = [jnp.where(jnp.logical_and(live, bin_at == b), 1.0, 0.0) for b in range(BINS)]
    to_left = jnp.where(lax.broadcasted_iota(I32, (slots, slots), 0) < lane_ids((slots, slots)), 1.0, 0.0).astype(BF16)
    ahead = jnp.dot(jnp.concatenate(member, axis=0).astype(BF16), to_left, preferred_element_type=F32)
    begin = jnp.ones((blocks, 1), F32)
    spot = jnp.zeros((blocks, slots), F32)
    for b in range(BINS):
        spot += member[b] * (ahead[b * blocks:(b + 1) * blocks] + begin)
        begin += jnp.sum(member[b], axis=1, keepdims=True)
    spots[...] = spot
    innov[...] = jnp.where(live, innov[...], 0.0)
    cells[...] = jnp.where(live, cell, 0).astype(F32)
    ranks = (lax.broadcasted_iota(I32, (slots, slots), 0) + 1).astype(F32)
    sub = lax.broadcasted_iota(I32, (ROWS8 - 4, slots), 0)

    def order(b, carry):
        move = jnp.where(ranks == spots[pl.ds(b, 1), :], 1.0, 0.0).astype(BF16)
        values = weight[b] * innov[pl.ds(b, 1), :]
        data = jnp.concatenate([values, jnp.where(sub == 0, cells[pl.ds(b, 1), :], 0.0)], axis=0)
        high = data.astype(BF16).astype(F32)
        mid = (data - high).astype(BF16).astype(F32)
        parts = jnp.concatenate([high, mid, data - high - mid], axis=0).astype(BF16)
        moved = lax.dot_general(parts, move, (((1,), (1,)), ((), ())), preferred_element_type=F32)
        ordered[pl.ds(pl.multiple_of(b * ROWS8, ROWS8), ROWS8), :] = moved[:ROWS8] + moved[ROWS8:2 * ROWS8] + moved[2 * ROWS8:]
        return carry

    lax.fori_loop(0, blocks, order, 0, unroll=max(d for d in range(1, 9) if blocks % d == 0))
    named = jnp.where(tile == lane_ids((blocks, lon)).astype(F32), 1.0, 0.0)
    earlier = jnp.where(lax.broadcasted_iota(I32, square, 0) > lane_ids(square), 1.0, 0.0)
    before = jnp.dot(earlier.astype(BF16), named.astype(BF16), preferred_element_type=F32)
    rank = jnp.sum(before * named, axis=1, keepdims=True)
    place = tile * CAP + rank
    wide = (blocks, ROWS8 * blocks)
    ids = lane_ids(wide)
    row_of = jnp.where(lax.broadcasted_iota(I32, wide, 0) == ids // ROWS8, place * ROWS8 + (ids % ROWS8).astype(F32), 0.0)
    row_of = jnp.sum(row_of, axis=0, keepdims=True)
    pick = lax.broadcasted_iota(I32, (CAP * lon * ROWS8, ROWS8 * blocks), 0).astype(F32) == row_of
    pick = jnp.where(pick, 1.0, 0.0).astype(BF16)
    data = ordered[...]
    high = data.astype(BF16)
    rest = data - high.astype(F32)
    mid = rest.astype(BF16)
    low = (rest - mid.astype(F32)).astype(BF16)
    sent = (jnp.dot(pick, high, preferred_element_type=F32) + jnp.dot(pick, mid, preferred_element_type=F32)
            + jnp.dot(pick, low, preferred_element_type=F32))
    send[...] = sent.reshape(CAP * lon, ROWS8, slots)[:, :PIECES, :]

    zero_rows = jnp.zeros((5, tiles, HALO, LANES), F32)

    @pl.when(jnp.logical_not(has_south))
    def _():
        fields[:, pl.ds(0, tiles), pl.ds(0, HALO), :] = zero_rows
        east_got[pl.ds(0, HALO), :] = zero_rows[0, 0]
        west_got[pl.ds(0, HALO), :] = zero_rows[0, 0]

    @pl.when(jnp.logical_not(has_north))
    def _():
        fields[:, pl.ds(0, tiles), pl.ds(HALO + rows, HALO), :] = zero_rows
        east_got[pl.ds(HALO + rows, HALO), :] = zero_rows[0, 0]
        west_got[pl.ds(HALO + rows, HALO), :] = zero_rows[0, 0]

    for load in loads:
        load.wait()

    @pl.when(jnp.logical_not(has_north))
    def _():
        wall = pl.ds(HALO + rows - ROWS8, ROWS8)
        keep = lax.broadcasted_iota(I32, (tiles, ROWS8, LANES), 1) < ROWS8 - 1
        fields[4, pl.ds(0, tiles), wall, :] = jnp.where(keep, fields[4, pl.ds(0, tiles), wall, :], 0.0)

    lane = lane_ids((ROWS8, LANES))

    def pack(index, carry):
        base = pl.multiple_of(index * ROWS8, ROWS8)
        here = pl.ds(HALO + base, ROWS8)
        to_west = jnp.zeros((ROWS8, LANES), F32)
        to_east = to_west
        for f in range(5):
            first = HALO * f
            inside = jnp.logical_and(lane >= first, lane < first + HALO)
            to_west = jnp.where(inside, pltpu.roll(fields[f, 0, here, :], first, 1) if f else fields[f, 0, here, :], to_west)
            first = (LANES - HALO + HALO * f) % LANES
            inside = jnp.logical_and(lane >= first, lane < first + HALO)
            value = fields[f, tiles - 1, here, :]
            to_east = jnp.where(inside, pltpu.roll(value, HALO * f, 1) if f else value, to_east)
        west_pack[pl.ds(base, ROWS8), :] = to_west
        east_pack[pl.ds(base, ROWS8), :] = to_east
        return carry

    lax.fori_loop(0, rows // ROWS8, pack, 0, unroll=2)

    pl.semaphore_wait(barrier, lon - 1 + 3 * has_north.astype(I32) + 3 * has_south.astype(I32))

    def remote(source, target, sems, where):
        return pltpu.make_async_remote_copy(src_ref=source, dst_ref=target, send_sem=sems.at[0], recv_sem=sems.at[1],
                                            device_id=where, device_id_type=MESH)

    main = pl.ds(HALO, rows)
    low_rows, high_rows = pl.ds(0, HALO), pl.ds(HALO + rows, HALO)
    inner = pl.ds(0, tiles)
    to_north = remote(fields.at[:, inner, pl.ds(rows, HALO), :], fields.at[:, inner, low_rows, :], row_sem.at[0], (my_lat + 1, my_lon))
    to_south = remote(fields.at[:, inner, pl.ds(HALO, HALO), :], fields.at[:, inner, high_rows, :], row_sem.at[1], (my_lat - 1, my_lon))
    to_east = remote(east_pack, west_got.at[main], pack_sem.at[0], (my_lat, east))
    to_west = remote(west_pack, east_got.at[main], pack_sem.at[1], (my_lat, west))
    tail = pl.ds(rows - HALO, HALO)
    north_east = remote(east_pack.at[tail], west_got.at[low_rows], corner_sem.at[0], (my_lat + 1, east))
    north_west = remote(west_pack.at[tail], east_got.at[low_rows], corner_sem.at[1], (my_lat + 1, west))
    south_east = remote(east_pack.at[low_rows], west_got.at[high_rows], corner_sem.at[2], (my_lat - 1, east))
    south_west = remote(west_pack.at[low_rows], east_got.at[high_rows], corner_sem.at[3], (my_lat - 1, west))
    northward, southward = (to_north, north_east, north_west), (to_south, south_east, south_west)

    @pl.when(has_north)
    def _():
        for copy in northward:
            copy.start()

    @pl.when(has_south)
    def _():
        for copy in southward:
            copy.start()

    to_east.start()
    to_west.start()

    def block_copy(index):
        where = shift_to(my_lon, index, lon)
        return remote(send.at[pl.ds(CAP * where, CAP)], recv.at[pl.ds(CAP * my_lon, CAP)], a2a_sem, (my_lat, where))

    def send_blocks(index, carry):
        block_copy(index).start()
        return carry

    lax.fori_loop(1, lon, send_blocks, 0)
    mine = pl.ds(CAP * my_lon, CAP)
    own = pltpu.make_async_copy(send.at[mine], recv.at[mine], own_sem)
    own.start()

    @pl.when(has_south)
    def _():
        for copy in northward:
            copy.wait_recv()

    @pl.when(has_north)
    def _():
        for copy in southward:
            copy.wait_recv()

    to_east.wait_recv()
    to_west.wait_recv()

    def unpack(index, carry):
        here = pl.ds(pl.multiple_of(index * ROWS8, ROWS8), ROWS8)
        from_east, from_west = east_got[here, :], west_got[here, :]
        for f in range(5):
            first = HALO * f
            right = jnp.logical_and(lane >= first, lane < first + HALO)
            first = (LANES - HALO + HALO * f) % LANES
            left = jnp.logical_and(lane >= first, lane < first + HALO)
            both = jnp.where(right, from_east, jnp.where(left, from_west, 0.0))
            fields[f, tiles, here, :] = pltpu.roll(both, LANES - HALO * f, 1) if f else both
        return carry

    lax.fori_loop(0, ext // ROWS8, unpack, 0, unroll=2)

    @pl.when(has_north)
    def _():
        for copy in northward:
            copy.wait_send()

    @pl.when(has_south)
    def _():
        for copy in southward:
            copy.wait_send()

    to_east.wait_send()
    to_west.wait_send()

    refs = (height, east_vel, north_vel, depth_east, depth_north)
    maps = columns_at(tiles + 1)

    def keep(f, c, k, value):
        refs[f][c, k] = value

    to_runs(maps, [fields.at[f] for f in range(5)], temp, number, keep)
    inner = pl.ds(0, number)
    stores = [pltpu.make_async_copy(ref.at[:, inner], fields_out.at[f], store_sem.at[f]) for f, ref in enumerate(refs)]
    for store in stores[3:]:
        store.start()
    steps(HALF, height, other, *refs[1:])
    for store in stores[:3]:
        store.start()

    own.wait()
    others = pl.ds(0, CAP * (lon - 1))
    every = pltpu.make_async_remote_copy(src_ref=send.at[others], dst_ref=recv.at[others], send_sem=a2a_sem.at[0],
                                         recv_sem=a2a_sem.at[1], device_id=(my_lat, east), device_id_type=MESH)
    every.wait_recv()
    stores.append(pltpu.make_async_copy(recv, recv_out, store_sem.at[5]))
    stores[5].start()
    cell = recv[:, PIECES - 1, :]
    ones = jnp.ones((ROWS8, slots), BF16)
    area = float(bin_rows * bin_cols)
    for b in range(BINS):
        within = jnp.logical_and(cell > b * area, cell <= (b + 1) * area)
        live_of = lax.dot_general(ones, jnp.where(within, 1.0, 0.0).astype(BF16), (((1,), (1,)), ((), ())), preferred_element_type=F32)
        count_out[pl.ds(b, 1), :] = live_of[:1].astype(I32)
    count_out[pl.ds(BINS, ROWS8 - BINS), :] = jnp.zeros((ROWS8 - BINS, CAP * lon), I32)
    every.wait_send()
    for store in stores:
        store.wait()


def spread_kernel(dims, counts, recv, out, packed, total, left_a, left_b, right_a, right_b):
    rows, cols, lat, lon, blocks = dims
    tiles = cols // LANES
    segments = CAP * lon
    bin_rows, bin_cols = rows // ROW_BINS, cols // COL_BINS
    bins = ROW_BINS * COL_BINS
    padded = left_a.shape[0] // 2
    depth = GROUP * LANES
    room = segments + GROUP
    lane = lane_ids((PIECES, LANES))
    zero = jnp.zeros((PIECES, LANES), F32)

    def append(segment, carry):
        block = recv[segment]
        begin = 0
        after = []
        for b, (fill, current) in enumerate(carry):
            number = counts[b, segment]
            chunk = lax.shift_right_logical(fill, 7)
            turned = pltpu.roll(block, (fill - begin) & (LANES - 1), 1)
            current = jnp.where(lane >= (fill & (LANES - 1)), turned, current)
            packed[chunk + b * room] = current
            begin = begin + number
            fill = fill + number
            after.append((fill, jnp.where(lax.shift_right_logical(fill, 7) > chunk, turned, current)))
        return tuple(after)

    filled = lax.fori_loop(0, segments, append, ((jnp.int32(0), zero),) * bins, unroll=min(UNROLL, segments))
    jobs, starts = [], [0]
    for b, (fill, current) in enumerate(filled):
        chunk = lax.shift_right_logical(fill, 7) + b * room
        packed[chunk] = jnp.where(lane < (fill & (LANES - 1)), current, 0.0)
        for extra in range(1, GROUP):
            packed[chunk + extra] = zero
        starts.append(starts[-1] + (fill + depth - 1) // depth)
    for extra in range(GROUP):
        packed[bins * room + extra] = zero
    total[...] = jnp.zeros_like(total)
    count = starts[-1]

    def place(job):
        which = 0
        begin = 0
        for b in range(1, bins):
            past = job >= starts[b]
            which = jnp.where(past, b, which)
            begin = jnp.where(past, starts[b], begin)
        chunk = which * room + (job - begin) * GROUP
        return jnp.where(job < count, chunk, bins * room), jnp.where(job < count, which, 0)

    row_ids = lax.broadcasted_iota(IDS, (padded, depth), 0)
    col_ids = lax.broadcasted_iota(IDS, (bin_cols, depth), 0)
    one, none = jnp.array(1, BF16), jnp.array(0, BF16)

    def build(job, left, right):
        chunk, which = place(job)
        both = jnp.concatenate([packed[chunk + j] for j in range(GROUP)], axis=1)
        cell = both[4:5, :].astype(I32) - 1 - which * (bin_rows * bin_cols)
        row_at = cell // bin_cols if bin_cols & (bin_cols - 1) else lax.shift_right_arithmetic(cell, bin_cols.bit_length() - 1)
        col_at = cell - row_at * bin_cols

        def wide(value, kind, number):
            return jnp.broadcast_to(value, (number, depth)).astype(kind)

        here = row_ids == wide(row_at, IDS, padded)
        past = row_ids == wide(row_at + 1, IDS, padded)
        column = jnp.where(col_ids == wide(col_at, IDS, bin_cols), one, none)
        right[:, :depth] = column
        right[:, depth:] = column
        high = both[:4, :].astype(BF16).astype(F32)
        for part, values in enumerate((high, both[:4, :] - high)):
            for side in range(2):
                at = wide(values[side:side + 1, :], BF16, padded)
                above = wide(values[side + 2:side + 3, :], BF16, padded)
                left[pl.ds(side * padded, padded), pl.ds(part * depth, depth)] = jnp.where(here, at, jnp.where(past, above, none))

    def add(job, left, right):
        _, which = place(job)
        total[which] += lax.dot_general(left[...], right[...], (((1,), (1,)), ((), ())), preferred_element_type=F32)

    build(0, left_a, right_a)

    def pair(index, carry):
        build(2 * index + 1, left_b, right_b)
        add(2 * index, left_a, right_a)
        build(2 * index + 2, left_a, right_a)
        add(2 * index + 1, left_b, right_b)
        return carry

    lax.fori_loop(0, (count + 1) // 2, pair, 0)

    bin_tiles = bin_cols // LANES
    lane = lane_ids((bin_rows, LANES))
    for i in range(ROW_BINS):
        if i:
            for j in range(COL_BINS):
                for at in (0, padded):
                    total[i * COL_BINS + j, pl.ds(at, ROWS8), :] += total[(i - 1) * COL_BINS + j, pl.ds(at + bin_rows, ROWS8), :]
        before = jnp.zeros((bin_rows, LANES), F32)
        for t in range(tiles):
            which, span = i * COL_BINS + t // bin_tiles, pl.ds(t % bin_tiles * LANES, LANES)
            turned = pltpu.roll(total[which, pl.ds(padded, bin_rows), span], 1, 1)
            out[t, pl.ds(i * bin_rows, bin_rows), :] = total[which, pl.ds(0, bin_rows), span] + jnp.where(lane == 0, before, turned)
            before = turned


def finish_kernel(dims, fields_in, forcing_in, out, forcing, height, other, east_vel, north_vel, depth_east, depth_north, temp, done,
                  east_pack, west_pack, east_got, west_got, load_sem, row_sem, pack_sem, corner_sem, store_sem):
    rows, cols, lat, lon, blocks = dims
    tiles = cols // LANES
    ext = rows + 2 * HALO
    number = ext // ROWS8
    my_lat, my_lon = lax.axis_index("lat"), lax.axis_index("lon")
    east, west = lax.rem(my_lon + 1, lon), lax.rem(my_lon + lon - 1, lon)
    has_north, has_south = my_lat < lat - 1, my_lat > 0
    refs = (height, east_vel, north_vel, depth_east, depth_north)
    inner = pl.ds(0, number)
    loads = [pltpu.make_async_copy(forcing_in, forcing.at[pl.ds(0, tiles), pl.ds(HALO, rows), :], load_sem.at[5])]
    loads += [pltpu.make_async_copy(fields_in.at[f], ref.at[:, inner], load_sem.at[f]) for f, ref in enumerate(refs)]
    for load in loads:
        load.start()
    barrier = pltpu.get_barrier_semaphore()
    for has, where in ((has_north, my_lat + 1), (has_south, my_lat - 1)):
        @pl.when(has)
        def _():
            for column in (west, my_lon, east):
                pl.semaphore_signal(barrier, inc=1, device_id=(where, column), device_id_type=MESH)
    for column in (west, east):
        pl.semaphore_signal(barrier, inc=1, device_id=(my_lat, column), device_id_type=MESH)

    beyond = HALO - FRINGE
    for at in (0, ext - beyond):
        forcing[:, pl.ds(at, beyond), :] = jnp.zeros((tiles + 1, beyond, LANES), F32)
    for has, at in ((has_south, beyond), (has_north, HALO + rows)):
        @pl.when(jnp.logical_not(has))
        def _():
            forcing[:, pl.ds(at, FRINGE), :] = jnp.zeros((tiles + 1, FRINGE, LANES), F32)

    loads[0].wait()
    run = rows // 8
    lane = lane_ids((run, LANES))
    to_west = jnp.zeros((run, LANES), F32)
    to_east = to_west
    for g in range(8):
        here = pl.ds(HALO + run * g, run)
        inside = lane // FRINGE == g
        value = forcing[0, here, :]
        to_west = jnp.where(inside, pltpu.roll(value, FRINGE * g, 1) if g else value, to_west)
        value = forcing[tiles - 1, here, :]
        to_east = jnp.where(inside, pltpu.roll(value, (FRINGE * (g + 1)) % LANES, 1) if g < 7 else value, to_east)
    west_pack[pl.ds(0, run), :] = to_west
    east_pack[pl.ds(0, run), :] = to_east
    ends = (pl.ds(HALO, FRINGE), pl.ds(HALO + rows - FRINGE, FRINGE))
    outer = (pl.ds(HALO - FRINGE, FRINGE), pl.ds(HALO + rows, FRINGE))
    for at, here in zip((run, run + FRINGE), ends):
        west_pack[pl.ds(at, FRINGE), :] = forcing[0, here, :]
        east_pack[pl.ds(at, FRINGE), :] = forcing[tiles - 1, here, :]

    pl.semaphore_wait(barrier, 2 + 3 * has_north.astype(I32) + 3 * has_south.astype(I32))

    def remote(source, target, sems, where):
        return pltpu.make_async_remote_copy(src_ref=source, dst_ref=target, send_sem=sems.at[0], recv_sem=sems.at[1],
                                            device_id=where, device_id_type=MESH)

    main = pl.ds(0, tiles)
    strip, low_end, high_end = pl.ds(0, run), pl.ds(run, FRINGE), pl.ds(run + FRINGE, FRINGE)
    to_north = remote(forcing.at[main, ends[1], :], forcing.at[main, outer[0], :], row_sem.at[0], (my_lat + 1, my_lon))
    to_south = remote(forcing.at[main, ends[0], :], forcing.at[main, outer[1], :], row_sem.at[1], (my_lat - 1, my_lon))
    go_east = remote(east_pack.at[strip], west_got.at[strip], pack_sem.at[0], (my_lat, east))
    go_west = remote(west_pack.at[strip], east_got.at[strip], pack_sem.at[1], (my_lat, west))
    north_east = remote(east_pack.at[high_end], west_got.at[low_end], corner_sem.at[0], (my_lat + 1, east))
    north_west = remote(west_pack.at[high_end], east_got.at[low_end], corner_sem.at[1], (my_lat + 1, west))
    south_east = remote(east_pack.at[low_end], west_got.at[high_end], corner_sem.at[2], (my_lat - 1, east))
    south_west = remote(west_pack.at[low_end], east_got.at[high_end], corner_sem.at[3], (my_lat - 1, west))
    northward, southward = (to_north, north_east, north_west), (to_south, south_east, south_west)

    @pl.when(has_north)
    def _():
        for copy in northward:
            copy.start()

    @pl.when(has_south)
    def _():
        for copy in southward:
            copy.start()

    go_east.start()
    go_west.start()

    for load in loads[1:]:
        load.wait()

    @pl.when(has_south)
    def _():
        for copy in northward:
            copy.wait_recv()

    @pl.when(has_north)
    def _():
        for copy in southward:
            copy.wait_recv()

    go_east.wait_recv()
    go_west.wait_recv()
    right = lane < FRINGE
    left = lane >= LANES - FRINGE
    from_east, from_west = east_got[strip, :], west_got[strip, :]
    for g in range(8):
        here = pl.ds(HALO + run * g, run)
        one = pltpu.roll(from_east, (LANES - FRINGE * g) % LANES, 1) if g else from_east
        two = pltpu.roll(from_west, (LANES - FRINGE * (g + 1)) % LANES, 1) if g < 7 else from_west
        forcing[tiles, here, :] = jnp.where(right, one, jnp.where(left, two, 0.0))
    lane = lane_ids((FRINGE, LANES))
    right = lane < FRINGE
    left = lane >= LANES - FRINGE
    for has, end, at in ((has_south, low_end, HALO - FRINGE), (has_north, high_end, HALO + rows)):
        @pl.when(has)
        def _():
            forcing[tiles, pl.ds(at, FRINGE), :] = jnp.where(right, east_got[end, :], jnp.where(left, west_got[end, :], 0.0))

    maps = columns_at(tiles + 1)

    def keep(f, c, k, value):
        height[c, k] += value

    to_runs(maps, [forcing], temp, number, keep)
    steps(HALF, height, other, *refs[1:])
    stores = []
    for f in range(3):
        from_runs(maps, refs[f], temp, number, done.at[f])
        for t in range(tiles):
            store = pltpu.make_async_copy(done.at[f, t, pl.ds(HALO, rows), :],
                                          out.at[f, :, pl.ds(t * LANES, LANES)], store_sem.at[f, t])
            store.start()
            stores.append(store)

    @pl.when(has_north)
    def _():
        for copy in northward:
            copy.wait_send()

    @pl.when(has_south)
    def _():
        for copy in southward:
            copy.wait_send()

    go_east.wait_send()
    go_west.wait_send()
    for store in stores:
        store.wait()


def per_device(lat, lon, adjoint_state, face_depth, innovation, interp_weight, block_tile, block_count, obs_row, obs_col):
    rows, cols = adjoint_state.shape[1:]
    blocks, slots = innovation.shape
    tiles = cols // LANES
    dims = (rows, cols, lat, lon, blocks)
    ext = rows + 2 * HALO
    segments = CAP * lon
    vmem = pl.BlockSpec(memory_space=pltpu.VMEM)
    anywhere = pl.BlockSpec(memory_space=pl.ANY)
    dma = pltpu.SemaphoreType.DMA
    number = ext // ROWS8
    natural = pltpu.VMEM((5, tiles + 1, ext, LANES), F32)
    runs = [pltpu.VMEM((tiles + 1, number + 1, ROWS8, LANES), F32)] * 2 + [pltpu.VMEM((tiles + 1, number, ROWS8, LANES), F32)] * 4
    params = functools.partial(pltpu.CompilerParams, has_side_effects=True)
    fields, recv, counts = pl.pallas_call(
        functools.partial(route_kernel, dims),
        name="route",
        out_shape=(
            jax.ShapeDtypeStruct((5, tiles + 1, number, ROWS8, LANES), F32),
            jax.ShapeDtypeStruct((segments, PIECES, slots), F32),
            jax.ShapeDtypeStruct((ROWS8, segments), I32),
        ),
        in_specs=[anywhere] * 8,
        out_specs=(anywhere, anywhere, vmem),
        scratch_shapes=[
            natural, *runs,
            pltpu.VMEM((blocks, slots), F32),
            pltpu.VMEM((blocks, 4, slots), F32),
            pltpu.VMEM((1, blocks), I32),
            pltpu.VMEM((1, blocks), I32),
            pltpu.VMEM((blocks, slots), I32),
            pltpu.VMEM((blocks, slots), I32),
            pltpu.VMEM((blocks, slots), F32),
            pltpu.VMEM((blocks, slots), F32),
            pltpu.VMEM((ROWS8 * blocks, slots), F32),
            pltpu.VMEM((5, tiles + 1, number, ROWS8, LANES), F32),
            pltpu.VMEM((segments, PIECES, slots), F32),
            pltpu.VMEM((segments, PIECES, slots), F32),
            pltpu.VMEM((rows, LANES), F32),
            pltpu.VMEM((rows, LANES), F32),
            pltpu.VMEM((ext, LANES), F32),
            pltpu.VMEM((ext, LANES), F32),
            dma((2 * tiles,)), dma((6,)), dma((2, 2)), dma((2, 2)), dma((4, 2)), dma((2,)), dma, dma((6,)),
        ],
        compiler_params=params(collective_id=0, vmem_limit_bytes=56 << 20),
    )(adjoint_state, face_depth, innovation, interp_weight, block_tile.reshape(1, blocks), block_count.reshape(1, blocks),
      obs_row, obs_col)
    padded = rows if ROW_BINS == 1 else rows // ROW_BINS + 16
    forcing = pl.pallas_call(
        functools.partial(spread_kernel, dims),
        name="spread",
        out_shape=jax.ShapeDtypeStruct((tiles, rows, LANES), F32),
        in_specs=[pl.BlockSpec(memory_space=pltpu.SMEM), vmem],
        out_specs=vmem,
        scratch_shapes=[
            pltpu.VMEM((BINS * (segments + GROUP) + GROUP, PIECES, LANES), F32),
            pltpu.VMEM((BINS, 2 * padded, cols // COL_BINS), F32),
            *[pltpu.VMEM((2 * padded, 2 * GROUP * LANES), BF16)] * 2,
            *[pltpu.VMEM((cols // COL_BINS, 2 * GROUP * LANES), BF16)] * 2,
        ],
        compiler_params=pltpu.CompilerParams(vmem_limit_bytes=24 << 20),
    )(counts, recv)
    run = rows // 8 + 2 * FRINGE
    return pl.pallas_call(
        functools.partial(finish_kernel, dims),
        name="finish",
        out_shape=jax.ShapeDtypeStruct((3, rows, cols), F32),
        in_specs=[anywhere] * 2,
        out_specs=anywhere,
        scratch_shapes=[
            pltpu.VMEM((tiles + 1, ext, LANES), F32),
            *runs,
            pltpu.VMEM((2, tiles + 1, number, ROWS8, LANES), F32),
            pltpu.VMEM((3, tiles, ext, LANES), F32),
            pltpu.VMEM((run, LANES), F32),
            pltpu.VMEM((run, LANES), F32),
            pltpu.VMEM((run, LANES), F32),
            pltpu.VMEM((run, LANES), F32),
            dma((6,)), dma((2, 2)), dma((2, 2)), dma((4, 2)), dma((3, tiles)),
        ],
        compiler_params=params(collective_id=1, vmem_limit_bytes=50 << 20),
    )(fields, forcing)


def solution(mesh):
    return jax.shard_map(
        functools.partial(per_device, mesh.shape["lat"], mesh.shape["lon"]),
        mesh=mesh,
        in_specs=(
            P(None, "lat", "lon"),
            P(None, "lat", "lon"),
            P(("lat", "lon"), None),
            P(("lat", "lon"), None, None),
            P(("lat", "lon"), None),
            P(("lat", "lon"), None),
            P(("lat", "lon"), None),
            P(("lat", "lon"), None),
        ),
        out_specs=P(None, "lat", "lon"),
        check_vma=False,
    )
```

```python
import functools

import jax
import jax.numpy as jnp
from jax import lax
from jax.experimental import pallas as pl
from jax.experimental.pallas import tpu as pltpu
from jax.sharding import PartitionSpec as P

WIN = 6
WINDOWS = 4
CAP = 2
LANES = 128
ROWS8 = 8
HALO = WIN * WINDOWS
HALF = HALO // 2
FRINGE = 16
PIECES = 5
GROUP = 8
ROW_BINS = 1
COL_BINS = 2
BINS = ROW_BINS * COL_BINS
UNROLL = 32
IDS = jnp.int16
MESH = pl.DeviceIdType.MESH
F32 = jnp.float32
BF16 = jnp.bfloat16
I32 = jnp.int32


def lane_ids(shape):
    return lax.broadcasted_iota(I32, shape, len(shape) - 1)


def shift_to(me, index, lon):
    if lon != 64:
        return lax.rem(me + index, lon)
    z = (me // 8 + index % 8) % 8
    y = (me // 2 + index // 8) % 4
    x = (me + index // 32) % 2
    return (z * 4 + y) * 2 + x


def columns_at(width):
    part = LANES // width
    lane = lane_ids((ROWS8, LANES))
    part_of, inside = lane // part, lane % part
    cuts = [(width * part * t - HALO) % LANES for t in range(width)]
    into = [(width * part * t - HALO + LANES + width * inside + (part_of + width - t) % width) % LANES for t in range(width)]
    turn = [part * ((part_of + c) % width) + inside for c in range(width)]
    back = [part * ((part_of + width - c) % width) + inside for c in range(width)]
    out = []
    for t in range(width):
        along = (lane + LANES - cuts[t]) % LANES
        out.append(jnp.minimum(part * ((along + t) % width) + along // width, LANES - 1))
    return lane, part_of, cuts, into, turn, back, out


def take(values, index):
    return jnp.take_along_axis(values, index, axis=1)


def by_part(part_of, choices):
    value = choices[-1]
    for p in range(len(choices) - 1):
        value = jnp.where(part_of == p, choices[p], value)
    return value


def over(number, body, most):
    unroll = max(d for d in range(1, number + 1) if number % d == 0 and d <= max(most, 1))

    def one(k, carry):
        body(k)
        return carry

    lax.fori_loop(0, number, one, 0, unroll=unroll)


def to_runs(maps, natural, temp, number, keep):
    lane, part_of, cuts, into, turn, back, out = maps
    width = len(cuts)
    most = 100 // len(natural)
    for t in range(width):
        def sort(k):
            rows = pl.ds(k, ROWS8, stride=number)
            for f, ref in enumerate(natural):
                temp[f, t, k] = take(jnp.where(lane >= cuts[t], ref[(t - 1) % width, rows, :], ref[t, rows, :]), into[t])

        over(number, sort, most)
    for c in range(width):
        def mix(k):
            for f in range(len(natural)):
                value = by_part(part_of, [temp[f, (p - c) % width, k] for p in range(width)])
                keep(f, c, k, take(value, turn[c]) if c else value)

        over(number, mix, most)


def from_runs(maps, refs, temp, number, natural, finished):
    lane, part_of, cuts, into, turn, back, out = maps
    width, fields = len(cuts), len(refs)
    most = 120 // fields
    for c in range(1, width):
        def unmix(k):
            for f in range(fields):
                temp[f, c, k] = take(refs[f][c, k], back[c])

        over(number, unmix, most)
    for t in range(width):
        def unsort(k):
            for f in range(fields):
                parts = [(p - t) % width for p in range(width)]
                value = by_part(part_of, [temp[f, c, k] if c else refs[f][0, k] for c in parts])
                temp[fields + f, t, k] = take(value, out[t])

        over(number, unsort, most)
        if t:
            def join(k):
                for f in range(fields):
                    value = jnp.where(lane < cuts[t], temp[fields + f, t - 1, k], temp[fields + f, t, k])
                    natural[f, t - 1, pl.ds(k, ROWS8, stride=number), :] = value

            over(number, join, most)
            finished(t - 1)


def one_step(old, new, east_vel, north_vel, depth_east, depth_north):
    width, number = east_vel.shape[:2]
    cols = range(width)
    for c in cols:
        old[c, number] = pltpu.roll(old[c, 0], ROWS8 - 1, 0)
    end = number - 1
    south = [pltpu.roll(north_vel[c, end] + depth_north[c, end] * (old[c, number] - old[c, end]), 1, 0) for c in cols]
    for k in range(number):
        height = [old[c, k] for c in cols]
        height_e = height[1:] + [pltpu.roll(height[0], LANES - 1, 1)]
        east = [None] * width
        for c in [width - 1] + list(range(width - 1)):
            east[c] = east_vel[c, k] + depth_east[c, k] * (height_e[c] - height[c])
        west = [pltpu.roll(east[-1], 1, 1)] + east[:-1]
        north = [None] * width
        for c in cols:
            north[c] = north_vel[c, k] + depth_north[c, k] * (old[c, k + 1] - height[c])
            new[c, k] = height[c] + (east[c] - west[c]) + (north[c] - south[c])
            east_vel[c, k] = east[c]
            north_vel[c, k] = north[c]
        south = north


def steps(number, height, other, *rest):
    def two(_, carry):
        one_step(height, other, *rest)
        one_step(other, height, *rest)
        return carry

    lax.fori_loop(0, number // 2, two, 0)


def route_kernel(dims, state, depth, innov_in, weight_in, tile_in, count_in, row_in, col_in, fields_out, recv_out, count_out,
                 fields, height, other, east_vel, north_vel, depth_east, depth_north,
                 innov, weight, tile_row, count_row, obs_row, obs_col, spots, cells, ordered, temp, send, recv, east_pack, west_pack, east_got, west_got,
                 load_sem, small_sem, row_sem, pack_sem, corner_sem, a2a_sem, own_sem, store_sem):
    rows, cols, lat, lon, blocks = dims
    tiles = cols // LANES
    ext = rows + 2 * HALO
    number = ext // ROWS8
    my_lat, my_lon = lax.axis_index("lat"), lax.axis_index("lon")
    east, west = lax.rem(my_lon + 1, lon), lax.rem(my_lon + lon - 1, lon)
    has_north, has_south = my_lat < lat - 1, my_lat > 0

    small = [pltpu.make_async_copy(source, target, small_sem.at[i]) for i, (source, target) in enumerate((
        (tile_in, tile_row), (count_in, count_row), (innov_in, innov), (weight_in, weight), (row_in, obs_row), (col_in, obs_col)))]
    for load in small:
        load.start()
    loads = []
    for t in range(tiles):
        span = pl.ds(t * LANES, LANES)
        for source, start, some in ((state, 0, 3), (depth, 3, 2)):
            loads.append(pltpu.make_async_copy(
                source.at[:, :, span], fields.at[pl.ds(start, some), t, pl.ds(HALO, rows), :], load_sem.at[len(loads)]))
    for load in loads:
        load.start()

    barrier = pltpu.get_barrier_semaphore()

    def greet(index, carry):
        pl.semaphore_signal(barrier, inc=1, device_id=(my_lat, shift_to(my_lon, index, lon)), device_id_type=MESH)
        return carry

    for has, where in ((has_north, my_lat + 1), (has_south, my_lat - 1)):
        @pl.when(has)
        def _():
            for column in (west, my_lon, east):
                pl.semaphore_signal(barrier, inc=1, device_id=(where, column), device_id_type=MESH)
    lax.fori_loop(1, lon, greet, 0)

    for load in small:
        load.wait()
    slots = innov.shape[1]
    square = (blocks, blocks)
    diagonal = lax.broadcasted_iota(I32, square, 0) == lane_ids(square)
    tile = jnp.sum(jnp.where(diagonal, tile_row[...].astype(F32), 0.0), axis=1, keepdims=True)
    count = jnp.sum(jnp.where(diagonal, count_row[...].astype(F32), 0.0), axis=1, keepdims=True)
    live = lane_ids((blocks, slots)).astype(F32) < count
    bin_rows, bin_cols = rows // ROW_BINS, cols // COL_BINS
    row_at, col_at = obs_row[...], obs_col[...]
    bin_at = row_at // bin_rows * COL_BINS + col_at // bin_cols
    cell = (bin_at * bin_rows + row_at % bin_rows) * bin_cols + col_at % bin_cols + 1
    member = [jnp.where(jnp.logical_and(live, bin_at == b), 1.0, 0.0) for b in range(BINS)]
    to_left = jnp.where(lax.broadcasted_iota(I32, (slots, slots), 0) < lane_ids((slots, slots)), 1.0, 0.0).astype(BF16)
    ahead = jnp.dot(jnp.concatenate(member, axis=0).astype(BF16), to_left, preferred_element_type=F32)
    begin = jnp.ones((blocks, 1), F32)
    spot = jnp.zeros((blocks, slots), F32)
    for b in range(BINS):
        spot += member[b] * (ahead[b * blocks:(b + 1) * blocks] + begin)
        begin += jnp.sum(member[b], axis=1, keepdims=True)
    spots[...] = spot
    innov[...] = jnp.where(live, innov[...], 0.0)
    cells[...] = jnp.where(live, cell, 0).astype(F32)
    ranks = (lax.broadcasted_iota(I32, (slots, slots), 0) + 1).astype(F32)
    sub = lax.broadcasted_iota(I32, (ROWS8 - 4, slots), 0)

    def order(b, carry):
        move = jnp.where(ranks == spots[pl.ds(b, 1), :], 1.0, 0.0).astype(BF16)
        values = weight[b] * innov[pl.ds(b, 1), :]
        data = jnp.concatenate([values, jnp.where(sub == 0, cells[pl.ds(b, 1), :], 0.0)], axis=0)
        high = data.astype(BF16).astype(F32)
        mid = (data - high).astype(BF16).astype(F32)
        parts = jnp.concatenate([high, mid, data - high - mid], axis=0).astype(BF16)
        moved = lax.dot_general(parts, move, (((1,), (1,)), ((), ())), preferred_element_type=F32)
        ordered[pl.ds(pl.multiple_of(b * ROWS8, ROWS8), ROWS8), :] = moved[:ROWS8] + moved[ROWS8:2 * ROWS8] + moved[2 * ROWS8:]
        return carry

    lax.fori_loop(0, blocks, order, 0, unroll=max(d for d in range(1, 17) if blocks % d == 0))
    named = jnp.where(tile == lane_ids((blocks, lon)).astype(F32), 1.0, 0.0)
    earlier = jnp.where(lax.broadcasted_iota(I32, square, 0) > lane_ids(square), 1.0, 0.0)
    before = jnp.dot(earlier.astype(BF16), named.astype(BF16), preferred_element_type=F32)
    rank = jnp.sum(before * named, axis=1, keepdims=True)
    place = tile * CAP + rank
    wide = (blocks, ROWS8 * blocks)
    ids = lane_ids(wide)
    row_of = jnp.where(lax.broadcasted_iota(I32, wide, 0) == ids // ROWS8, place * ROWS8 + (ids % ROWS8).astype(F32), 0.0)
    row_of = jnp.sum(row_of, axis=0, keepdims=True)
    pick = lax.broadcasted_iota(I32, (CAP * lon * ROWS8, ROWS8 * blocks), 0).astype(F32) == row_of
    pick = jnp.where(pick, 1.0, 0.0).astype(BF16)
    data = ordered[...]
    high = data.astype(BF16)
    rest = data - high.astype(F32)
    mid = rest.astype(BF16)
    low = (rest - mid.astype(F32)).astype(BF16)
    sent = (jnp.dot(pick, high, preferred_element_type=F32) + jnp.dot(pick, mid, preferred_element_type=F32)
            + jnp.dot(pick, low, preferred_element_type=F32))
    send[...] = sent.reshape(CAP * lon, ROWS8, slots)[:, :PIECES, :]

    zero_rows = jnp.zeros((5, tiles, HALO, LANES), F32)

    @pl.when(jnp.logical_not(has_south))
    def _():
        fields[:, pl.ds(0, tiles), pl.ds(0, HALO), :] = zero_rows
        east_got[pl.ds(0, HALO), :] = zero_rows[0, 0]
        west_got[pl.ds(0, HALO), :] = zero_rows[0, 0]

    @pl.when(jnp.logical_not(has_north))
    def _():
        fields[:, pl.ds(0, tiles), pl.ds(HALO + rows, HALO), :] = zero_rows
        east_got[pl.ds(HALO + rows, HALO), :] = zero_rows[0, 0]
        west_got[pl.ds(HALO + rows, HALO), :] = zero_rows[0, 0]

    for load in loads:
        load.wait()

    @pl.when(jnp.logical_not(has_north))
    def _():
        wall = pl.ds(HALO + rows - ROWS8, ROWS8)
        keep = lax.broadcasted_iota(I32, (tiles, ROWS8, LANES), 1) < ROWS8 - 1
        fields[4, pl.ds(0, tiles), wall, :] = jnp.where(keep, fields[4, pl.ds(0, tiles), wall, :], 0.0)

    lane = lane_ids((ROWS8, LANES))

    def pack(index, carry):
        base = pl.multiple_of(index * ROWS8, ROWS8)
        here = pl.ds(HALO + base, ROWS8)
        to_west = jnp.zeros((ROWS8, LANES), F32)
        to_east = to_west
        for f in range(5):
            first = HALO * f
            inside = jnp.logical_and(lane >= first, lane < first + HALO)
            to_west = jnp.where(inside, pltpu.roll(fields[f, 0, here, :], first, 1) if f else fields[f, 0, here, :], to_west)
            first = (LANES - HALO + HALO * f) % LANES
            inside = jnp.logical_and(lane >= first, lane < first + HALO)
            value = fields[f, tiles - 1, here, :]
            to_east = jnp.where(inside, pltpu.roll(value, HALO * f, 1) if f else value, to_east)
        west_pack[pl.ds(base, ROWS8), :] = to_west
        east_pack[pl.ds(base, ROWS8), :] = to_east
        return carry

    lax.fori_loop(0, rows // ROWS8, pack, 0, unroll=8)

    pl.semaphore_wait(barrier, lon - 1 + 3 * has_north.astype(I32) + 3 * has_south.astype(I32))

    def remote(source, target, sems, where):
        return pltpu.make_async_remote_copy(src_ref=source, dst_ref=target, send_sem=sems.at[0], recv_sem=sems.at[1],
                                            device_id=where, device_id_type=MESH)

    main = pl.ds(HALO, rows)
    low_rows, high_rows = pl.ds(0, HALO), pl.ds(HALO + rows, HALO)
    inner = pl.ds(0, tiles)
    to_north = remote(fields.at[:, inner, pl.ds(rows, HALO), :], fields.at[:, inner, low_rows, :], row_sem.at[0], (my_lat + 1, my_lon))
    to_south = remote(fields.at[:, inner, pl.ds(HALO, HALO), :], fields.at[:, inner, high_rows, :], row_sem.at[1], (my_lat - 1, my_lon))
    to_east = remote(east_pack, west_got.at[main], pack_sem.at[0], (my_lat, east))
    to_west = remote(west_pack, east_got.at[main], pack_sem.at[1], (my_lat, west))
    tail = pl.ds(rows - HALO, HALO)
    north_east = remote(east_pack.at[tail], west_got.at[low_rows], corner_sem.at[0], (my_lat + 1, east))
    north_west = remote(west_pack.at[tail], east_got.at[low_rows], corner_sem.at[1], (my_lat + 1, west))
    south_east = remote(east_pack.at[low_rows], west_got.at[high_rows], corner_sem.at[2], (my_lat - 1, east))
    south_west = remote(west_pack.at[low_rows], east_got.at[high_rows], corner_sem.at[3], (my_lat - 1, west))
    northward, southward = (to_north, north_east, north_west), (to_south, south_east, south_west)

    @pl.when(has_north)
    def _():
        for copy in northward:
            copy.start()

    @pl.when(has_south)
    def _():
        for copy in southward:
            copy.start()

    to_east.start()
    to_west.start()

    def block_copy(index):
        where = shift_to(my_lon, index, lon)
        return remote(send.at[pl.ds(CAP * where, CAP)], recv.at[pl.ds(CAP * my_lon, CAP)], a2a_sem, (my_lat, where))

    def send_blocks(index, carry):
        block_copy(index).start()
        return carry

    lax.fori_loop(1, lon, send_blocks, 0)
    mine = pl.ds(CAP * my_lon, CAP)
    own = pltpu.make_async_copy(send.at[mine], recv.at[mine], own_sem)
    own.start()

    @pl.when(has_south)
    def _():
        for copy in northward:
            copy.wait_recv()

    @pl.when(has_north)
    def _():
        for copy in southward:
            copy.wait_recv()

    to_east.wait_recv()
    to_west.wait_recv()

    def unpack(index):
        here = pl.ds(pl.multiple_of(index * ROWS8, ROWS8), ROWS8)
        from_east, from_west = east_got[here, :], west_got[here, :]
        for f in range(5):
            first = HALO * f
            right = jnp.logical_and(lane >= first, lane < first + HALO)
            first = (LANES - HALO + HALO * f) % LANES
            left = jnp.logical_and(lane >= first, lane < first + HALO)
            both = jnp.where(right, from_east, jnp.where(left, from_west, 0.0))
            fields[f, tiles, here, :] = pltpu.roll(both, LANES - HALO * f, 1) if f else both

    over(ext // ROWS8, unpack, 19)

    @pl.when(has_north)
    def _():
        for copy in northward:
            copy.wait_send()

    @pl.when(has_south)
    def _():
        for copy in southward:
            copy.wait_send()

    to_east.wait_send()
    to_west.wait_send()

    refs = (height, east_vel, north_vel, depth_east, depth_north)
    maps = columns_at(tiles + 1)

    def keep(f, c, k, value):
        refs[f][c, k] = value

    to_runs(maps, [fields.at[f] for f in range(5)], temp, number, keep)
    inner = pl.ds(0, number)
    stores = [pltpu.make_async_copy(ref.at[:, inner], fields_out.at[f], store_sem.at[f]) for f, ref in enumerate(refs)]
    for store in stores[3:]:
        store.start()
    steps(HALF, height, other, *refs[1:])
    for store in stores[:3]:
        store.start()

    own.wait()
    others = pl.ds(0, CAP * (lon - 1))
    every = pltpu.make_async_remote_copy(src_ref=send.at[others], dst_ref=recv.at[others], send_sem=a2a_sem.at[0],
                                         recv_sem=a2a_sem.at[1], device_id=(my_lat, east), device_id_type=MESH)
    every.wait_recv()
    stores.append(pltpu.make_async_copy(recv, recv_out, store_sem.at[5]))
    stores[5].start()
    cell = recv[:, PIECES - 1, :]
    ones = jnp.ones((ROWS8, slots), BF16)
    area = float(bin_rows * bin_cols)
    for b in range(BINS):
        within = jnp.logical_and(cell > b * area, cell <= (b + 1) * area)
        live_of = lax.dot_general(ones, jnp.where(within, 1.0, 0.0).astype(BF16), (((1,), (1,)), ((), ())), preferred_element_type=F32)
        count_out[pl.ds(b, 1), :] = live_of[:1].astype(I32)
    count_out[pl.ds(BINS, ROWS8 - BINS), :] = jnp.zeros((ROWS8 - BINS, CAP * lon), I32)
    every.wait_send()
    for store in stores:
        store.wait()


def spread_kernel(dims, counts_in, recv_in, out, counts, recv, packed, total, left_a, left_b, right_a, right_b, load_sem):
    rows, cols, lat, lon, blocks = dims
    tiles = cols // LANES
    segments = CAP * lon
    bin_rows, bin_cols = rows // ROW_BINS, cols // COL_BINS
    bins = ROW_BINS * COL_BINS
    padded = left_a.shape[0] // 2
    depth = GROUP * LANES
    room = segments + GROUP
    loads = [pltpu.make_async_copy(counts_in, counts, load_sem.at[0]), pltpu.make_async_copy(recv_in, recv, load_sem.at[1])]
    for load in loads:
        load.start()
    total[...] = jnp.zeros_like(total)
    for load in loads:
        load.wait()
    lane = lane_ids((PIECES, LANES))
    zero = jnp.zeros((PIECES, LANES), F32)

    def append(segment, carry):
        block = recv[segment]
        begin = 0
        after = []
        for b, (fill, current) in enumerate(carry):
            number = counts[b, segment]
            chunk = lax.shift_right_logical(fill, 7)
            turned = pltpu.roll(block, (fill - begin) & (LANES - 1), 1)
            current = jnp.where(lane >= (fill & (LANES - 1)), turned, current)
            packed[chunk + b * room] = current
            begin = begin + number
            fill = fill + number
            after.append((fill, jnp.where(lax.shift_right_logical(fill, 7) > chunk, turned, current)))
        return tuple(after)

    filled = lax.fori_loop(0, segments, append, ((jnp.int32(0), zero),) * bins, unroll=min(UNROLL, segments))
    jobs, starts = [], [0]
    for b, (fill, current) in enumerate(filled):
        chunk = lax.shift_right_logical(fill, 7) + b * room
        packed[chunk] = jnp.where(lane < (fill & (LANES - 1)), current, 0.0)
        for extra in range(1, GROUP):
            packed[chunk + extra] = zero
        starts.append(starts[-1] + (fill + depth - 1) // depth)
    for extra in range(GROUP):
        packed[bins * room + extra] = zero
    count = starts[-1]

    def place(job):
        which = 0
        begin = 0
        for b in range(1, bins):
            past = job >= starts[b]
            which = jnp.where(past, b, which)
            begin = jnp.where(past, starts[b], begin)
        chunk = which * room + (job - begin) * GROUP
        return jnp.where(job < count, chunk, bins * room), jnp.where(job < count, which, 0)

    row_ids = lax.broadcasted_iota(IDS, (padded, depth), 0)
    col_ids = lax.broadcasted_iota(IDS, (bin_cols, depth), 0)
    one, none = jnp.array(1, BF16), jnp.array(0, BF16)

    def build(job, left, right):
        chunk, which = place(job)
        both = jnp.concatenate([packed[chunk + j] for j in range(GROUP)], axis=1)
        cell = both[4:5, :].astype(I32) - 1 - which * (bin_rows * bin_cols)
        row_at = cell // bin_cols if bin_cols & (bin_cols - 1) else lax.shift_right_arithmetic(cell, bin_cols.bit_length() - 1)
        col_at = cell - row_at * bin_cols

        def wide(value, kind, number):
            return jnp.broadcast_to(value, (number, depth)).astype(kind)

        here = row_ids == wide(row_at, IDS, padded)
        past = row_ids == wide(row_at + 1, IDS, padded)
        column = jnp.where(col_ids == wide(col_at, IDS, bin_cols), one, none)
        right[:, :depth] = column
        right[:, depth:] = column
        high = both[:4, :].astype(BF16).astype(F32)
        for part, values in enumerate((high, both[:4, :] - high)):
            for side in range(2):
                at = wide(values[side:side + 1, :], BF16, padded)
                above = wide(values[side + 2:side + 3, :], BF16, padded)
                left[pl.ds(side * padded, padded), pl.ds(part * depth, depth)] = jnp.where(here, at, jnp.where(past, above, none))

    def add(job, left, right):
        _, which = place(job)
        total[which] += lax.dot_general(left[...], right[...], (((1,), (1,)), ((), ())), preferred_element_type=F32)

    build(0, left_a, right_a)

    def pair(index, carry):
        build(2 * index + 1, left_b, right_b)
        add(2 * index, left_a, right_a)
        build(2 * index + 2, left_a, right_a)
        add(2 * index + 1, left_b, right_b)
        return carry

    lax.fori_loop(0, (count + 1) // 2, pair, 0)

    bin_tiles = bin_cols // LANES
    lane = lane_ids((bin_rows, LANES))
    for i in range(ROW_BINS):
        if i:
            for j in range(COL_BINS):
                for at in (0, padded):
                    total[i * COL_BINS + j, pl.ds(at, ROWS8), :] += total[(i - 1) * COL_BINS + j, pl.ds(at + bin_rows, ROWS8), :]
        before = jnp.zeros((bin_rows, LANES), F32)
        for t in range(tiles):
            which, span = i * COL_BINS + t // bin_tiles, pl.ds(t % bin_tiles * LANES, LANES)
            turned = pltpu.roll(total[which, pl.ds(padded, bin_rows), span], 1, 1)
            out[t, pl.ds(i * bin_rows, bin_rows), :] = total[which, pl.ds(0, bin_rows), span] + jnp.where(lane == 0, before, turned)
            before = turned


def finish_kernel(dims, fields_in, forcing_in, out, forcing, height, other, east_vel, north_vel, depth_east, depth_north, temp, done,
                  east_pack, west_pack, east_got, west_got, load_sem, row_sem, pack_sem, corner_sem, store_sem):
    rows, cols, lat, lon, blocks = dims
    tiles = cols // LANES
    ext = rows + 2 * HALO
    number = ext // ROWS8
    my_lat, my_lon = lax.axis_index("lat"), lax.axis_index("lon")
    east, west = lax.rem(my_lon + 1, lon), lax.rem(my_lon + lon - 1, lon)
    has_north, has_south = my_lat < lat - 1, my_lat > 0
    refs = (height, east_vel, north_vel, depth_east, depth_north)
    inner = pl.ds(0, number)
    loads = [pltpu.make_async_copy(forcing_in, forcing.at[pl.ds(0, tiles), pl.ds(HALO, rows), :], load_sem.at[5])]
    loads += [pltpu.make_async_copy(fields_in.at[f], ref.at[:, inner], load_sem.at[f]) for f, ref in enumerate(refs)]
    for load in loads:
        load.start()
    barrier = pltpu.get_barrier_semaphore()
    for has, where in ((has_north, my_lat + 1), (has_south, my_lat - 1)):
        @pl.when(has)
        def _():
            for column in (west, my_lon, east):
                pl.semaphore_signal(barrier, inc=1, device_id=(where, column), device_id_type=MESH)
    for column in (west, east):
        pl.semaphore_signal(barrier, inc=1, device_id=(my_lat, column), device_id_type=MESH)

    beyond = HALO - FRINGE
    for at in (0, ext - beyond):
        forcing[:, pl.ds(at, beyond), :] = jnp.zeros((tiles + 1, beyond, LANES), F32)
    for has, at in ((has_south, beyond), (has_north, HALO + rows)):
        @pl.when(jnp.logical_not(has))
        def _():
            forcing[:, pl.ds(at, FRINGE), :] = jnp.zeros((tiles + 1, FRINGE, LANES), F32)

    loads[0].wait()
    run = rows // 8
    lane = lane_ids((run, LANES))
    to_west = jnp.zeros((run, LANES), F32)
    to_east = to_west
    for g in range(8):
        here = pl.ds(HALO + run * g, run)
        inside = lane // FRINGE == g
        value = forcing[0, here, :]
        to_west = jnp.where(inside, pltpu.roll(value, FRINGE * g, 1) if g else value, to_west)
        value = forcing[tiles - 1, here, :]
        to_east = jnp.where(inside, pltpu.roll(value, (FRINGE * (g + 1)) % LANES, 1) if g < 7 else value, to_east)
    west_pack[pl.ds(0, run), :] = to_west
    east_pack[pl.ds(0, run), :] = to_east
    ends = (pl.ds(HALO, FRINGE), pl.ds(HALO + rows - FRINGE, FRINGE))
    outer = (pl.ds(HALO - FRINGE, FRINGE), pl.ds(HALO + rows, FRINGE))
    for at, here in zip((run, run + FRINGE), ends):
        west_pack[pl.ds(at, FRINGE), :] = forcing[0, here, :]
        east_pack[pl.ds(at, FRINGE), :] = forcing[tiles - 1, here, :]

    pl.semaphore_wait(barrier, 2 + 3 * has_north.astype(I32) + 3 * has_south.astype(I32))

    def remote(source, target, sems, where):
        return pltpu.make_async_remote_copy(src_ref=source, dst_ref=target, send_sem=sems.at[0], recv_sem=sems.at[1],
                                            device_id=where, device_id_type=MESH)

    main = pl.ds(0, tiles)
    strip, low_end, high_end = pl.ds(0, run), pl.ds(run, FRINGE), pl.ds(run + FRINGE, FRINGE)
    to_north = remote(forcing.at[main, ends[1], :], forcing.at[main, outer[0], :], row_sem.at[0], (my_lat + 1, my_lon))
    to_south = remote(forcing.at[main, ends[0], :], forcing.at[main, outer[1], :], row_sem.at[1], (my_lat - 1, my_lon))
    go_east = remote(east_pack.at[strip], west_got.at[strip], pack_sem.at[0], (my_lat, east))
    go_west = remote(west_pack.at[strip], east_got.at[strip], pack_sem.at[1], (my_lat, west))
    north_east = remote(east_pack.at[high_end], west_got.at[low_end], corner_sem.at[0], (my_lat + 1, east))
    north_west = remote(west_pack.at[high_end], east_got.at[low_end], corner_sem.at[1], (my_lat + 1, west))
    south_east = remote(east_pack.at[low_end], west_got.at[high_end], corner_sem.at[2], (my_lat - 1, east))
    south_west = remote(west_pack.at[low_end], east_got.at[high_end], corner_sem.at[3], (my_lat - 1, west))
    northward, southward = (to_north, north_east, north_west), (to_south, south_east, south_west)

    @pl.when(has_north)
    def _():
        for copy in northward:
            copy.start()

    @pl.when(has_south)
    def _():
        for copy in southward:
            copy.start()

    go_east.start()
    go_west.start()

    for load in loads[1:]:
        load.wait()

    @pl.when(has_south)
    def _():
        for copy in northward:
            copy.wait_recv()

    @pl.when(has_north)
    def _():
        for copy in southward:
            copy.wait_recv()

    go_east.wait_recv()
    go_west.wait_recv()
    right = lane < FRINGE
    left = lane >= LANES - FRINGE
    from_east, from_west = east_got[strip, :], west_got[strip, :]
    for g in range(8):
        here = pl.ds(HALO + run * g, run)
        one = pltpu.roll(from_east, (LANES - FRINGE * g) % LANES, 1) if g else from_east
        two = pltpu.roll(from_west, (LANES - FRINGE * (g + 1)) % LANES, 1) if g < 7 else from_west
        forcing[tiles, here, :] = jnp.where(right, one, jnp.where(left, two, 0.0))
    lane = lane_ids((FRINGE, LANES))
    right = lane < FRINGE
    left = lane >= LANES - FRINGE
    for has, end, at in ((has_south, low_end, HALO - FRINGE), (has_north, high_end, HALO + rows)):
        @pl.when(has)
        def _():
            forcing[tiles, pl.ds(at, FRINGE), :] = jnp.where(right, east_got[end, :], jnp.where(left, west_got[end, :], 0.0))

    maps = columns_at(tiles + 1)

    def keep(f, c, k, value):
        height[c, k] += value

    to_runs(maps, [forcing], temp, number, keep)
    steps(HALF, height, other, *refs[1:])
    stores = []

    def finished(t):
        store = pltpu.make_async_copy(done.at[:, t, pl.ds(HALO, rows), :], out.at[:, :, pl.ds(t * LANES, LANES)], store_sem.at[t])
        store.start()
        stores.append(store)

    from_runs(maps, refs[:3], temp, number, done, finished)

    @pl.when(has_north)
    def _():
        for copy in northward:
            copy.wait_send()

    @pl.when(has_south)
    def _():
        for copy in southward:
            copy.wait_send()

    go_east.wait_send()
    go_west.wait_send()
    for store in stores:
        store.wait()


def per_device(lat, lon, adjoint_state, face_depth, innovation, interp_weight, block_tile, block_count, obs_row, obs_col):
    rows, cols = adjoint_state.shape[1:]
    blocks, slots = innovation.shape
    tiles = cols // LANES
    dims = (rows, cols, lat, lon, blocks)
    ext = rows + 2 * HALO
    segments = CAP * lon
    vmem = pl.BlockSpec(memory_space=pltpu.VMEM)
    anywhere = pl.BlockSpec(memory_space=pl.ANY)
    dma = pltpu.SemaphoreType.DMA
    number = ext // ROWS8
    natural = pltpu.VMEM((5, tiles + 1, ext, LANES), F32)
    runs = [pltpu.VMEM((tiles + 1, number + 1, ROWS8, LANES), F32)] * 2 + [pltpu.VMEM((tiles + 1, number, ROWS8, LANES), F32)] * 4
    params = functools.partial(pltpu.CompilerParams, has_side_effects=True)
    fields, recv, counts = pl.pallas_call(
        functools.partial(route_kernel, dims),
        name="route",
        out_shape=(
            jax.ShapeDtypeStruct((5, tiles + 1, number, ROWS8, LANES), F32),
            jax.ShapeDtypeStruct((segments, PIECES, slots), F32),
            jax.ShapeDtypeStruct((ROWS8, segments), I32),
        ),
        in_specs=[anywhere] * 8,
        out_specs=(anywhere, anywhere, vmem),
        scratch_shapes=[
            natural, *runs,
            pltpu.VMEM((blocks, slots), F32),
            pltpu.VMEM((blocks, 4, slots), F32),
            pltpu.VMEM((1, blocks), I32),
            pltpu.VMEM((1, blocks), I32),
            pltpu.VMEM((blocks, slots), I32),
            pltpu.VMEM((blocks, slots), I32),
            pltpu.VMEM((blocks, slots), F32),
            pltpu.VMEM((blocks, slots), F32),
            pltpu.VMEM((ROWS8 * blocks, slots), F32),
            pltpu.VMEM((5, tiles + 1, number, ROWS8, LANES), F32),
            pltpu.VMEM((segments, PIECES, slots), F32),
            pltpu.VMEM((segments, PIECES, slots), F32),
            pltpu.VMEM((rows, LANES), F32),
            pltpu.VMEM((rows, LANES), F32),
            pltpu.VMEM((ext, LANES), F32),
            pltpu.VMEM((ext, LANES), F32),
            dma((2 * tiles,)), dma((6,)), dma((2, 2)), dma((2, 2)), dma((4, 2)), dma((2,)), dma, dma((6,)),
        ],
        compiler_params=params(collective_id=0, vmem_limit_bytes=56 << 20),
    )(adjoint_state, face_depth, innovation, interp_weight, block_tile.reshape(1, blocks), block_count.reshape(1, blocks),
      obs_row, obs_col)
    padded = rows if ROW_BINS == 1 else rows // ROW_BINS + 16
    forcing = pl.pallas_call(
        functools.partial(spread_kernel, dims),
        name="spread",
        out_shape=jax.ShapeDtypeStruct((tiles, rows, LANES), F32),
        in_specs=[anywhere] * 2,
        out_specs=vmem,
        scratch_shapes=[
            pltpu.SMEM((ROWS8, segments), I32),
            pltpu.VMEM((segments, PIECES, slots), F32),
            pltpu.VMEM((BINS * (segments + GROUP) + GROUP, PIECES, LANES), F32),
            pltpu.VMEM((BINS, 2 * padded, cols // COL_BINS), F32),
            *[pltpu.VMEM((2 * padded, 2 * GROUP * LANES), BF16)] * 2,
            *[pltpu.VMEM((cols // COL_BINS, 2 * GROUP * LANES), BF16)] * 2,
            dma((2,)),
        ],
        compiler_params=pltpu.CompilerParams(vmem_limit_bytes=56 << 20),
    )(counts, recv)
    run = rows // 8 + 2 * FRINGE
    return pl.pallas_call(
        functools.partial(finish_kernel, dims),
        name="finish",
        out_shape=jax.ShapeDtypeStruct((3, rows, cols), F32),
        in_specs=[anywhere] * 2,
        out_specs=anywhere,
        scratch_shapes=[
            pltpu.VMEM((tiles + 1, ext, LANES), F32),
            *runs,
            pltpu.VMEM((6, tiles + 1, number, ROWS8, LANES), F32),
            pltpu.VMEM((3, tiles, ext, LANES), F32),
            pltpu.VMEM((run, LANES), F32),
            pltpu.VMEM((run, LANES), F32),
            pltpu.VMEM((run, LANES), F32),
            pltpu.VMEM((run, LANES), F32),
            dma((6,)), dma((2, 2)), dma((2, 2)), dma((4, 2)), dma((tiles,)),
        ],
        compiler_params=params(collective_id=1, vmem_limit_bytes=50 << 20),
    )(fields, forcing)


def solution(mesh):
    return jax.shard_map(
        functools.partial(per_device, mesh.shape["lat"], mesh.shape["lon"]),
        mesh=mesh,
        in_specs=(
            P(None, "lat", "lon"),
            P(None, "lat", "lon"),
            P(("lat", "lon"), None),
            P(("lat", "lon"), None, None),
            P(("lat", "lon"), None),
            P(("lat", "lon"), None),
            P(("lat", "lon"), None),
            P(("lat", "lon"), None),
        ),
        out_specs=P(None, "lat", "lon"),
        check_vma=False,
    )
```

```python
import functools

import jax
import jax.numpy as jnp
from jax import lax
from jax.experimental import pallas as pl
from jax.experimental.pallas import tpu as pltpu
from jax.sharding import PartitionSpec as P

WIN = 6
WINDOWS = 4
CAP = 2
LANES = 128
ROWS8 = 8
HALO = WIN * WINDOWS
HALF = HALO // 2
FRINGE = 16
PIECES = 5
GROUP = 8
ROW_BINS = 1
COL_BINS = 2
BINS = ROW_BINS * COL_BINS
UNROLL = 32
IDS = jnp.int16
MESH = pl.DeviceIdType.MESH
F32 = jnp.float32
BF16 = jnp.bfloat16
I32 = jnp.int32


def lane_ids(shape):
    return lax.broadcasted_iota(I32, shape, len(shape) - 1)


def shift_to(me, index, lon):
    where = me + index
    return jnp.where(where >= lon, where - lon, where)


def columns_at(width):
    part = LANES // width
    lane = lane_ids((ROWS8, LANES))
    part_of, inside = lane // part, lane % part
    cuts = [(width * part * t - HALO) % LANES for t in range(width)]
    into = [(width * part * t - HALO + LANES + width * inside + (part_of + width - t) % width) % LANES for t in range(width)]
    turn = [part * ((part_of + c) % width) + inside for c in range(width)]
    back = [part * ((part_of + width - c) % width) + inside for c in range(width)]
    out = []
    for t in range(width):
        along = (lane + LANES - cuts[t]) % LANES
        out.append(jnp.minimum(part * ((along + t) % width) + along // width, LANES - 1))
    return lane, part_of, cuts, into, turn, back, out


def take(values, index):
    return jnp.take_along_axis(values, index, axis=1)


def by_part(part_of, choices):
    value = choices[-1]
    for p in range(len(choices) - 1):
        value = jnp.where(part_of == p, choices[p], value)
    return value


def piece(number, most):
    return max(d for d in range(1, number + 1) if number % d == 0 and d <= max(most, 1))


def over(number, body, most, also=None):
    size = piece(number, most)

    def one(p, carry):
        for j in range(size):
            body(p * size + j)
        if also is not None:
            also(p)
        return carry

    lax.fori_loop(0, number // size, one, 0)


def to_runs(maps, natural, temp, number, keep, also=None):
    lane, part_of, cuts, into, turn, back, out = maps
    width = len(cuts)
    most = 100 // len(natural)
    pieces = number // piece(number, most)

    def beside(turn_number):
        return None if also is None else lambda p: also(turn_number * pieces + p)

    for t in range(width):
        def sort(k):
            rows = pl.ds(k, ROWS8, stride=number)
            for f, ref in enumerate(natural):
                temp[f, t, k] = take(jnp.where(lane >= cuts[t], ref[(t - 1) % width, rows, :], ref[t, rows, :]), into[t])

        over(number, sort, most, beside(t))
    for c in range(width):
        def mix(k):
            for f in range(len(natural)):
                value = by_part(part_of, [temp[f, (p - c) % width, k] for p in range(width)])
                keep(f, c, k, take(value, turn[c]) if c else value)

        over(number, mix, most, beside(width + c))


def from_runs(maps, refs, temp, number, natural, finished):
    lane, part_of, cuts, into, turn, back, out = maps
    width, fields = len(cuts), len(refs)
    most = 120 // fields
    for c in range(1, width):
        def unmix(k):
            for f in range(fields):
                temp[f, c, k] = take(refs[f][c, k], back[c])

        over(number, unmix, most)
    for t in range(width):
        def unsort(k):
            for f in range(fields):
                parts = [(p - t) % width for p in range(width)]
                value = by_part(part_of, [temp[f, c, k] if c else refs[f][0, k] for c in parts])
                temp[fields + f, t, k] = take(value, out[t])

        over(number, unsort, most)
        if t:
            def join(k):
                for f in range(fields):
                    value = jnp.where(lane < cuts[t], temp[fields + f, t - 1, k], temp[fields + f, t, k])
                    natural[f, t - 1, pl.ds(k, ROWS8, stride=number), :] = value

            over(number, join, most)
            finished(t - 1)


def one_step(old, new, east_vel, north_vel, depth_east, depth_north):
    width, number = east_vel.shape[:2]
    cols = range(width)
    for c in cols:
        old[c, number] = pltpu.roll(old[c, 0], ROWS8 - 1, 0)
    end = number - 1
    south = [pltpu.roll(north_vel[c, end] + depth_north[c, end] * (old[c, number] - old[c, end]), 1, 0) for c in cols]
    for k in range(number):
        height = [old[c, k] for c in cols]
        height_e = height[1:] + [pltpu.roll(height[0], LANES - 1, 1)]
        east = [None] * width
        for c in [width - 1] + list(range(width - 1)):
            east[c] = east_vel[c, k] + depth_east[c, k] * (height_e[c] - height[c])
        west = [pltpu.roll(east[-1], 1, 1)] + east[:-1]
        north = [None] * width
        for c in cols:
            north[c] = north_vel[c, k] + depth_north[c, k] * (old[c, k + 1] - height[c])
            new[c, k] = height[c] + (east[c] - west[c]) + (north[c] - south[c])
            east_vel[c, k] = east[c]
            north_vel[c, k] = north[c]
        south = north


def steps(number, height, other, *rest):
    def two(_, carry):
        one_step(height, other, *rest)
        one_step(other, height, *rest)
        return carry

    lax.fori_loop(0, number // 2, two, 0)


def route_kernel(dims, state, depth, innov_in, weight_in, tile_in, count_in, row_in, col_in, fields_out, recv_out, count_out,
                 fields, height, other, east_vel, north_vel, depth_east, depth_north,
                 innov, weight, tile_row, count_row, obs_row, obs_col, spots, cells, ordered, temp, send, recv, east_pack, west_pack, east_got, west_got,
                 load_sem, small_sem, row_sem, pack_sem, corner_sem, a2a_sem, own_sem, store_sem):
    rows, cols, lat, lon, blocks = dims
    tiles = cols // LANES
    ext = rows + 2 * HALO
    number = ext // ROWS8
    my_lat, my_lon = lax.axis_index("lat"), lax.axis_index("lon")
    east, west = lax.rem(my_lon + 1, lon), lax.rem(my_lon + lon - 1, lon)
    has_north, has_south = my_lat < lat - 1, my_lat > 0

    small = [pltpu.make_async_copy(source, target, small_sem.at[i]) for i, (source, target) in enumerate((
        (tile_in, tile_row), (count_in, count_row), (innov_in, innov), (weight_in, weight), (row_in, obs_row), (col_in, obs_col)))]
    for load in small:
        load.start()
    loads = []
    for t in range(tiles):
        span = pl.ds(t * LANES, LANES)
        for source, start, some in ((state, 0, 3), (depth, 3, 2)):
            loads.append(pltpu.make_async_copy(
                source.at[:, :, span], fields.at[pl.ds(start, some), t, pl.ds(HALO, rows), :], load_sem.at[len(loads)]))
    for load in loads:
        load.start()

    barrier = pltpu.get_barrier_semaphore()

    def greet(index, carry):
        pl.semaphore_signal(barrier, inc=1, device_id=(my_lat, shift_to(my_lon, index, lon)), device_id_type=MESH)
        return carry

    for has, where in ((has_north, my_lat + 1), (has_south, my_lat - 1)):
        @pl.when(has)
        def _():
            for column in (west, my_lon, east):
                pl.semaphore_signal(barrier, inc=1, device_id=(where, column), device_id_type=MESH)
    greetings = (lon - 1) // blocks
    lax.fori_loop(1 + greetings * blocks, lon, greet, 0)

    for load in small:
        load.wait()
    slots = innov.shape[1]
    square = (blocks, blocks)
    diagonal = lax.broadcasted_iota(I32, square, 0) == lane_ids(square)
    tile = jnp.sum(jnp.where(diagonal, tile_row[...].astype(F32), 0.0), axis=1, keepdims=True)
    count = jnp.sum(jnp.where(diagonal, count_row[...].astype(F32), 0.0), axis=1, keepdims=True)
    live = lane_ids((blocks, slots)).astype(F32) < count
    bin_rows, bin_cols = rows // ROW_BINS, cols // COL_BINS
    row_at, col_at = obs_row[...], obs_col[...]
    bin_at = row_at // bin_rows * COL_BINS + col_at // bin_cols
    cell = (bin_at * bin_rows + row_at % bin_rows) * bin_cols + col_at % bin_cols + 1
    member = [jnp.where(jnp.logical_and(live, bin_at == b), 1.0, 0.0) for b in range(BINS)]
    to_left = jnp.where(lax.broadcasted_iota(I32, (slots, slots), 0) < lane_ids((slots, slots)), 1.0, 0.0).astype(BF16)
    ahead = jnp.dot(jnp.concatenate(member, axis=0).astype(BF16), to_left, preferred_element_type=F32)
    begin = jnp.ones((blocks, 1), F32)
    spot = jnp.zeros((blocks, slots), F32)
    for b in range(BINS):
        spot += member[b] * (ahead[b * blocks:(b + 1) * blocks] + begin)
        begin += jnp.sum(member[b], axis=1, keepdims=True)
    spots[...] = spot
    innov[...] = jnp.where(live, innov[...], 0.0)
    cells[...] = jnp.where(live, cell, 0).astype(F32)
    ranks = (lax.broadcasted_iota(I32, (slots, slots), 0) + 1).astype(F32)
    sub = lax.broadcasted_iota(I32, (ROWS8 - 4, slots), 0)

    def order(b, carry):
        for j in range(greetings):
            greet(1 + b * greetings + j, 0)
        move = jnp.where(ranks == spots[pl.ds(b, 1), :], 1.0, 0.0).astype(BF16)
        values = weight[b] * innov[pl.ds(b, 1), :]
        data = jnp.concatenate([values, jnp.where(sub == 0, cells[pl.ds(b, 1), :], 0.0)], axis=0)
        high = data.astype(BF16).astype(F32)
        mid = (data - high).astype(BF16).astype(F32)
        parts = jnp.concatenate([high, mid, data - high - mid], axis=0).astype(BF16)
        moved = lax.dot_general(parts, move, (((1,), (1,)), ((), ())), preferred_element_type=F32)
        ordered[pl.ds(pl.multiple_of(b * ROWS8, ROWS8), ROWS8), :] = moved[:ROWS8] + moved[ROWS8:2 * ROWS8] + moved[2 * ROWS8:]
        return carry

    lax.fori_loop(0, blocks, order, 0, unroll=max(d for d in range(1, 17) if blocks % d == 0))
    named = jnp.where(tile == lane_ids((blocks, lon)).astype(F32), 1.0, 0.0)
    earlier = jnp.where(lax.broadcasted_iota(I32, square, 0) > lane_ids(square), 1.0, 0.0)
    before = jnp.dot(earlier.astype(BF16), named.astype(BF16), preferred_element_type=F32)
    rank = jnp.sum(before * named, axis=1, keepdims=True)
    place = tile * CAP + rank
    wide = (blocks, ROWS8 * blocks)
    ids = lane_ids(wide)
    row_of = jnp.where(lax.broadcasted_iota(I32, wide, 0) == ids // ROWS8, place * ROWS8 + (ids % ROWS8).astype(F32), 0.0)
    row_of = jnp.sum(row_of, axis=0, keepdims=True)
    pick = lax.broadcasted_iota(I32, (CAP * lon * ROWS8, ROWS8 * blocks), 0).astype(F32) == row_of
    pick = jnp.where(pick, 1.0, 0.0).astype(BF16)
    data = ordered[...]
    high = data.astype(BF16)
    rest = data - high.astype(F32)
    mid = rest.astype(BF16)
    low = (rest - mid.astype(F32)).astype(BF16)
    sent = (jnp.dot(pick, high, preferred_element_type=F32) + jnp.dot(pick, mid, preferred_element_type=F32)
            + jnp.dot(pick, low, preferred_element_type=F32))
    send[...] = sent.reshape(CAP * lon, ROWS8, slots)[:, :PIECES, :]

    zero_rows = jnp.zeros((5, tiles, HALO, LANES), F32)

    @pl.when(jnp.logical_not(has_south))
    def _():
        fields[:, pl.ds(0, tiles), pl.ds(0, HALO), :] = zero_rows
        east_got[pl.ds(0, HALO), :] = zero_rows[0, 0]
        west_got[pl.ds(0, HALO), :] = zero_rows[0, 0]

    @pl.when(jnp.logical_not(has_north))
    def _():
        fields[:, pl.ds(0, tiles), pl.ds(HALO + rows, HALO), :] = zero_rows
        east_got[pl.ds(HALO + rows, HALO), :] = zero_rows[0, 0]
        west_got[pl.ds(HALO + rows, HALO), :] = zero_rows[0, 0]

    for load in loads:
        load.wait()

    @pl.when(jnp.logical_not(has_north))
    def _():
        wall = pl.ds(HALO + rows - ROWS8, ROWS8)
        keep = lax.broadcasted_iota(I32, (tiles, ROWS8, LANES), 1) < ROWS8 - 1
        fields[4, pl.ds(0, tiles), wall, :] = jnp.where(keep, fields[4, pl.ds(0, tiles), wall, :], 0.0)

    lane = lane_ids((ROWS8, LANES))

    def pack(index, carry):
        base = pl.multiple_of(index * ROWS8, ROWS8)
        here = pl.ds(HALO + base, ROWS8)
        to_west = jnp.zeros((ROWS8, LANES), F32)
        to_east = to_west
        for f in range(5):
            first = HALO * f
            inside = jnp.logical_and(lane >= first, lane < first + HALO)
            to_west = jnp.where(inside, pltpu.roll(fields[f, 0, here, :], first, 1) if f else fields[f, 0, here, :], to_west)
            first = (LANES - HALO + HALO * f) % LANES
            inside = jnp.logical_and(lane >= first, lane < first + HALO)
            value = fields[f, tiles - 1, here, :]
            to_east = jnp.where(inside, pltpu.roll(value, HALO * f, 1) if f else value, to_east)
        west_pack[pl.ds(base, ROWS8), :] = to_west
        east_pack[pl.ds(base, ROWS8), :] = to_east
        return carry

    lax.fori_loop(0, rows // ROWS8, pack, 0, unroll=8)

    pl.semaphore_wait(barrier, lon - 1 + 3 * has_north.astype(I32) + 3 * has_south.astype(I32))

    def remote(source, target, sems, where):
        return pltpu.make_async_remote_copy(src_ref=source, dst_ref=target, send_sem=sems.at[0], recv_sem=sems.at[1],
                                            device_id=where, device_id_type=MESH)

    main = pl.ds(HALO, rows)
    low_rows, high_rows = pl.ds(0, HALO), pl.ds(HALO + rows, HALO)
    inner = pl.ds(0, tiles)
    to_north = remote(fields.at[:, inner, pl.ds(rows, HALO), :], fields.at[:, inner, low_rows, :], row_sem.at[0], (my_lat + 1, my_lon))
    to_south = remote(fields.at[:, inner, pl.ds(HALO, HALO), :], fields.at[:, inner, high_rows, :], row_sem.at[1], (my_lat - 1, my_lon))
    to_east = remote(east_pack, west_got.at[main], pack_sem.at[0], (my_lat, east))
    to_west = remote(west_pack, east_got.at[main], pack_sem.at[1], (my_lat, west))
    tail = pl.ds(rows - HALO, HALO)
    north_east = remote(east_pack.at[tail], west_got.at[low_rows], corner_sem.at[0], (my_lat + 1, east))
    north_west = remote(west_pack.at[tail], east_got.at[low_rows], corner_sem.at[1], (my_lat + 1, west))
    south_east = remote(east_pack.at[low_rows], west_got.at[high_rows], corner_sem.at[2], (my_lat - 1, east))
    south_west = remote(west_pack.at[low_rows], east_got.at[high_rows], corner_sem.at[3], (my_lat - 1, west))
    northward, southward = (to_north, north_east, north_west), (to_south, south_east, south_west)

    @pl.when(has_north)
    def _():
        for copy in northward:
            copy.start()

    @pl.when(has_south)
    def _():
        for copy in southward:
            copy.start()

    to_east.start()
    to_west.start()

    def block_copy(index):
        where = shift_to(my_lon, index, lon)
        return remote(send.at[pl.ds(CAP * where, CAP)], recv.at[pl.ds(CAP * my_lon, CAP)], a2a_sem, (my_lat, where))

    def send_blocks(index, carry):
        block_copy(index).start()
        return carry

    pieces = 2 * (tiles + 1) * (number // piece(number, 20))
    beside = (lon - 1) // pieces
    lax.fori_loop(1, lon - beside * pieces, send_blocks, 0)
    mine = pl.ds(CAP * my_lon, CAP)
    own = pltpu.make_async_copy(send.at[mine], recv.at[mine], own_sem)
    own.start()

    @pl.when(has_south)
    def _():
        for copy in northward:
            copy.wait_recv()

    @pl.when(has_north)
    def _():
        for copy in southward:
            copy.wait_recv()

    to_east.wait_recv()
    to_west.wait_recv()

    def unpack(index):
        here = pl.ds(pl.multiple_of(index * ROWS8, ROWS8), ROWS8)
        from_east, from_west = east_got[here, :], west_got[here, :]
        for f in range(5):
            first = HALO * f
            right = jnp.logical_and(lane >= first, lane < first + HALO)
            first = (LANES - HALO + HALO * f) % LANES
            left = jnp.logical_and(lane >= first, lane < first + HALO)
            both = jnp.where(right, from_east, jnp.where(left, from_west, 0.0))
            fields[f, tiles, here, :] = pltpu.roll(both, LANES - HALO * f, 1) if f else both

    over(ext // ROWS8, unpack, 19)

    @pl.when(has_north)
    def _():
        for copy in northward:
            copy.wait_send()

    @pl.when(has_south)
    def _():
        for copy in southward:
            copy.wait_send()

    to_east.wait_send()
    to_west.wait_send()

    refs = (height, east_vel, north_vel, depth_east, depth_north)
    maps = columns_at(tiles + 1)

    def keep(f, c, k, value):
        refs[f][c, k] = value

    def send_some(p):
        for j in range(beside):
            block_copy(lon - beside * pieces + p * beside + j).start()

    to_runs(maps, [fields.at[f] for f in range(5)], temp, number, keep, send_some)
    inner = pl.ds(0, number)
    stores = [pltpu.make_async_copy(ref.at[:, inner], fields_out.at[f], store_sem.at[f]) for f, ref in enumerate(refs)]
    for store in stores[3:]:
        store.start()
    steps(HALF, height, other, *refs[1:])
    for store in stores[:3]:
        store.start()

    own.wait()
    others = pl.ds(0, CAP * (lon - 1))
    every = pltpu.make_async_remote_copy(src_ref=send.at[others], dst_ref=recv.at[others], send_sem=a2a_sem.at[0],
                                         recv_sem=a2a_sem.at[1], device_id=(my_lat, east), device_id_type=MESH)
    every.wait_recv()
    stores.append(pltpu.make_async_copy(recv, recv_out, store_sem.at[5]))
    stores[5].start()
    cell = recv[:, PIECES - 1, :]
    ones = jnp.ones((ROWS8, slots), BF16)
    area = float(bin_rows * bin_cols)
    for b in range(BINS):
        within = jnp.logical_and(cell > b * area, cell <= (b + 1) * area)
        live_of = lax.dot_general(ones, jnp.where(within, 1.0, 0.0).astype(BF16), (((1,), (1,)), ((), ())), preferred_element_type=F32)
        count_out[pl.ds(b, 1), :] = live_of[:1].astype(I32)
    count_out[pl.ds(BINS, ROWS8 - BINS), :] = jnp.zeros((ROWS8 - BINS, CAP * lon), I32)
    every.wait_send()
    for store in stores:
        store.wait()


def spread_kernel(dims, counts_in, recv_in, out, counts, recv, packed, total, left_a, left_b, right_a, right_b, load_sem):
    rows, cols, lat, lon, blocks = dims
    tiles = cols // LANES
    segments = CAP * lon
    bin_rows, bin_cols = rows // ROW_BINS, cols // COL_BINS
    bins = ROW_BINS * COL_BINS
    padded = left_a.shape[0] // 2
    depth = GROUP * LANES
    room = segments + GROUP
    loads = [pltpu.make_async_copy(counts_in, counts, load_sem.at[0]), pltpu.make_async_copy(recv_in, recv, load_sem.at[1])]
    for load in loads:
        load.start()
    total[...] = jnp.zeros_like(total)
    for load in loads:
        load.wait()
    lane = lane_ids((PIECES, LANES))
    zero = jnp.zeros((PIECES, LANES), F32)

    def append(segment, carry):
        block = recv[segment]
        begin = 0
        after = []
        for b, (fill, current) in enumerate(carry):
            number = counts[b, segment]
            chunk = lax.shift_right_logical(fill, 7)
            turned = pltpu.roll(block, (fill - begin) & (LANES - 1), 1)
            current = jnp.where(lane >= (fill & (LANES - 1)), turned, current)
            packed[chunk + b * room] = current
            begin = begin + number
            fill = fill + number
            after.append((fill, jnp.where(lax.shift_right_logical(fill, 7) > chunk, turned, current)))
        return tuple(after)

    filled = lax.fori_loop(0, segments, append, ((jnp.int32(0), zero),) * bins, unroll=min(UNROLL, segments))
    jobs, starts = [], [0]
    for b, (fill, current) in enumerate(filled):
        chunk = lax.shift_right_logical(fill, 7) + b * room
        packed[chunk] = jnp.where(lane < (fill & (LANES - 1)), current, 0.0)
        for extra in range(1, GROUP):
            packed[chunk + extra] = zero
        starts.append(starts[-1] + (fill + depth - 1) // depth)
    for extra in range(GROUP):
        packed[bins * room + extra] = zero
    count = starts[-1]

    def place(job):
        which = 0
        begin = 0
        for b in range(1, bins):
            past = job >= starts[b]
            which = jnp.where(past, b, which)
            begin = jnp.where(past, starts[b], begin)
        chunk = which * room + (job - begin) * GROUP
        return jnp.where(job < count, chunk, bins * room), jnp.where(job < count, which, 0)

    row_ids = lax.broadcasted_iota(IDS, (padded, depth), 0)
    col_ids = lax.broadcasted_iota(IDS, (bin_cols, depth), 0)
    one, none = jnp.array(1, BF16), jnp.array(0, BF16)

    def build(job, left, right):
        chunk, which = place(job)
        both = jnp.concatenate([packed[chunk + j] for j in range(GROUP)], axis=1)
        cell = both[4:5, :].astype(I32) - 1 - which * (bin_rows * bin_cols)
        row_at = cell // bin_cols if bin_cols & (bin_cols - 1) else lax.shift_right_arithmetic(cell, bin_cols.bit_length() - 1)
        col_at = cell - row_at * bin_cols

        def wide(value, kind, number):
            return jnp.broadcast_to(value, (number, depth)).astype(kind)

        here = row_ids == wide(row_at, IDS, padded)
        past = row_ids == wide(row_at + 1, IDS, padded)
        column = jnp.where(col_ids == wide(col_at, IDS, bin_cols), one, none)
        right[:, :depth] = column
        right[:, depth:] = column
        high = both[:4, :].astype(BF16).astype(F32)
        for part, values in enumerate((high, both[:4, :] - high)):
            for side in range(2):
                at = wide(values[side:side + 1, :], BF16, padded)
                above = wide(values[side + 2:side + 3, :], BF16, padded)
                left[pl.ds(side * padded, padded), pl.ds(part * depth, depth)] = jnp.where(here, at, jnp.where(past, above, none))

    def add(job, left, right):
        _, which = place(job)
        total[which] += lax.dot_general(left[...], right[...], (((1,), (1,)), ((), ())), preferred_element_type=F32)

    build(0, left_a, right_a)

    def pair(index, carry):
        build(2 * index + 1, left_b, right_b)
        add(2 * index, left_a, right_a)
        build(2 * index + 2, left_a, right_a)
        add(2 * index + 1, left_b, right_b)
        return carry

    lax.fori_loop(0, (count + 1) // 2, pair, 0)

    bin_tiles = bin_cols // LANES
    lane = lane_ids((bin_rows, LANES))
    for i in range(ROW_BINS):
        if i:
            for j in range(COL_BINS):
                for at in (0, padded):
                    total[i * COL_BINS + j, pl.ds(at, ROWS8), :] += total[(i - 1) * COL_BINS + j, pl.ds(at + bin_rows, ROWS8), :]
        before = jnp.zeros((bin_rows, LANES), F32)
        for t in range(tiles):
            which, span = i * COL_BINS + t // bin_tiles, pl.ds(t % bin_tiles * LANES, LANES)
            turned = pltpu.roll(total[which, pl.ds(padded, bin_rows), span], 1, 1)
            out[t, pl.ds(i * bin_rows, bin_rows), :] = total[which, pl.ds(0, bin_rows), span] + jnp.where(lane == 0, before, turned)
            before = turned


def finish_kernel(dims, fields_in, forcing_in, out, forcing, height, other, east_vel, north_vel, depth_east, depth_north, temp, done,
                  east_pack, west_pack, east_got, west_got, load_sem, row_sem, pack_sem, corner_sem, store_sem):
    rows, cols, lat, lon, blocks = dims
    tiles = cols // LANES
    ext = rows + 2 * HALO
    number = ext // ROWS8
    my_lat, my_lon = lax.axis_index("lat"), lax.axis_index("lon")
    east, west = lax.rem(my_lon + 1, lon), lax.rem(my_lon + lon - 1, lon)
    has_north, has_south = my_lat < lat - 1, my_lat > 0
    refs = (height, east_vel, north_vel, depth_east, depth_north)
    inner = pl.ds(0, number)
    loads = [pltpu.make_async_copy(forcing_in, forcing.at[pl.ds(0, tiles), pl.ds(HALO, rows), :], load_sem.at[5])]
    loads += [pltpu.make_async_copy(fields_in.at[f], ref.at[:, inner], load_sem.at[f]) for f, ref in enumerate(refs)]
    for load in loads:
        load.start()
    barrier = pltpu.get_barrier_semaphore()
    for has, where in ((has_north, my_lat + 1), (has_south, my_lat - 1)):
        @pl.when(has)
        def _():
            for column in (west, my_lon, east):
                pl.semaphore_signal(barrier, inc=1, device_id=(where, column), device_id_type=MESH)
    for column in (west, east):
        pl.semaphore_signal(barrier, inc=1, device_id=(my_lat, column), device_id_type=MESH)

    beyond = HALO - FRINGE
    for at in (0, ext - beyond):
        forcing[:, pl.ds(at, beyond), :] = jnp.zeros((tiles + 1, beyond, LANES), F32)
    for has, at in ((has_south, beyond), (has_north, HALO + rows)):
        @pl.when(jnp.logical_not(has))
        def _():
            forcing[:, pl.ds(at, FRINGE), :] = jnp.zeros((tiles + 1, FRINGE, LANES), F32)

    loads[0].wait()
    run = rows // 8
    lane = lane_ids((run, LANES))
    to_west = jnp.zeros((run, LANES), F32)
    to_east = to_west
    for g in range(8):
        here = pl.ds(HALO + run * g, run)
        inside = lane // FRINGE == g
        value = forcing[0, here, :]
        to_west = jnp.where(inside, pltpu.roll(value, FRINGE * g, 1) if g else value, to_west)
        value = forcing[tiles - 1, here, :]
        to_east = jnp.where(inside, pltpu.roll(value, (FRINGE * (g + 1)) % LANES, 1) if g < 7 else value, to_east)
    west_pack[pl.ds(0, run), :] = to_west
    east_pack[pl.ds(0, run), :] = to_east
    ends = (pl.ds(HALO, FRINGE), pl.ds(HALO + rows - FRINGE, FRINGE))
    outer = (pl.ds(HALO - FRINGE, FRINGE), pl.ds(HALO + rows, FRINGE))
    for at, here in zip((run, run + FRINGE), ends):
        west_pack[pl.ds(at, FRINGE), :] = forcing[0, here, :]
        east_pack[pl.ds(at, FRINGE), :] = forcing[tiles - 1, here, :]

    pl.semaphore_wait(barrier, 2 + 3 * has_north.astype(I32) + 3 * has_south.astype(I32))

    def remote(source, target, sems, where):
        return pltpu.make_async_remote_copy(src_ref=source, dst_ref=target, send_sem=sems.at[0], recv_sem=sems.at[1],
                                            device_id=where, device_id_type=MESH)

    main = pl.ds(0, tiles)
    strip, low_end, high_end = pl.ds(0, run), pl.ds(run, FRINGE), pl.ds(run + FRINGE, FRINGE)
    to_north = remote(forcing.at[main, ends[1], :], forcing.at[main, outer[0], :], row_sem.at[0], (my_lat + 1, my_lon))
    to_south = remote(forcing.at[main, ends[0], :], forcing.at[main, outer[1], :], row_sem.at[1], (my_lat - 1, my_lon))
    go_east = remote(east_pack.at[strip], west_got.at[strip], pack_sem.at[0], (my_lat, east))
    go_west = remote(west_pack.at[strip], east_got.at[strip], pack_sem.at[1], (my_lat, west))
    north_east = remote(east_pack.at[high_end], west_got.at[low_end], corner_sem.at[0], (my_lat + 1, east))
    north_west = remote(west_pack.at[high_end], east_got.at[low_end], corner_sem.at[1], (my_lat + 1, west))
    south_east = remote(east_pack.at[low_end], west_got.at[high_end], corner_sem.at[2], (my_lat - 1, east))
    south_west = remote(west_pack.at[low_end], east_got.at[high_end], corner_sem.at[3], (my_lat - 1, west))
    northward, southward = (to_north, north_east, north_west), (to_south, south_east, south_west)

    @pl.when(has_north)
    def _():
        for copy in northward:
            copy.start()

    @pl.when(has_south)
    def _():
        for copy in southward:
            copy.start()

    go_east.start()
    go_west.start()

    for load in loads[1:]:
        load.wait()

    @pl.when(has_south)
    def _():
        for copy in northward:
            copy.wait_recv()

    @pl.when(has_north)
    def _():
        for copy in southward:
            copy.wait_recv()

    go_east.wait_recv()
    go_west.wait_recv()
    right = lane < FRINGE
    left = lane >= LANES - FRINGE
    from_east, from_west = east_got[strip, :], west_got[strip, :]
    for g in range(8):
        here = pl.ds(HALO + run * g, run)
        one = pltpu.roll(from_east, (LANES - FRINGE * g) % LANES, 1) if g else from_east
        two = pltpu.roll(from_west, (LANES - FRINGE * (g + 1)) % LANES, 1) if g < 7 else from_west
        forcing[tiles, here, :] = jnp.where(right, one, jnp.where(left, two, 0.0))
    lane = lane_ids((FRINGE, LANES))
    right = lane < FRINGE
    left = lane >= LANES - FRINGE
    for has, end, at in ((has_south, low_end, HALO - FRINGE), (has_north, high_end, HALO + rows)):
        @pl.when(has)
        def _():
            forcing[tiles, pl.ds(at, FRINGE), :] = jnp.where(right, east_got[end, :], jnp.where(left, west_got[end, :], 0.0))

    maps = columns_at(tiles + 1)

    def keep(f, c, k, value):
        height[c, k] += value

    to_runs(maps, [forcing], temp, number, keep)
    steps(HALF, height, other, *refs[1:])
    stores = []

    def finished(t):
        store = pltpu.make_async_copy(done.at[:, t, pl.ds(HALO, rows), :], out.at[:, :, pl.ds(t * LANES, LANES)], store_sem.at[t])
        store.start()
        stores.append(store)

    from_runs(maps, refs[:3], temp, number, done, finished)

    @pl.when(has_north)
    def _():
        for copy in northward:
            copy.wait_send()

    @pl.when(has_south)
    def _():
        for copy in southward:
            copy.wait_send()

    go_east.wait_send()
    go_west.wait_send()
    for store in stores:
        store.wait()


def per_device(lat, lon, adjoint_state, face_depth, innovation, interp_weight, block_tile, block_count, obs_row, obs_col):
    rows, cols = adjoint_state.shape[1:]
    blocks, slots = innovation.shape
    tiles = cols // LANES
    dims = (rows, cols, lat, lon, blocks)
    ext = rows + 2 * HALO
    segments = CAP * lon
    vmem = pl.BlockSpec(memory_space=pltpu.VMEM)
    anywhere = pl.BlockSpec(memory_space=pl.ANY)
    dma = pltpu.SemaphoreType.DMA
    number = ext // ROWS8
    natural = pltpu.VMEM((5, tiles + 1, ext, LANES), F32)
    runs = [pltpu.VMEM((tiles + 1, number + 1, ROWS8, LANES), F32)] * 2 + [pltpu.VMEM((tiles + 1, number, ROWS8, LANES), F32)] * 4
    params = functools.partial(pltpu.CompilerParams, has_side_effects=True)
    fields, recv, counts = pl.pallas_call(
        functools.partial(route_kernel, dims),
        name="route",
        out_shape=(
            jax.ShapeDtypeStruct((5, tiles + 1, number, ROWS8, LANES), F32),
            jax.ShapeDtypeStruct((segments, PIECES, slots), F32),
            jax.ShapeDtypeStruct((ROWS8, segments), I32),
        ),
        in_specs=[anywhere] * 8,
        out_specs=(anywhere, anywhere, vmem),
        scratch_shapes=[
            natural, *runs,
            pltpu.VMEM((blocks, slots), F32),
            pltpu.VMEM((blocks, 4, slots), F32),
            pltpu.VMEM((1, blocks), I32),
            pltpu.VMEM((1, blocks), I32),
            pltpu.VMEM((blocks, slots), I32),
            pltpu.VMEM((blocks, slots), I32),
            pltpu.VMEM((blocks, slots), F32),
            pltpu.VMEM((blocks, slots), F32),
            pltpu.VMEM((ROWS8 * blocks, slots), F32),
            pltpu.VMEM((5, tiles + 1, number, ROWS8, LANES), F32),
            pltpu.VMEM((segments, PIECES, slots), F32),
            pltpu.VMEM((segments, PIECES, slots), F32),
            pltpu.VMEM((rows, LANES), F32),
            pltpu.VMEM((rows, LANES), F32),
            pltpu.VMEM((ext, LANES), F32),
            pltpu.VMEM((ext, LANES), F32),
            dma((2 * tiles,)), dma((6,)), dma((2, 2)), dma((2, 2)), dma((4, 2)), dma((2,)), dma, dma((6,)),
        ],
        compiler_params=params(collective_id=0, vmem_limit_bytes=56 << 20),
    )(adjoint_state, face_depth, innovation, interp_weight, block_tile.reshape(1, blocks), block_count.reshape(1, blocks),
      obs_row, obs_col)
    padded = rows if ROW_BINS == 1 else rows // ROW_BINS + 16
    forcing = pl.pallas_call(
        functools.partial(spread_kernel, dims),
        name="spread",
        out_shape=jax.ShapeDtypeStruct((tiles, rows, LANES), F32),
        in_specs=[anywhere] * 2,
        out_specs=vmem,
        scratch_shapes=[
            pltpu.SMEM((ROWS8, segments), I32),
            pltpu.VMEM((segments, PIECES, slots), F32),
            pltpu.VMEM((BINS * (segments + GROUP) + GROUP, PIECES, LANES), F32),
            pltpu.VMEM((BINS, 2 * padded, cols // COL_BINS), F32),
            *[pltpu.VMEM((2 * padded, 2 * GROUP * LANES), BF16)] * 2,
            *[pltpu.VMEM((cols // COL_BINS, 2 * GROUP * LANES), BF16)] * 2,
            dma((2,)),
        ],
        compiler_params=pltpu.CompilerParams(vmem_limit_bytes=24 << 20),
    )(counts, recv)
    run = rows // 8 + 2 * FRINGE
    return pl.pallas_call(
        functools.partial(finish_kernel, dims),
        name="finish",
        out_shape=jax.ShapeDtypeStruct((3, rows, cols), F32),
        in_specs=[anywhere] * 2,
        out_specs=anywhere,
        scratch_shapes=[
            pltpu.VMEM((tiles + 1, ext, LANES), F32),
            *runs,
            pltpu.VMEM((6, tiles + 1, number, ROWS8, LANES), F32),
            pltpu.VMEM((3, tiles, ext, LANES), F32),
            pltpu.VMEM((run, LANES), F32),
            pltpu.VMEM((run, LANES), F32),
            pltpu.VMEM((run, LANES), F32),
            pltpu.VMEM((run, LANES), F32),
            dma((6,)), dma((2, 2)), dma((2, 2)), dma((4, 2)), dma((tiles,)),
        ],
        compiler_params=params(collective_id=1, vmem_limit_bytes=50 << 20),
    )(fields, forcing)


def solution(mesh):
    return jax.shard_map(
        functools.partial(per_device, mesh.shape["lat"], mesh.shape["lon"]),
        mesh=mesh,
        in_specs=(
            P(None, "lat", "lon"),
            P(None, "lat", "lon"),
            P(("lat", "lon"), None),
            P(("lat", "lon"), None, None),
            P(("lat", "lon"), None),
            P(("lat", "lon"), None),
            P(("lat", "lon"), None),
            P(("lat", "lon"), None),
        ),
        out_specs=P(None, "lat", "lon"),
        check_vma=False,
    )
```

```python
import functools

import jax
import jax.numpy as jnp
from jax import lax
from jax.experimental import pallas as pl
from jax.experimental.pallas import tpu as pltpu
from jax.sharding import PartitionSpec as P

WIN = 6
WINDOWS = 4
CAP = 2
LANES = 128
ROWS8 = 8
HALO = WIN * WINDOWS
HALF = HALO // 2
FRINGE = 16
PIECES = 5
GROUP = 8
ROW_BINS = 1
COL_BINS = 2
BINS = ROW_BINS * COL_BINS
UNROLL = 32
IDS = jnp.int16
MESH = pl.DeviceIdType.MESH
F32 = jnp.float32
BF16 = jnp.bfloat16
I32 = jnp.int32


def lane_ids(shape):
    return lax.broadcasted_iota(I32, shape, len(shape) - 1)


def shift_to(me, index, lon):
    where = me + index
    return jnp.where(where >= lon, where - lon, where)


def columns_at(width):
    part = LANES // width
    lane = lane_ids((ROWS8, LANES))
    part_of, inside = lane // part, lane % part
    cuts = [(width * part * t - HALO) % LANES for t in range(width)]
    into = [(width * part * t - HALO + LANES + width * inside + (part_of + width - t) % width) % LANES for t in range(width)]
    turn = [part * ((part_of + c) % width) + inside for c in range(width)]
    back = [part * ((part_of + width - c) % width) + inside for c in range(width)]
    out = []
    for t in range(width):
        along = (lane + LANES - cuts[t]) % LANES
        out.append(jnp.minimum(part * ((along + t) % width) + along // width, LANES - 1))
    return lane, part_of, cuts, into, turn, back, out


def take(values, index):
    return jnp.take_along_axis(values, index, axis=1)


def by_part(part_of, choices):
    value = choices[-1]
    for p in range(len(choices) - 1):
        value = jnp.where(part_of == p, choices[p], value)
    return value


def over(number, body, most):
    size = max(d for d in range(1, number + 1) if number % d == 0 and d <= max(most, 1))

    def one(p, carry):
        for j in range(size):
            body(p * size + j)
        return carry

    lax.fori_loop(0, number // size, one, 0)


def to_runs(maps, natural, temp, number, keep):
    lane, part_of, cuts, into, turn, back, out = maps
    width = len(cuts)
    most = 100 // len(natural)
    for t in range(width):
        def sort(k):
            rows = pl.ds(k, ROWS8, stride=number)
            for f, ref in enumerate(natural):
                temp[f, t, k] = take(jnp.where(lane >= cuts[t], ref[(t - 1) % width, rows, :], ref[t, rows, :]), into[t])

        over(number, sort, most)
    for c in range(width):
        def mix(k):
            for f in range(len(natural)):
                value = by_part(part_of, [temp[f, (p - c) % width, k] for p in range(width)])
                keep(f, c, k, take(value, turn[c]) if c else value)

        over(number, mix, most)


def from_runs(maps, refs, temp, number, natural, finished):
    lane, part_of, cuts, into, turn, back, out = maps
    width, fields = len(cuts), len(refs)
    most = 120 // fields
    for c in range(1, width):
        def unmix(k):
            for f in range(fields):
                temp[f, c, k] = take(refs[f][c, k], back[c])

        over(number, unmix, most)
    for t in range(width):
        def unsort(k):
            for f in range(fields):
                parts = [(p - t) % width for p in range(width)]
                value = by_part(part_of, [temp[f, c, k] if c else refs[f][0, k] for c in parts])
                temp[fields + f, t, k] = take(value, out[t])

        over(number, unsort, most)
        if t:
            def join(k):
                for f in range(fields):
                    value = jnp.where(lane < cuts[t], temp[fields + f, t - 1, k], temp[fields + f, t, k])
                    natural[f, t - 1, pl.ds(k, ROWS8, stride=number), :] = value

            over(number, join, most)
            finished(t - 1)


def one_step(old, new, east_vel, north_vel, depth_east, depth_north):
    width, number = east_vel.shape[:2]
    cols = range(width)
    for c in cols:
        old[c, number] = pltpu.roll(old[c, 0], ROWS8 - 1, 0)
    end = number - 1
    south = [pltpu.roll(north_vel[c, end] + depth_north[c, end] * (old[c, number] - old[c, end]), 1, 0) for c in cols]
    for k in range(number):
        height = [old[c, k] for c in cols]
        height_e = height[1:] + [pltpu.roll(height[0], LANES - 1, 1)]
        east = [None] * width
        for c in [width - 1] + list(range(width - 1)):
            east[c] = east_vel[c, k] + depth_east[c, k] * (height_e[c] - height[c])
        west = [pltpu.roll(east[-1], 1, 1)] + east[:-1]
        north = [None] * width
        for c in cols:
            north[c] = north_vel[c, k] + depth_north[c, k] * (old[c, k + 1] - height[c])
            new[c, k] = height[c] + (east[c] - west[c]) + (north[c] - south[c])
            east_vel[c, k] = east[c]
            north_vel[c, k] = north[c]
        south = north


def steps(number, height, other, *rest):
    def two(_, carry):
        one_step(height, other, *rest)
        one_step(other, height, *rest)
        return carry

    lax.fori_loop(0, number // 2, two, 0)


def route_kernel(dims, state, depth, innov_in, weight_in, tile_in, count_in, row_in, col_in, fields_out, recv,
                 fields, height, other, east_vel, north_vel, depth_east, depth_north,
                 innov, weight, tile_row, count_row, obs_row, obs_col, spots, cells, ordered, temp, send, east_pack, west_pack, east_got, west_got,
                 load_sem, small_sem, row_sem, pack_sem, corner_sem, a2a_sem, own_sem, store_sem):
    rows, cols, lat, lon, blocks = dims
    tiles = cols // LANES
    ext = rows + 2 * HALO
    number = ext // ROWS8
    my_lat, my_lon = lax.axis_index("lat"), lax.axis_index("lon")
    east, west = lax.rem(my_lon + 1, lon), lax.rem(my_lon + lon - 1, lon)
    has_north, has_south = my_lat < lat - 1, my_lat > 0

    small = [pltpu.make_async_copy(source, target, small_sem.at[i]) for i, (source, target) in enumerate((
        (tile_in, tile_row), (count_in, count_row), (innov_in, innov), (weight_in, weight), (row_in, obs_row), (col_in, obs_col)))]
    for load in small:
        load.start()
    loads = []
    for t in range(tiles):
        span = pl.ds(t * LANES, LANES)
        for source, start, some in ((state, 0, 3), (depth, 3, 2)):
            loads.append(pltpu.make_async_copy(
                source.at[:, :, span], fields.at[pl.ds(start, some), t, pl.ds(HALO, rows), :], load_sem.at[len(loads)]))
    for load in loads:
        load.start()

    barrier = pltpu.get_barrier_semaphore()

    def greet(index, carry):
        pl.semaphore_signal(barrier, inc=1, device_id=(my_lat, shift_to(my_lon, index, lon)), device_id_type=MESH)
        return carry

    for has, where in ((has_north, my_lat + 1), (has_south, my_lat - 1)):
        @pl.when(has)
        def _():
            for column in (west, my_lon, east):
                pl.semaphore_signal(barrier, inc=1, device_id=(where, column), device_id_type=MESH)
    lax.fori_loop(1, lon, greet, 0)

    zero_rows = jnp.zeros((5, tiles, HALO, LANES), F32)

    @pl.when(jnp.logical_not(has_south))
    def _():
        fields[:, pl.ds(0, tiles), pl.ds(0, HALO), :] = zero_rows
        east_got[pl.ds(0, HALO), :] = zero_rows[0, 0]
        west_got[pl.ds(0, HALO), :] = zero_rows[0, 0]

    @pl.when(jnp.logical_not(has_north))
    def _():
        fields[:, pl.ds(0, tiles), pl.ds(HALO + rows, HALO), :] = zero_rows
        east_got[pl.ds(HALO + rows, HALO), :] = zero_rows[0, 0]
        west_got[pl.ds(HALO + rows, HALO), :] = zero_rows[0, 0]

    for load in loads:
        load.wait()

    @pl.when(jnp.logical_not(has_north))
    def _():
        wall = pl.ds(HALO + rows - ROWS8, ROWS8)
        keep = lax.broadcasted_iota(I32, (tiles, ROWS8, LANES), 1) < ROWS8 - 1
        fields[4, pl.ds(0, tiles), wall, :] = jnp.where(keep, fields[4, pl.ds(0, tiles), wall, :], 0.0)

    lane = lane_ids((ROWS8, LANES))

    def pack(index, carry):
        base = pl.multiple_of(index * ROWS8, ROWS8)
        here = pl.ds(HALO + base, ROWS8)
        to_west = jnp.zeros((ROWS8, LANES), F32)
        to_east = to_west
        for f in range(5):
            first = HALO * f
            inside = jnp.logical_and(lane >= first, lane < first + HALO)
            to_west = jnp.where(inside, pltpu.roll(fields[f, 0, here, :], first, 1) if f else fields[f, 0, here, :], to_west)
            first = (LANES - HALO + HALO * f) % LANES
            inside = jnp.logical_and(lane >= first, lane < first + HALO)
            value = fields[f, tiles - 1, here, :]
            to_east = jnp.where(inside, pltpu.roll(value, HALO * f, 1) if f else value, to_east)
        west_pack[pl.ds(base, ROWS8), :] = to_west
        east_pack[pl.ds(base, ROWS8), :] = to_east
        return carry

    lax.fori_loop(0, rows // ROWS8, pack, 0, unroll=8)

    pl.semaphore_wait(barrier, lon - 1 + 3 * has_north.astype(I32) + 3 * has_south.astype(I32))

    def remote(source, target, sems, where):
        return pltpu.make_async_remote_copy(src_ref=source, dst_ref=target, send_sem=sems.at[0], recv_sem=sems.at[1],
                                            device_id=where, device_id_type=MESH)

    main = pl.ds(HALO, rows)
    low_rows, high_rows = pl.ds(0, HALO), pl.ds(HALO + rows, HALO)
    inner = pl.ds(0, tiles)
    to_north = remote(fields.at[:, inner, pl.ds(rows, HALO), :], fields.at[:, inner, low_rows, :], row_sem.at[0], (my_lat + 1, my_lon))
    to_south = remote(fields.at[:, inner, pl.ds(HALO, HALO), :], fields.at[:, inner, high_rows, :], row_sem.at[1], (my_lat - 1, my_lon))
    to_east = remote(east_pack, west_got.at[main], pack_sem.at[0], (my_lat, east))
    to_west = remote(west_pack, east_got.at[main], pack_sem.at[1], (my_lat, west))
    tail = pl.ds(rows - HALO, HALO)
    north_east = remote(east_pack.at[tail], west_got.at[low_rows], corner_sem.at[0], (my_lat + 1, east))
    north_west = remote(west_pack.at[tail], east_got.at[low_rows], corner_sem.at[1], (my_lat + 1, west))
    south_east = remote(east_pack.at[low_rows], west_got.at[high_rows], corner_sem.at[2], (my_lat - 1, east))
    south_west = remote(west_pack.at[low_rows], east_got.at[high_rows], corner_sem.at[3], (my_lat - 1, west))
    northward, southward = (to_north, north_east, north_west), (to_south, south_east, south_west)

    @pl.when(has_north)
    def _():
        for copy in northward:
            copy.start()

    @pl.when(has_south)
    def _():
        for copy in southward:
            copy.start()

    to_east.start()
    to_west.start()

    for load in small:
        load.wait()
    slots = innov.shape[1]
    square = (blocks, blocks)
    diagonal = lax.broadcasted_iota(I32, square, 0) == lane_ids(square)
    tile = jnp.sum(jnp.where(diagonal, tile_row[...].astype(F32), 0.0), axis=1, keepdims=True)
    count = jnp.sum(jnp.where(diagonal, count_row[...].astype(F32), 0.0), axis=1, keepdims=True)
    live = lane_ids((blocks, slots)).astype(F32) < count
    bin_rows, bin_cols = rows // ROW_BINS, cols // COL_BINS
    row_at, col_at = obs_row[...], obs_col[...]
    bin_at = row_at // bin_rows * COL_BINS + col_at // bin_cols
    cell = (bin_at * bin_rows + row_at % bin_rows) * bin_cols + col_at % bin_cols + 1
    member = [jnp.where(jnp.logical_and(live, bin_at == b), 1.0, 0.0) for b in range(BINS)]
    to_left = jnp.where(lax.broadcasted_iota(I32, (slots, slots), 0) < lane_ids((slots, slots)), 1.0, 0.0).astype(BF16)
    ahead = jnp.dot(jnp.concatenate(member, axis=0).astype(BF16), to_left, preferred_element_type=F32)
    begin = jnp.ones((blocks, 1), F32)
    spot = jnp.zeros((blocks, slots), F32)
    for b in range(BINS):
        spot += member[b] * (ahead[b * blocks:(b + 1) * blocks] + begin)
        begin += jnp.sum(member[b], axis=1, keepdims=True)
    spots[...] = spot
    innov[...] = jnp.where(live, innov[...], 0.0)
    cells[...] = jnp.where(live, cell, 0).astype(F32)
    ranks = (lax.broadcasted_iota(I32, (slots, slots), 0) + 1).astype(F32)
    sub = lax.broadcasted_iota(I32, (ROWS8 - 4, slots), 0)

    def order(b, carry):
        move = jnp.where(ranks == spots[pl.ds(b, 1), :], 1.0, 0.0).astype(BF16)
        values = weight[b] * innov[pl.ds(b, 1), :]
        data = jnp.concatenate([values, jnp.where(sub == 0, cells[pl.ds(b, 1), :], 0.0)], axis=0)
        high = data.astype(BF16).astype(F32)
        mid = (data - high).astype(BF16).astype(F32)
        parts = jnp.concatenate([high, mid, data - high - mid], axis=0).astype(BF16)
        moved = lax.dot_general(parts, move, (((1,), (1,)), ((), ())), preferred_element_type=F32)
        ordered[pl.ds(pl.multiple_of(b * ROWS8, ROWS8), ROWS8), :] = moved[:ROWS8] + moved[ROWS8:2 * ROWS8] + moved[2 * ROWS8:]
        return carry

    lax.fori_loop(0, blocks, order, 0, unroll=max(d for d in range(1, 17) if blocks % d == 0))
    named = jnp.where(tile == lane_ids((blocks, lon)).astype(F32), 1.0, 0.0)
    earlier = jnp.where(lax.broadcasted_iota(I32, square, 0) > lane_ids(square), 1.0, 0.0)
    before = jnp.dot(earlier.astype(BF16), named.astype(BF16), preferred_element_type=F32)
    rank = jnp.sum(before * named, axis=1, keepdims=True)
    place = tile * CAP + rank
    wide = (blocks, ROWS8 * blocks)
    ids = lane_ids(wide)
    row_of = jnp.where(lax.broadcasted_iota(I32, wide, 0) == ids // ROWS8, place * ROWS8 + (ids % ROWS8).astype(F32), 0.0)
    row_of = jnp.sum(row_of, axis=0, keepdims=True)
    pick = lax.broadcasted_iota(I32, (CAP * lon * ROWS8, ROWS8 * blocks), 0).astype(F32) == row_of
    pick = jnp.where(pick, 1.0, 0.0).astype(BF16)
    data = ordered[...]
    high = data.astype(BF16)
    rest = data - high.astype(F32)
    mid = rest.astype(BF16)
    low = (rest - mid.astype(F32)).astype(BF16)
    sent = (jnp.dot(pick, high, preferred_element_type=F32) + jnp.dot(pick, mid, preferred_element_type=F32)
            + jnp.dot(pick, low, preferred_element_type=F32))
    send[...] = sent.reshape(CAP * lon, ROWS8, slots)[:, :PIECES, :]

    def block_copy(index):
        where = shift_to(my_lon, index, lon)
        return remote(send.at[pl.ds(CAP * where, CAP)], recv.at[pl.ds(CAP * my_lon, CAP)], a2a_sem, (my_lat, where))

    def send_blocks(index, carry):
        block_copy(index).start()
        return carry

    lax.fori_loop(1, lon, send_blocks, 0)
    mine = pl.ds(CAP * my_lon, CAP)
    own = pltpu.make_async_copy(send.at[mine], recv.at[mine], own_sem)
    own.start()

    @pl.when(has_south)
    def _():
        for copy in northward:
            copy.wait_recv()

    @pl.when(has_north)
    def _():
        for copy in southward:
            copy.wait_recv()

    to_east.wait_recv()
    to_west.wait_recv()

    def unpack(index):
        here = pl.ds(pl.multiple_of(index * ROWS8, ROWS8), ROWS8)
        from_east, from_west = east_got[here, :], west_got[here, :]
        for f in range(5):
            first = HALO * f
            right = jnp.logical_and(lane >= first, lane < first + HALO)
            first = (LANES - HALO + HALO * f) % LANES
            left = jnp.logical_and(lane >= first, lane < first + HALO)
            both = jnp.where(right, from_east, jnp.where(left, from_west, 0.0))
            fields[f, tiles, here, :] = pltpu.roll(both, LANES - HALO * f, 1) if f else both

    over(ext // ROWS8, unpack, 19)

    @pl.when(has_north)
    def _():
        for copy in northward:
            copy.wait_send()

    @pl.when(has_south)
    def _():
        for copy in southward:
            copy.wait_send()

    to_east.wait_send()
    to_west.wait_send()

    refs = (height, east_vel, north_vel, depth_east, depth_north)
    maps = columns_at(tiles + 1)

    def keep(f, c, k, value):
        refs[f][c, k] = value

    to_runs(maps, [fields.at[f] for f in range(5)], temp, number, keep)
    inner = pl.ds(0, number)
    stores = [pltpu.make_async_copy(ref.at[:, inner], fields_out.at[f], store_sem.at[f]) for f, ref in enumerate(refs)]
    for store in stores[3:]:
        store.start()
    steps(HALF, height, other, *refs[1:])
    for store in stores[:3]:
        store.start()

    own.wait()
    others = pl.ds(0, CAP * (lon - 1))
    every = pltpu.make_async_remote_copy(src_ref=send.at[others], dst_ref=recv.at[others], send_sem=a2a_sem.at[0],
                                         recv_sem=a2a_sem.at[1], device_id=(my_lat, east), device_id_type=MESH)
    every.wait_recv()
    every.wait_send()
    for store in stores:
        store.wait()


def spread_kernel(dims, recv, out, counts, found, packed, total, left_a, left_b, right_a, right_b, load_sem):
    rows, cols, lat, lon, blocks = dims
    tiles = cols // LANES
    segments = CAP * lon
    bin_rows, bin_cols = rows // ROW_BINS, cols // COL_BINS
    bins = ROW_BINS * COL_BINS
    padded = left_a.shape[0] // 2
    depth = GROUP * LANES
    room = segments + GROUP
    cell = recv[:, PIECES - 1, :]
    ones = jnp.ones((ROWS8, LANES), BF16)
    area = float(bin_rows * bin_cols)
    for b in range(bins):
        within = jnp.logical_and(cell > b * area, cell <= (b + 1) * area)
        live_of = lax.dot_general(ones, jnp.where(within, 1.0, 0.0).astype(BF16), (((1,), (1,)), ((), ())), preferred_element_type=F32)
        found[pl.ds(b, 1), :] = live_of[:1].astype(I32)
    found[pl.ds(bins, ROWS8 - bins), :] = jnp.zeros((ROWS8 - bins, segments), I32)
    load = pltpu.make_async_copy(found, counts, load_sem)
    load.start()
    total[...] = jnp.zeros_like(total)
    load.wait()
    lane = lane_ids((PIECES, LANES))
    zero = jnp.zeros((PIECES, LANES), F32)

    def append(segment, carry):
        block = recv[segment]
        begin = 0
        after = []
        for b, (fill, current) in enumerate(carry):
            number = counts[b, segment]
            chunk = lax.shift_right_logical(fill, 7)
            turned = pltpu.roll(block, (fill - begin) & (LANES - 1), 1)
            current = jnp.where(lane >= (fill & (LANES - 1)), turned, current)
            packed[chunk + b * room] = current
            begin = begin + number
            fill = fill + number
            after.append((fill, jnp.where(lax.shift_right_logical(fill, 7) > chunk, turned, current)))
        return tuple(after)

    filled = lax.fori_loop(0, segments, append, ((jnp.int32(0), zero),) * bins, unroll=min(UNROLL, segments))
    jobs, starts = [], [0]
    for b, (fill, current) in enumerate(filled):
        chunk = lax.shift_right_logical(fill, 7) + b * room
        packed[chunk] = jnp.where(lane < (fill & (LANES - 1)), current, 0.0)
        for extra in range(1, GROUP):
            packed[chunk + extra] = zero
        starts.append(starts[-1] + (fill + depth - 1) // depth)
    for extra in range(GROUP):
        packed[bins * room + extra] = zero
    count = starts[-1]

    def place(job):
        which = 0
        begin = 0
        for b in range(1, bins):
            past = job >= starts[b]
            which = jnp.where(past, b, which)
            begin = jnp.where(past, starts[b], begin)
        chunk = which * room + (job - begin) * GROUP
        return jnp.where(job < count, chunk, bins * room), jnp.where(job < count, which, 0)

    row_ids = lax.broadcasted_iota(IDS, (padded, depth), 0)
    col_ids = lax.broadcasted_iota(IDS, (bin_cols, depth), 0)
    one, none = jnp.array(1, BF16), jnp.array(0, BF16)

    def build(job, left, right):
        chunk, which = place(job)
        both = jnp.concatenate([packed[chunk + j] for j in range(GROUP)], axis=1)
        cell = both[4:5, :].astype(I32) - 1 - which * (bin_rows * bin_cols)
        row_at = cell // bin_cols if bin_cols & (bin_cols - 1) else lax.shift_right_arithmetic(cell, bin_cols.bit_length() - 1)
        col_at = cell - row_at * bin_cols

        def wide(value, kind, number):
            return jnp.broadcast_to(value, (number, depth)).astype(kind)

        here = row_ids == wide(row_at, IDS, padded)
        past = row_ids == wide(row_at + 1, IDS, padded)
        column = jnp.where(col_ids == wide(col_at, IDS, bin_cols), one, none)
        right[:, :depth] = column
        right[:, depth:] = column
        high = both[:4, :].astype(BF16).astype(F32)
        for part, values in enumerate((high, both[:4, :] - high)):
            for side in range(2):
                at = wide(values[side:side + 1, :], BF16, padded)
                above = wide(values[side + 2:side + 3, :], BF16, padded)
                left[pl.ds(side * padded, padded), pl.ds(part * depth, depth)] = jnp.where(here, at, jnp.where(past, above, none))

    def add(job, left, right):
        _, which = place(job)
        total[which] += lax.dot_general(left[...], right[...], (((1,), (1,)), ((), ())), preferred_element_type=F32)

    build(0, left_a, right_a)

    def pair(index, carry):
        build(2 * index + 1, left_b, right_b)
        add(2 * index, left_a, right_a)
        build(2 * index + 2, left_a, right_a)
        add(2 * index + 1, left_b, right_b)
        return carry

    lax.fori_loop(0, (count + 1) // 2, pair, 0)

    bin_tiles = bin_cols // LANES
    lane = lane_ids((bin_rows, LANES))
    for i in range(ROW_BINS):
        if i:
            for j in range(COL_BINS):
                for at in (0, padded):
                    total[i * COL_BINS + j, pl.ds(at, ROWS8), :] += total[(i - 1) * COL_BINS + j, pl.ds(at + bin_rows, ROWS8), :]
        before = jnp.zeros((bin_rows, LANES), F32)
        for t in range(tiles):
            which, span = i * COL_BINS + t // bin_tiles, pl.ds(t % bin_tiles * LANES, LANES)
            turned = pltpu.roll(total[which, pl.ds(padded, bin_rows), span], 1, 1)
            out[t, pl.ds(i * bin_rows, bin_rows), :] = total[which, pl.ds(0, bin_rows), span] + jnp.where(lane == 0, before, turned)
            before = turned


def finish_kernel(dims, fields_in, forcing_in, out, forcing, height, other, east_vel, north_vel, depth_east, depth_north, temp, done,
                  east_pack, west_pack, east_got, west_got, load_sem, row_sem, pack_sem, corner_sem, store_sem):
    rows, cols, lat, lon, blocks = dims
    tiles = cols // LANES
    ext = rows + 2 * HALO
    number = ext // ROWS8
    my_lat, my_lon = lax.axis_index("lat"), lax.axis_index("lon")
    east, west = lax.rem(my_lon + 1, lon), lax.rem(my_lon + lon - 1, lon)
    has_north, has_south = my_lat < lat - 1, my_lat > 0
    refs = (height, east_vel, north_vel, depth_east, depth_north)
    inner = pl.ds(0, number)
    loads = [pltpu.make_async_copy(forcing_in, forcing.at[pl.ds(0, tiles), pl.ds(HALO, rows), :], load_sem.at[5])]
    loads += [pltpu.make_async_copy(fields_in.at[f], ref.at[:, inner], load_sem.at[f]) for f, ref in enumerate(refs)]
    for load in loads:
        load.start()
    barrier = pltpu.get_barrier_semaphore()
    for has, where in ((has_north, my_lat + 1), (has_south, my_lat - 1)):
        @pl.when(has)
        def _():
            for column in (west, my_lon, east):
                pl.semaphore_signal(barrier, inc=1, device_id=(where, column), device_id_type=MESH)
    for column in (west, east):
        pl.semaphore_signal(barrier, inc=1, device_id=(my_lat, column), device_id_type=MESH)

    beyond = HALO - FRINGE
    for at in (0, ext - beyond):
        forcing[:, pl.ds(at, beyond), :] = jnp.zeros((tiles + 1, beyond, LANES), F32)
    for has, at in ((has_south, beyond), (has_north, HALO + rows)):
        @pl.when(jnp.logical_not(has))
        def _():
            forcing[:, pl.ds(at, FRINGE), :] = jnp.zeros((tiles + 1, FRINGE, LANES), F32)

    loads[0].wait()
    run = rows // 8
    lane = lane_ids((run, LANES))
    to_west = jnp.zeros((run, LANES), F32)
    to_east = to_west
    for g in range(8):
        here = pl.ds(HALO + run * g, run)
        inside = lane // FRINGE == g
        value = forcing[0, here, :]
        to_west = jnp.where(inside, pltpu.roll(value, FRINGE * g, 1) if g else value, to_west)
        value = forcing[tiles - 1, here, :]
        to_east = jnp.where(inside, pltpu.roll(value, (FRINGE * (g + 1)) % LANES, 1) if g < 7 else value, to_east)
    west_pack[pl.ds(0, run), :] = to_west
    east_pack[pl.ds(0, run), :] = to_east
    ends = (pl.ds(HALO, FRINGE), pl.ds(HALO + rows - FRINGE, FRINGE))
    outer = (pl.ds(HALO - FRINGE, FRINGE), pl.ds(HALO + rows, FRINGE))
    for at, here in zip((run, run + FRINGE), ends):
        west_pack[pl.ds(at, FRINGE), :] = forcing[0, here, :]
        east_pack[pl.ds(at, FRINGE), :] = forcing[tiles - 1, here, :]

    pl.semaphore_wait(barrier, 2 + 3 * has_north.astype(I32) + 3 * has_south.astype(I32))

    def remote(source, target, sems, where):
        return pltpu.make_async_remote_copy(src_ref=source, dst_ref=target, send_sem=sems.at[0], recv_sem=sems.at[1],
                                            device_id=where, device_id_type=MESH)

    main = pl.ds(0, tiles)
    strip, low_end, high_end = pl.ds(0, run), pl.ds(run, FRINGE), pl.ds(run + FRINGE, FRINGE)
    to_north = remote(forcing.at[main, ends[1], :], forcing.at[main, outer[0], :], row_sem.at[0], (my_lat + 1, my_lon))
    to_south = remote(forcing.at[main, ends[0], :], forcing.at[main, outer[1], :], row_sem.at[1], (my_lat - 1, my_lon))
    go_east = remote(east_pack.at[strip], west_got.at[strip], pack_sem.at[0], (my_lat, east))
    go_west = remote(west_pack.at[strip], east_got.at[strip], pack_sem.at[1], (my_lat, west))
    north_east = remote(east_pack.at[high_end], west_got.at[low_end], corner_sem.at[0], (my_lat + 1, east))
    north_west = remote(west_pack.at[high_end], east_got.at[low_end], corner_sem.at[1], (my_lat + 1, west))
    south_east = remote(east_pack.at[low_end], west_got.at[high_end], corner_sem.at[2], (my_lat - 1, east))
    south_west = remote(west_pack.at[low_end], east_got.at[high_end], corner_sem.at[3], (my_lat - 1, west))
    northward, southward = (to_north, north_east, north_west), (to_south, south_east, south_west)

    @pl.when(has_north)
    def _():
        for copy in northward:
            copy.start()

    @pl.when(has_south)
    def _():
        for copy in southward:
            copy.start()

    go_east.start()
    go_west.start()

    for load in loads[1:]:
        load.wait()

    @pl.when(has_south)
    def _():
        for copy in northward:
            copy.wait_recv()

    @pl.when(has_north)
    def _():
        for copy in southward:
            copy.wait_recv()

    go_east.wait_recv()
    go_west.wait_recv()
    right = lane < FRINGE
    left = lane >= LANES - FRINGE
    from_east, from_west = east_got[strip, :], west_got[strip, :]
    for g in range(8):
        here = pl.ds(HALO + run * g, run)
        one = pltpu.roll(from_east, (LANES - FRINGE * g) % LANES, 1) if g else from_east
        two = pltpu.roll(from_west, (LANES - FRINGE * (g + 1)) % LANES, 1) if g < 7 else from_west
        forcing[tiles, here, :] = jnp.where(right, one, jnp.where(left, two, 0.0))
    lane = lane_ids((FRINGE, LANES))
    right = lane < FRINGE
    left = lane >= LANES - FRINGE
    for has, end, at in ((has_south, low_end, HALO - FRINGE), (has_north, high_end, HALO + rows)):
        @pl.when(has)
        def _():
            forcing[tiles, pl.ds(at, FRINGE), :] = jnp.where(right, east_got[end, :], jnp.where(left, west_got[end, :], 0.0))

    maps = columns_at(tiles + 1)

    def keep(f, c, k, value):
        height[c, k] += value

    to_runs(maps, [forcing], temp, number, keep)
    steps(HALF, height, other, *refs[1:])
    stores = []

    def finished(t):
        store = pltpu.make_async_copy(done.at[:, t, pl.ds(HALO, rows), :], out.at[:, :, pl.ds(t * LANES, LANES)], store_sem.at[t])
        store.start()
        stores.append(store)

    from_runs(maps, refs[:3], temp, number, done, finished)

    @pl.when(has_north)
    def _():
        for copy in northward:
            copy.wait_send()

    @pl.when(has_south)
    def _():
        for copy in southward:
            copy.wait_send()

    go_east.wait_send()
    go_west.wait_send()
    for store in stores:
        store.wait()


def per_device(lat, lon, adjoint_state, face_depth, innovation, interp_weight, block_tile, block_count, obs_row, obs_col):
    rows, cols = adjoint_state.shape[1:]
    blocks, slots = innovation.shape
    tiles = cols // LANES
    dims = (rows, cols, lat, lon, blocks)
    ext = rows + 2 * HALO
    segments = CAP * lon
    vmem = pl.BlockSpec(memory_space=pltpu.VMEM)
    anywhere = pl.BlockSpec(memory_space=pl.ANY)
    dma = pltpu.SemaphoreType.DMA
    number = ext // ROWS8
    natural = pltpu.VMEM((5, tiles + 1, ext, LANES), F32)
    runs = [pltpu.VMEM((tiles + 1, number + 1, ROWS8, LANES), F32)] * 2 + [pltpu.VMEM((tiles + 1, number, ROWS8, LANES), F32)] * 4
    params = functools.partial(pltpu.CompilerParams, has_side_effects=True)
    fields, recv = pl.pallas_call(
        functools.partial(route_kernel, dims),
        name="route",
        out_shape=(
            jax.ShapeDtypeStruct((5, tiles + 1, number, ROWS8, LANES), F32),
            jax.ShapeDtypeStruct((segments, PIECES, slots), F32),
        ),
        in_specs=[anywhere] * 8,
        out_specs=(anywhere, anywhere),
        scratch_shapes=[
            natural, *runs,
            pltpu.VMEM((blocks, slots), F32),
            pltpu.VMEM((blocks, 4, slots), F32),
            pltpu.VMEM((1, blocks), I32),
            pltpu.VMEM((1, blocks), I32),
            pltpu.VMEM((blocks, slots), I32),
            pltpu.VMEM((blocks, slots), I32),
            pltpu.VMEM((blocks, slots), F32),
            pltpu.VMEM((blocks, slots), F32),
            pltpu.VMEM((ROWS8 * blocks, slots), F32),
            pltpu.VMEM((5, tiles + 1, number, ROWS8, LANES), F32),
            pltpu.VMEM((segments, PIECES, slots), F32),
            pltpu.VMEM((rows, LANES), F32),
            pltpu.VMEM((rows, LANES), F32),
            pltpu.VMEM((ext, LANES), F32),
            pltpu.VMEM((ext, LANES), F32),
            dma((2 * tiles,)), dma((6,)), dma((2, 2)), dma((2, 2)), dma((4, 2)), dma((2,)), dma, dma((5,)),
        ],
        compiler_params=params(collective_id=0, vmem_limit_bytes=56 << 20),
    )(adjoint_state, face_depth, innovation, interp_weight, block_tile.reshape(1, blocks), block_count.reshape(1, blocks),
      obs_row, obs_col)
    padded = rows if ROW_BINS == 1 else rows // ROW_BINS + 16
    forcing = pl.pallas_call(
        functools.partial(spread_kernel, dims),
        name="spread",
        out_shape=jax.ShapeDtypeStruct((tiles, rows, LANES), F32),
        in_specs=[vmem],
        out_specs=vmem,
        scratch_shapes=[
            pltpu.SMEM((ROWS8, segments), I32),
            pltpu.VMEM((ROWS8, segments), I32),
            pltpu.VMEM((BINS * (segments + GROUP) + GROUP, PIECES, LANES), F32),
            pltpu.VMEM((BINS, 2 * padded, cols // COL_BINS), F32),
            *[pltpu.VMEM((2 * padded, 2 * GROUP * LANES), BF16)] * 2,
            *[pltpu.VMEM((cols // COL_BINS, 2 * GROUP * LANES), BF16)] * 2,
            dma,
        ],
        compiler_params=pltpu.CompilerParams(vmem_limit_bytes=24 << 20),
    )(recv)
    run = rows // 8 + 2 * FRINGE
    return pl.pallas_call(
        functools.partial(finish_kernel, dims),
        name="finish",
        out_shape=jax.ShapeDtypeStruct((3, rows, cols), F32),
        in_specs=[anywhere] * 2,
        out_specs=anywhere,
        scratch_shapes=[
            pltpu.VMEM((tiles + 1, ext, LANES), F32),
            *runs,
            pltpu.VMEM((6, tiles + 1, number, ROWS8, LANES), F32),
            pltpu.VMEM((3, tiles, ext, LANES), F32),
            pltpu.VMEM((run, LANES), F32),
            pltpu.VMEM((run, LANES), F32),
            pltpu.VMEM((run, LANES), F32),
            pltpu.VMEM((run, LANES), F32),
            dma((6,)), dma((2, 2)), dma((2, 2)), dma((4, 2)), dma((tiles,)),
        ],
        compiler_params=params(collective_id=1, vmem_limit_bytes=50 << 20),
    )(fields, forcing)


def solution(mesh):
    return jax.shard_map(
        functools.partial(per_device, mesh.shape["lat"], mesh.shape["lon"]),
        mesh=mesh,
        in_specs=(
            P(None, "lat", "lon"),
            P(None, "lat", "lon"),
            P(("lat", "lon"), None),
            P(("lat", "lon"), None, None),
            P(("lat", "lon"), None),
            P(("lat", "lon"), None),
            P(("lat", "lon"), None),
            P(("lat", "lon"), None),
        ),
        out_specs=P(None, "lat", "lon"),
        check_vma=False,
    )
```

```python
import functools

import jax
import jax.numpy as jnp
from jax import lax
from jax.experimental import pallas as pl
from jax.experimental.pallas import tpu as pltpu
from jax.sharding import PartitionSpec as P

WIN = 6
WINDOWS = 4
CAP = 2
LANES = 128
ROWS8 = 8
HALO = WIN * WINDOWS
HALF = HALO // 2
FRINGE = 16
PIECES = 5
GROUP = 8
ROW_BINS = 1
COL_BINS = 2
BINS = ROW_BINS * COL_BINS
UNROLL = 32
IDS = jnp.int16
MESH = pl.DeviceIdType.MESH
F32 = jnp.float32
BF16 = jnp.bfloat16
I32 = jnp.int32


def lane_ids(shape):
    return lax.broadcasted_iota(I32, shape, len(shape) - 1)


def shift_to(me, index, lon):
    where = me + index
    return jnp.where(where >= lon, where - lon, where)


def columns_at(width):
    part = LANES // width
    lane = lane_ids((ROWS8, LANES))
    part_of, inside = lane // part, lane % part
    cuts = [(width * part * t - HALO) % LANES for t in range(width)]
    into = [(width * part * t - HALO + LANES + width * inside + (part_of + width - t) % width) % LANES for t in range(width)]
    turn = [part * ((part_of + c) % width) + inside for c in range(width)]
    back = [part * ((part_of + width - c) % width) + inside for c in range(width)]
    out = []
    for t in range(width):
        along = (lane + LANES - cuts[t]) % LANES
        out.append(jnp.minimum(part * ((along + t) % width) + along // width, LANES - 1))
    return lane, part_of, cuts, into, turn, back, out


def take(values, index):
    return jnp.take_along_axis(values, index, axis=1)


def by_part(part_of, choices):
    value = choices[-1]
    for p in range(len(choices) - 1):
        value = jnp.where(part_of == p, choices[p], value)
    return value


def over(number, body, most):
    size = max(d for d in range(1, number + 1) if number % d == 0 and d <= max(most, 1))

    def one(p, carry):
        for j in range(size):
            body(p * size + j)
        return carry

    lax.fori_loop(0, number // size, one, 0)


def to_runs(maps, natural, temp, number, keep):
    lane, part_of, cuts, into, turn, back, out = maps
    width = len(cuts)
    most = 100 // len(natural)
    for t in range(width):
        def sort(k):
            rows = pl.ds(k, ROWS8, stride=number)
            for f, ref in enumerate(natural):
                temp[f, t, k] = take(jnp.where(lane >= cuts[t], ref[(t - 1) % width, rows, :], ref[t, rows, :]), into[t])

        over(number, sort, most)
    for c in range(width):
        def mix(k):
            for f in range(len(natural)):
                value = by_part(part_of, [temp[f, (p - c) % width, k] for p in range(width)])
                keep(f, c, k, take(value, turn[c]) if c else value)

        over(number, mix, most)


def from_runs(maps, refs, temp, number, natural, finished):
    lane, part_of, cuts, into, turn, back, out = maps
    width, fields = len(cuts), len(refs)
    most = 120 // fields
    for c in range(1, width):
        def unmix(k):
            for f in range(fields):
                temp[f, c, k] = take(refs[f][c, k], back[c])

        over(number, unmix, most)
    for t in range(width):
        def unsort(k):
            for f in range(fields):
                parts = [(p - t) % width for p in range(width)]
                value = by_part(part_of, [temp[f, c, k] if c else refs[f][0, k] for c in parts])
                temp[fields + f, t, k] = take(value, out[t])

        over(number, unsort, most)
        if t:
            def join(k):
                for f in range(fields):
                    value = jnp.where(lane < cuts[t], temp[fields + f, t - 1, k], temp[fields + f, t, k])
                    natural[f, t - 1, pl.ds(k, ROWS8, stride=number), :] = value

            over(number, join, most)
            finished(t - 1)


def one_step(old, new, east_vel, north_vel, depth_east, depth_north):
    width, number = east_vel.shape[:2]
    cols = range(width)
    for c in cols:
        old[c, number] = pltpu.roll(old[c, 0], ROWS8 - 1, 0)
    end = number - 1
    south = [pltpu.roll(north_vel[c, end] + depth_north[c, end] * (old[c, number] - old[c, end]), 1, 0) for c in cols]
    for k in range(number):
        height = [old[c, k] for c in cols]
        height_e = height[1:] + [pltpu.roll(height[0], LANES - 1, 1)]
        east = [None] * width
        for c in [width - 1] + list(range(width - 1)):
            east[c] = east_vel[c, k] + depth_east[c, k] * (height_e[c] - height[c])
        west = [pltpu.roll(east[-1], 1, 1)] + east[:-1]
        north = [None] * width
        for c in cols:
            north[c] = north_vel[c, k] + depth_north[c, k] * (old[c, k + 1] - height[c])
            new[c, k] = height[c] + (east[c] - west[c]) + (north[c] - south[c])
            east_vel[c, k] = east[c]
            north_vel[c, k] = north[c]
        south = north


def steps(number, height, other, *rest):
    def two(_, carry):
        one_step(height, other, *rest)
        one_step(other, height, *rest)
        return carry

    lax.fori_loop(0, number // 2, two, 0)


def route_kernel(dims, state, depth, innov_in, weight_in, tile_in, count_in, row_in, col_in, fields_out, recv,
                 fields, height, other, east_vel, north_vel, depth_east, depth_north,
                 innov, weight, tile_row, count_row, obs_row, obs_col, spots, cells, ordered, temp, send, east_pack, west_pack, east_got, west_got,
                 load_sem, small_sem, row_sem, pack_sem, corner_sem, a2a_sem, own_sem, store_sem):
    rows, cols, lat, lon, blocks = dims
    tiles = cols // LANES
    ext = rows + 2 * HALO
    number = ext // ROWS8
    my_lat, my_lon = lax.axis_index("lat"), lax.axis_index("lon")
    east, west = lax.rem(my_lon + 1, lon), lax.rem(my_lon + lon - 1, lon)
    has_north, has_south = my_lat < lat - 1, my_lat > 0

    small = [pltpu.make_async_copy(source, target, small_sem.at[i]) for i, (source, target) in enumerate((
        (tile_in, tile_row), (count_in, count_row), (innov_in, innov), (weight_in, weight), (row_in, obs_row), (col_in, obs_col)))]
    for load in small:
        load.start()
    loads = []
    for t in range(tiles):
        span = pl.ds(t * LANES, LANES)
        for source, start, some in ((state, 0, 3), (depth, 3, 2)):
            loads.append(pltpu.make_async_copy(
                source.at[:, :, span], fields.at[pl.ds(start, some), t, pl.ds(HALO, rows), :], load_sem.at[len(loads)]))
    for load in loads:
        load.start()

    barrier = pltpu.get_barrier_semaphore()

    def greet(index, carry):
        pl.semaphore_signal(barrier, inc=1, device_id=(my_lat, shift_to(my_lon, index, lon)), device_id_type=MESH)
        return carry

    for has, where in ((has_north, my_lat + 1), (has_south, my_lat - 1)):
        @pl.when(has)
        def _():
            for column in (west, my_lon, east):
                pl.semaphore_signal(barrier, inc=1, device_id=(where, column), device_id_type=MESH)
    lax.fori_loop(1, lon, greet, 0, unroll=max(d for d in range(1, 10) if (lon - 1) % d == 0))

    for load in small:
        load.wait()
    slots = innov.shape[1]
    square = (blocks, blocks)
    diagonal = lax.broadcasted_iota(I32, square, 0) == lane_ids(square)
    tile = jnp.sum(jnp.where(diagonal, tile_row[...].astype(F32), 0.0), axis=1, keepdims=True)
    count = jnp.sum(jnp.where(diagonal, count_row[...].astype(F32), 0.0), axis=1, keepdims=True)
    live = lane_ids((blocks, slots)).astype(F32) < count
    bin_rows, bin_cols = rows // ROW_BINS, cols // COL_BINS
    row_at, col_at = obs_row[...], obs_col[...]
    bin_at = row_at // bin_rows * COL_BINS + col_at // bin_cols
    cell = (bin_at * bin_rows + row_at % bin_rows) * bin_cols + col_at % bin_cols + 1
    member = [jnp.where(jnp.logical_and(live, bin_at == b), 1.0, 0.0) for b in range(BINS)]
    to_left = jnp.where(lax.broadcasted_iota(I32, (slots, slots), 0) < lane_ids((slots, slots)), 1.0, 0.0).astype(BF16)
    ahead = jnp.dot(jnp.concatenate(member, axis=0).astype(BF16), to_left, preferred_element_type=F32)
    begin = jnp.ones((blocks, 1), F32)
    spot = jnp.zeros((blocks, slots), F32)
    for b in range(BINS):
        spot += member[b] * (ahead[b * blocks:(b + 1) * blocks] + begin)
        begin += jnp.sum(member[b], axis=1, keepdims=True)
    spots[...] = spot
    innov[...] = jnp.where(live, innov[...], 0.0)
    cells[...] = jnp.where(live, cell, 0).astype(F32)
    ranks = (lax.broadcasted_iota(I32, (slots, slots), 0) + 1).astype(F32)
    sub = lax.broadcasted_iota(I32, (ROWS8 - 4, slots), 0)

    def order(b, carry):
        move = jnp.where(ranks == spots[pl.ds(b, 1), :], 1.0, 0.0).astype(BF16)
        values = weight[b] * innov[pl.ds(b, 1), :]
        data = jnp.concatenate([values, jnp.where(sub == 0, cells[pl.ds(b, 1), :], 0.0)], axis=0)
        high = data.astype(BF16).astype(F32)
        mid = (data - high).astype(BF16).astype(F32)
        parts = jnp.concatenate([high, mid, data - high - mid], axis=0).astype(BF16)
        moved = lax.dot_general(parts, move, (((1,), (1,)), ((), ())), preferred_element_type=F32)
        ordered[pl.ds(pl.multiple_of(b * ROWS8, ROWS8), ROWS8), :] = moved[:ROWS8] + moved[ROWS8:2 * ROWS8] + moved[2 * ROWS8:]
        return carry

    lax.fori_loop(0, blocks, order, 0, unroll=max(d for d in range(1, 17) if blocks % d == 0))
    named = jnp.where(tile == lane_ids((blocks, lon)).astype(F32), 1.0, 0.0)
    earlier = jnp.where(lax.broadcasted_iota(I32, square, 0) > lane_ids(square), 1.0, 0.0)
    before = jnp.dot(earlier.astype(BF16), named.astype(BF16), preferred_element_type=F32)
    rank = jnp.sum(before * named, axis=1, keepdims=True)
    place = tile * CAP + rank
    wide = (blocks, ROWS8 * blocks)
    ids = lane_ids(wide)
    row_of = jnp.where(lax.broadcasted_iota(I32, wide, 0) == ids // ROWS8, place * ROWS8 + (ids % ROWS8).astype(F32), 0.0)
    row_of = jnp.sum(row_of, axis=0, keepdims=True)
    pick = lax.broadcasted_iota(I32, (CAP * lon * ROWS8, ROWS8 * blocks), 0).astype(F32) == row_of
    pick = jnp.where(pick, 1.0, 0.0).astype(BF16)
    data = ordered[...]
    high = data.astype(BF16)
    rest = data - high.astype(F32)
    mid = rest.astype(BF16)
    low = (rest - mid.astype(F32)).astype(BF16)
    sent = (jnp.dot(pick, high, preferred_element_type=F32) + jnp.dot(pick, mid, preferred_element_type=F32)
            + jnp.dot(pick, low, preferred_element_type=F32))
    send[...] = sent.reshape(CAP * lon, ROWS8, slots)[:, :PIECES, :]

    zero_rows = jnp.zeros((5, tiles, HALO, LANES), F32)

    @pl.when(jnp.logical_not(has_south))
    def _():
        fields[:, pl.ds(0, tiles), pl.ds(0, HALO), :] = zero_rows
        east_got[pl.ds(0, HALO), :] = zero_rows[0, 0]
        west_got[pl.ds(0, HALO), :] = zero_rows[0, 0]

    @pl.when(jnp.logical_not(has_north))
    def _():
        fields[:, pl.ds(0, tiles), pl.ds(HALO + rows, HALO), :] = zero_rows
        east_got[pl.ds(HALO + rows, HALO), :] = zero_rows[0, 0]
        west_got[pl.ds(HALO + rows, HALO), :] = zero_rows[0, 0]

    for load in loads:
        load.wait()

    @pl.when(jnp.logical_not(has_north))
    def _():
        wall = pl.ds(HALO + rows - ROWS8, ROWS8)
        keep = lax.broadcasted_iota(I32, (tiles, ROWS8, LANES), 1) < ROWS8 - 1
        fields[4, pl.ds(0, tiles), wall, :] = jnp.where(keep, fields[4, pl.ds(0, tiles), wall, :], 0.0)

    lane = lane_ids((ROWS8, LANES))

    def pack(index, carry):
        base = pl.multiple_of(index * ROWS8, ROWS8)
        here = pl.ds(HALO + base, ROWS8)
        to_west = jnp.zeros((ROWS8, LANES), F32)
        to_east = to_west
        for f in range(5):
            first = HALO * f
            inside = jnp.logical_and(lane >= first, lane < first + HALO)
            to_west = jnp.where(inside, pltpu.roll(fields[f, 0, here, :], first, 1) if f else fields[f, 0, here, :], to_west)
            first = (LANES - HALO + HALO * f) % LANES
            inside = jnp.logical_and(lane >= first, lane < first + HALO)
            value = fields[f, tiles - 1, here, :]
            to_east = jnp.where(inside, pltpu.roll(value, HALO * f, 1) if f else value, to_east)
        west_pack[pl.ds(base, ROWS8), :] = to_west
        east_pack[pl.ds(base, ROWS8), :] = to_east
        return carry

    lax.fori_loop(0, rows // ROWS8, pack, 0, unroll=8)

    pl.semaphore_wait(barrier, lon - 1 + 3 * has_north.astype(I32) + 3 * has_south.astype(I32))

    def remote(source, target, sems, where):
        return pltpu.make_async_remote_copy(src_ref=source, dst_ref=target, send_sem=sems.at[0], recv_sem=sems.at[1],
                                            device_id=where, device_id_type=MESH)

    main = pl.ds(HALO, rows)
    low_rows, high_rows = pl.ds(0, HALO), pl.ds(HALO + rows, HALO)
    inner = pl.ds(0, tiles)
    to_north = remote(fields.at[:, inner, pl.ds(rows, HALO), :], fields.at[:, inner, low_rows, :], row_sem.at[0], (my_lat + 1, my_lon))
    to_south = remote(fields.at[:, inner, pl.ds(HALO, HALO), :], fields.at[:, inner, high_rows, :], row_sem.at[1], (my_lat - 1, my_lon))
    to_east = remote(east_pack, west_got.at[main], pack_sem.at[0], (my_lat, east))
    to_west = remote(west_pack, east_got.at[main], pack_sem.at[1], (my_lat, west))
    tail = pl.ds(rows - HALO, HALO)
    north_east = remote(east_pack.at[tail], west_got.at[low_rows], corner_sem.at[0], (my_lat + 1, east))
    north_west = remote(west_pack.at[tail], east_got.at[low_rows], corner_sem.at[1], (my_lat + 1, west))
    south_east = remote(east_pack.at[low_rows], west_got.at[high_rows], corner_sem.at[2], (my_lat - 1, east))
    south_west = remote(west_pack.at[low_rows], east_got.at[high_rows], corner_sem.at[3], (my_lat - 1, west))
    northward, southward = (to_north, north_east, north_west), (to_south, south_east, south_west)

    @pl.when(has_north)
    def _():
        for copy in northward:
            copy.start()

    @pl.when(has_south)
    def _():
        for copy in southward:
            copy.start()

    to_east.start()
    to_west.start()

    def block_copy(index):
        where = shift_to(my_lon, index, lon)
        return remote(send.at[pl.ds(CAP * where, CAP)], recv.at[pl.ds(CAP * my_lon, CAP)], a2a_sem, (my_lat, where))

    def send_blocks(index, carry):
        block_copy(index).start()
        return carry

    lax.fori_loop(1, lon, send_blocks, 0, unroll=max(d for d in range(1, 10) if (lon - 1) % d == 0))
    mine = pl.ds(CAP * my_lon, CAP)
    own = pltpu.make_async_copy(send.at[mine], recv.at[mine], own_sem)
    own.start()

    @pl.when(has_south)
    def _():
        for copy in northward:
            copy.wait_recv()

    @pl.when(has_north)
    def _():
        for copy in southward:
            copy.wait_recv()

    to_east.wait_recv()
    to_west.wait_recv()

    def unpack(index):
        here = pl.ds(pl.multiple_of(index * ROWS8, ROWS8), ROWS8)
        from_east, from_west = east_got[here, :], west_got[here, :]
        for f in range(5):
            first = HALO * f
            right = jnp.logical_and(lane >= first, lane < first + HALO)
            first = (LANES - HALO + HALO * f) % LANES
            left = jnp.logical_and(lane >= first, lane < first + HALO)
            both = jnp.where(right, from_east, jnp.where(left, from_west, 0.0))
            fields[f, tiles, here, :] = pltpu.roll(both, LANES - HALO * f, 1) if f else both

    over(ext // ROWS8, unpack, 19)

    @pl.when(has_north)
    def _():
        for copy in northward:
            copy.wait_send()

    @pl.when(has_south)
    def _():
        for copy in southward:
            copy.wait_send()

    to_east.wait_send()
    to_west.wait_send()

    refs = (height, east_vel, north_vel, depth_east, depth_north)
    maps = columns_at(tiles + 1)

    def keep(f, c, k, value):
        refs[f][c, k] = value

    to_runs(maps, [fields.at[f] for f in range(5)], temp, number, keep)
    inner = pl.ds(0, number)
    stores = [pltpu.make_async_copy(ref.at[:, inner], fields_out.at[f], store_sem.at[f]) for f, ref in enumerate(refs)]
    for store in stores[3:]:
        store.start()
    steps(HALF, height, other, *refs[1:])
    for store in stores[:3]:
        store.start()

    own.wait()
    others = pl.ds(0, CAP * (lon - 1))
    every = pltpu.make_async_remote_copy(src_ref=send.at[others], dst_ref=recv.at[others], send_sem=a2a_sem.at[0],
                                         recv_sem=a2a_sem.at[1], device_id=(my_lat, east), device_id_type=MESH)
    every.wait_recv()
    every.wait_send()
    for store in stores:
        store.wait()


def spread_kernel(dims, recv, out, counts, found, packed, total, left_a, left_b, right_a, right_b, load_sem):
    rows, cols, lat, lon, blocks = dims
    tiles = cols // LANES
    segments = CAP * lon
    bin_rows, bin_cols = rows // ROW_BINS, cols // COL_BINS
    bins = ROW_BINS * COL_BINS
    padded = left_a.shape[0] // 2
    depth = GROUP * LANES
    room = segments + GROUP
    cell = recv[:, PIECES - 1, :]
    ones = jnp.ones((ROWS8, LANES), BF16)
    area = float(bin_rows * bin_cols)
    for b in range(bins):
        within = jnp.logical_and(cell > b * area, cell <= (b + 1) * area)
        live_of = lax.dot_general(ones, jnp.where(within, 1.0, 0.0).astype(BF16), (((1,), (1,)), ((), ())), preferred_element_type=F32)
        found[pl.ds(b, 1), :] = live_of[:1].astype(I32)
    found[pl.ds(bins, ROWS8 - bins), :] = jnp.zeros((ROWS8 - bins, segments), I32)
    load = pltpu.make_async_copy(found, counts, load_sem)
    load.start()
    total[...] = jnp.zeros_like(total)
    load.wait()
    lane = lane_ids((PIECES, LANES))
    zero = jnp.zeros((PIECES, LANES), F32)

    def append(segment, carry):
        block = recv[segment]
        begin = 0
        after = []
        for b, (fill, current) in enumerate(carry):
            number = counts[b, segment]
            chunk = lax.shift_right_logical(fill, 7)
            turned = pltpu.roll(block, (fill - begin) & (LANES - 1), 1)
            current = jnp.where(lane >= (fill & (LANES - 1)), turned, current)
            packed[chunk + b * room] = current
            begin = begin + number
            fill = fill + number
            after.append((fill, jnp.where(lax.shift_right_logical(fill, 7) > chunk, turned, current)))
        return tuple(after)

    filled = lax.fori_loop(0, segments, append, ((jnp.int32(0), zero),) * bins, unroll=min(UNROLL, segments))
    jobs, starts = [], [0]
    for b, (fill, current) in enumerate(filled):
        chunk = lax.shift_right_logical(fill, 7) + b * room
        packed[chunk] = jnp.where(lane < (fill & (LANES - 1)), current, 0.0)
        for extra in range(1, GROUP):
            packed[chunk + extra] = zero
        starts.append(starts[-1] + (fill + depth - 1) // depth)
    for extra in range(GROUP):
        packed[bins * room + extra] = zero
    count = starts[-1]

    def place(job):
        which = 0
        begin = 0
        for b in range(1, bins):
            past = job >= starts[b]
            which = jnp.where(past, b, which)
            begin = jnp.where(past, starts[b], begin)
        chunk = which * room + (job - begin) * GROUP
        return jnp.where(job < count, chunk, bins * room), jnp.where(job < count, which, 0)

    row_ids = lax.broadcasted_iota(IDS, (padded, depth), 0)
    col_ids = lax.broadcasted_iota(IDS, (bin_cols, depth), 0)
    one, none = jnp.array(1, BF16), jnp.array(0, BF16)

    def build(job, left, right):
        chunk, which = place(job)
        both = jnp.concatenate([packed[chunk + j] for j in range(GROUP)], axis=1)
        cell = both[4:5, :].astype(I32) - 1 - which * (bin_rows * bin_cols)
        row_at = cell // bin_cols if bin_cols & (bin_cols - 1) else lax.shift_right_arithmetic(cell, bin_cols.bit_length() - 1)
        col_at = cell - row_at * bin_cols

        def wide(value, kind, number):
            return jnp.broadcast_to(value, (number, depth)).astype(kind)

        here = row_ids == wide(row_at, IDS, padded)
        past = row_ids == wide(row_at + 1, IDS, padded)
        column = jnp.where(col_ids == wide(col_at, IDS, bin_cols), one, none)
        right[:, :depth] = column
        right[:, depth:] = column
        high = both[:4, :].astype(BF16).astype(F32)
        for part, values in enumerate((high, both[:4, :] - high)):
            for side in range(2):
                at = wide(values[side:side + 1, :], BF16, padded)
                above = wide(values[side + 2:side + 3, :], BF16, padded)
                left[pl.ds(side * padded, padded), pl.ds(part * depth, depth)] = jnp.where(here, at, jnp.where(past, above, none))

    def add(job, left, right):
        _, which = place(job)
        total[which] += lax.dot_general(left[...], right[...], (((1,), (1,)), ((), ())), preferred_element_type=F32)

    build(0, left_a, right_a)

    def pair(index, carry):
        build(2 * index + 1, left_b, right_b)
        add(2 * index, left_a, right_a)
        build(2 * index + 2, left_a, right_a)
        add(2 * index + 1, left_b, right_b)
        return carry

    lax.fori_loop(0, (count + 1) // 2, pair, 0)

    bin_tiles = bin_cols // LANES
    lane = lane_ids((bin_rows, LANES))
    for i in range(ROW_BINS):
        if i:
            for j in range(COL_BINS):
                for at in (0, padded):
                    total[i * COL_BINS + j, pl.ds(at, ROWS8), :] += total[(i - 1) * COL_BINS + j, pl.ds(at + bin_rows, ROWS8), :]
        before = jnp.zeros((bin_rows, LANES), F32)
        for t in range(tiles):
            which, span = i * COL_BINS + t // bin_tiles, pl.ds(t % bin_tiles * LANES, LANES)
            turned = pltpu.roll(total[which, pl.ds(padded, bin_rows), span], 1, 1)
            out[t, pl.ds(i * bin_rows, bin_rows), :] = total[which, pl.ds(0, bin_rows), span] + jnp.where(lane == 0, before, turned)
            before = turned


def finish_kernel(dims, fields_in, forcing_in, out, forcing, height, other, east_vel, north_vel, depth_east, depth_north, temp, done,
                  east_pack, west_pack, east_got, west_got, load_sem, row_sem, pack_sem, corner_sem, store_sem):
    rows, cols, lat, lon, blocks = dims
    tiles = cols // LANES
    ext = rows + 2 * HALO
    number = ext // ROWS8
    my_lat, my_lon = lax.axis_index("lat"), lax.axis_index("lon")
    east, west = lax.rem(my_lon + 1, lon), lax.rem(my_lon + lon - 1, lon)
    has_north, has_south = my_lat < lat - 1, my_lat > 0
    refs = (height, east_vel, north_vel, depth_east, depth_north)
    inner = pl.ds(0, number)
    loads = [pltpu.make_async_copy(forcing_in, forcing.at[pl.ds(0, tiles), pl.ds(HALO, rows), :], load_sem.at[5])]
    loads += [pltpu.make_async_copy(fields_in.at[f], ref.at[:, inner], load_sem.at[f]) for f, ref in enumerate(refs)]
    for load in loads:
        load.start()
    barrier = pltpu.get_barrier_semaphore()
    for has, where in ((has_north, my_lat + 1), (has_south, my_lat - 1)):
        @pl.when(has)
        def _():
            for column in (west, my_lon, east):
                pl.semaphore_signal(barrier, inc=1, device_id=(where, column), device_id_type=MESH)
    for column in (west, east):
        pl.semaphore_signal(barrier, inc=1, device_id=(my_lat, column), device_id_type=MESH)

    beyond = HALO - FRINGE
    for at in (0, ext - beyond):
        forcing[:, pl.ds(at, beyond), :] = jnp.zeros((tiles + 1, beyond, LANES), F32)
    for has, at in ((has_south, beyond), (has_north, HALO + rows)):
        @pl.when(jnp.logical_not(has))
        def _():
            forcing[:, pl.ds(at, FRINGE), :] = jnp.zeros((tiles + 1, FRINGE, LANES), F32)

    loads[0].wait()
    run = rows // 8
    lane = lane_ids((run, LANES))
    to_west = jnp.zeros((run, LANES), F32)
    to_east = to_west
    for g in range(8):
        here = pl.ds(HALO + run * g, run)
        inside = lane // FRINGE == g
        value = forcing[0, here, :]
        to_west = jnp.where(inside, pltpu.roll(value, FRINGE * g, 1) if g else value, to_west)
        value = forcing[tiles - 1, here, :]
        to_east = jnp.where(inside, pltpu.roll(value, (FRINGE * (g + 1)) % LANES, 1) if g < 7 else value, to_east)
    west_pack[pl.ds(0, run), :] = to_west
    east_pack[pl.ds(0, run), :] = to_east
    ends = (pl.ds(HALO, FRINGE), pl.ds(HALO + rows - FRINGE, FRINGE))
    outer = (pl.ds(HALO - FRINGE, FRINGE), pl.ds(HALO + rows, FRINGE))
    for at, here in zip((run, run + FRINGE), ends):
        west_pack[pl.ds(at, FRINGE), :] = forcing[0, here, :]
        east_pack[pl.ds(at, FRINGE), :] = forcing[tiles - 1, here, :]

    pl.semaphore_wait(barrier, 2 + 3 * has_north.astype(I32) + 3 * has_south.astype(I32))

    def remote(source, target, sems, where):
        return pltpu.make_async_remote_copy(src_ref=source, dst_ref=target, send_sem=sems.at[0], recv_sem=sems.at[1],
                                            device_id=where, device_id_type=MESH)

    main = pl.ds(0, tiles)
    strip, low_end, high_end = pl.ds(0, run), pl.ds(run, FRINGE), pl.ds(run + FRINGE, FRINGE)
    to_north = remote(forcing.at[main, ends[1], :], forcing.at[main, outer[0], :], row_sem.at[0], (my_lat + 1, my_lon))
    to_south = remote(forcing.at[main, ends[0], :], forcing.at[main, outer[1], :], row_sem.at[1], (my_lat - 1, my_lon))
    go_east = remote(east_pack.at[strip], west_got.at[strip], pack_sem.at[0], (my_lat, east))
    go_west = remote(west_pack.at[strip], east_got.at[strip], pack_sem.at[1], (my_lat, west))
    north_east = remote(east_pack.at[high_end], west_got.at[low_end], corner_sem.at[0], (my_lat + 1, east))
    north_west = remote(west_pack.at[high_end], east_got.at[low_end], corner_sem.at[1], (my_lat + 1, west))
    south_east = remote(east_pack.at[low_end], west_got.at[high_end], corner_sem.at[2], (my_lat - 1, east))
    south_west = remote(west_pack.at[low_end], east_got.at[high_end], corner_sem.at[3], (my_lat - 1, west))
    northward, southward = (to_north, north_east, north_west), (to_south, south_east, south_west)

    @pl.when(has_north)
    def _():
        for copy in northward:
            copy.start()

    @pl.when(has_south)
    def _():
        for copy in southward:
            copy.start()

    go_east.start()
    go_west.start()

    for load in loads[1:]:
        load.wait()

    @pl.when(has_south)
    def _():
        for copy in northward:
            copy.wait_recv()

    @pl.when(has_north)
    def _():
        for copy in southward:
            copy.wait_recv()

    go_east.wait_recv()
    go_west.wait_recv()
    right = lane < FRINGE
    left = lane >= LANES - FRINGE
    from_east, from_west = east_got[strip, :], west_got[strip, :]
    for g in range(8):
        here = pl.ds(HALO + run * g, run)
        one = pltpu.roll(from_east, (LANES - FRINGE * g) % LANES, 1) if g else from_east
        two = pltpu.roll(from_west, (LANES - FRINGE * (g + 1)) % LANES, 1) if g < 7 else from_west
        forcing[tiles, here, :] = jnp.where(right, one, jnp.where(left, two, 0.0))
    lane = lane_ids((FRINGE, LANES))
    right = lane < FRINGE
    left = lane >= LANES - FRINGE
    for has, end, at in ((has_south, low_end, HALO - FRINGE), (has_north, high_end, HALO + rows)):
        @pl.when(has)
        def _():
            forcing[tiles, pl.ds(at, FRINGE), :] = jnp.where(right, east_got[end, :], jnp.where(left, west_got[end, :], 0.0))

    maps = columns_at(tiles + 1)

    def keep(f, c, k, value):
        height[c, k] += value

    to_runs(maps, [forcing], temp, number, keep)
    steps(HALF, height, other, *refs[1:])
    stores = []

    def finished(t):
        store = pltpu.make_async_copy(done.at[:, t, pl.ds(HALO, rows), :], out.at[:, :, pl.ds(t * LANES, LANES)], store_sem.at[t])
        store.start()
        stores.append(store)

    from_runs(maps, refs[:3], temp, number, done, finished)

    @pl.when(has_north)
    def _():
        for copy in northward:
            copy.wait_send()

    @pl.when(has_south)
    def _():
        for copy in southward:
            copy.wait_send()

    go_east.wait_send()
    go_west.wait_send()
    for store in stores:
        store.wait()


def per_device(lat, lon, adjoint_state, face_depth, innovation, interp_weight, block_tile, block_count, obs_row, obs_col):
    rows, cols = adjoint_state.shape[1:]
    blocks, slots = innovation.shape
    tiles = cols // LANES
    dims = (rows, cols, lat, lon, blocks)
    ext = rows + 2 * HALO
    segments = CAP * lon
    vmem = pl.BlockSpec(memory_space=pltpu.VMEM)
    anywhere = pl.BlockSpec(memory_space=pl.ANY)
    dma = pltpu.SemaphoreType.DMA
    number = ext // ROWS8
    natural = pltpu.VMEM((5, tiles + 1, ext, LANES), F32)
    runs = [pltpu.VMEM((tiles + 1, number + 1, ROWS8, LANES), F32)] * 2 + [pltpu.VMEM((tiles + 1, number, ROWS8, LANES), F32)] * 4
    params = functools.partial(pltpu.CompilerParams, has_side_effects=True)
    fields, recv = pl.pallas_call(
        functools.partial(route_kernel, dims),
        name="route",
        out_shape=(
            jax.ShapeDtypeStruct((5, tiles + 1, number, ROWS8, LANES), F32),
            jax.ShapeDtypeStruct((segments, PIECES, slots), F32),
        ),
        in_specs=[anywhere] * 8,
        out_specs=(anywhere, anywhere),
        scratch_shapes=[
            natural, *runs,
            pltpu.VMEM((blocks, slots), F32),
            pltpu.VMEM((blocks, 4, slots), F32),
            pltpu.VMEM((1, blocks), I32),
            pltpu.VMEM((1, blocks), I32),
            pltpu.VMEM((blocks, slots), I32),
            pltpu.VMEM((blocks, slots), I32),
            pltpu.VMEM((blocks, slots), F32),
            pltpu.VMEM((blocks, slots), F32),
            pltpu.VMEM((ROWS8 * blocks, slots), F32),
            pltpu.VMEM((5, tiles + 1, number, ROWS8, LANES), F32),
            pltpu.VMEM((segments, PIECES, slots), F32),
            pltpu.VMEM((rows, LANES), F32),
            pltpu.VMEM((rows, LANES), F32),
            pltpu.VMEM((ext, LANES), F32),
            pltpu.VMEM((ext, LANES), F32),
            dma((2 * tiles,)), dma((6,)), dma((2, 2)), dma((2, 2)), dma((4, 2)), dma((2,)), dma, dma((5,)),
        ],
        compiler_params=params(collective_id=0, vmem_limit_bytes=56 << 20),
    )(adjoint_state, face_depth, innovation, interp_weight, block_tile.reshape(1, blocks), block_count.reshape(1, blocks),
      obs_row, obs_col)
    padded = rows if ROW_BINS == 1 else rows // ROW_BINS + 16
    forcing = pl.pallas_call(
        functools.partial(spread_kernel, dims),
        name="spread",
        out_shape=jax.ShapeDtypeStruct((tiles, rows, LANES), F32),
        in_specs=[vmem],
        out_specs=vmem,
        scratch_shapes=[
            pltpu.SMEM((ROWS8, segments), I32),
            pltpu.VMEM((ROWS8, segments), I32),
            pltpu.VMEM((BINS * (segments + GROUP) + GROUP, PIECES, LANES), F32),
            pltpu.VMEM((BINS, 2 * padded, cols // COL_BINS), F32),
            *[pltpu.VMEM((2 * padded, 2 * GROUP * LANES), BF16)] * 2,
            *[pltpu.VMEM((cols // COL_BINS, 2 * GROUP * LANES), BF16)] * 2,
            dma,
        ],
        compiler_params=pltpu.CompilerParams(vmem_limit_bytes=24 << 20),
    )(recv)
    run = rows // 8 + 2 * FRINGE
    return pl.pallas_call(
        functools.partial(finish_kernel, dims),
        name="finish",
        out_shape=jax.ShapeDtypeStruct((3, rows, cols), F32),
        in_specs=[anywhere] * 2,
        out_specs=anywhere,
        scratch_shapes=[
            pltpu.VMEM((tiles + 1, ext, LANES), F32),
            *runs,
            pltpu.VMEM((6, tiles + 1, number, ROWS8, LANES), F32),
            pltpu.VMEM((3, tiles, ext, LANES), F32),
            pltpu.VMEM((run, LANES), F32),
            pltpu.VMEM((run, LANES), F32),
            pltpu.VMEM((run, LANES), F32),
            pltpu.VMEM((run, LANES), F32),
            dma((6,)), dma((2, 2)), dma((2, 2)), dma((4, 2)), dma((tiles,)),
        ],
        compiler_params=params(collective_id=1, vmem_limit_bytes=50 << 20),
    )(fields, forcing)


def solution(mesh):
    return jax.shard_map(
        functools.partial(per_device, mesh.shape["lat"], mesh.shape["lon"]),
        mesh=mesh,
        in_specs=(
            P(None, "lat", "lon"),
            P(None, "lat", "lon"),
            P(("lat", "lon"), None),
            P(("lat", "lon"), None, None),
            P(("lat", "lon"), None),
            P(("lat", "lon"), None),
            P(("lat", "lon"), None),
            P(("lat", "lon"), None),
        ),
        out_specs=P(None, "lat", "lon"),
        check_vma=False,
    )
```

```python
import functools

import jax
import jax.numpy as jnp
from jax import lax
from jax.experimental import pallas as pl
from jax.experimental.pallas import tpu as pltpu
from jax.sharding import PartitionSpec as P

WIN = 6
WINDOWS = 4
CAP = 2
LANES = 128
ROWS8 = 8
HALO = WIN * WINDOWS
HALF = HALO // 2
FRINGE = 16
PIECES = 5
GROUP = 8
ROW_BINS = 1
COL_BINS = 2
BINS = ROW_BINS * COL_BINS
UNROLL = 32
IDS = jnp.int16
MESH = pl.DeviceIdType.MESH
F32 = jnp.float32
BF16 = jnp.bfloat16
I32 = jnp.int32


def lane_ids(shape):
    return lax.broadcasted_iota(I32, shape, len(shape) - 1)


def shift_to(me, index, lon):
    where = me + index
    return jnp.where(where >= lon, where - lon, where)


def columns_at(width):
    part = LANES // width
    lane = lane_ids((ROWS8, LANES))
    part_of, inside = lane // part, lane % part
    cuts = [(width * part * t - HALO) % LANES for t in range(width)]
    into = [(width * part * t - HALO + LANES + width * inside + (part_of + width - t) % width) % LANES for t in range(width)]
    turn = [part * ((part_of + c) % width) + inside for c in range(width)]
    back = [part * ((part_of + width - c) % width) + inside for c in range(width)]
    out = []
    for t in range(width):
        along = (lane + LANES - cuts[t]) % LANES
        out.append(jnp.minimum(part * ((along + t) % width) + along // width, LANES - 1))
    return lane, part_of, cuts, into, turn, back, out


def take(values, index):
    return jnp.take_along_axis(values, index, axis=1)


def by_part(part_of, choices):
    value = choices[-1]
    for p in range(len(choices) - 1):
        value = jnp.where(part_of == p, choices[p], value)
    return value


def over(number, body, most):
    size = max(d for d in range(1, number + 1) if number % d == 0 and d <= max(most, 1))

    def one(p, carry):
        for j in range(size):
            body(p * size + j)
        return carry

    lax.fori_loop(0, number // size, one, 0)


def to_runs(maps, natural, temp, number, keep):
    lane, part_of, cuts, into, turn, back, out = maps
    width = len(cuts)
    most = 100 // len(natural)
    for t in range(width):
        def sort(k):
            rows = pl.ds(k, ROWS8, stride=number)
            for f, ref in enumerate(natural):
                temp[f, t, k] = take(jnp.where(lane >= cuts[t], ref[(t - 1) % width, rows, :], ref[t, rows, :]), into[t])

        over(number, sort, most)
    for c in range(width):
        def mix(k):
            for f in range(len(natural)):
                value = by_part(part_of, [temp[f, (p - c) % width, k] for p in range(width)])
                keep(f, c, k, take(value, turn[c]) if c else value)

        over(number, mix, most)


def from_runs(maps, refs, temp, number, natural, finished):
    lane, part_of, cuts, into, turn, back, out = maps
    width, fields = len(cuts), len(refs)
    most = 120 // fields
    for c in range(1, width):
        def unmix(k):
            for f in range(fields):
                temp[f, c, k] = take(refs[f][c, k], back[c])

        over(number, unmix, most)
    for t in range(width):
        def unsort(k):
            for f in range(fields):
                parts = [(p - t) % width for p in range(width)]
                value = by_part(part_of, [temp[f, c, k] if c else refs[f][0, k] for c in parts])
                temp[fields + f, t, k] = take(value, out[t])

        over(number, unsort, most)
        if t:
            def join(k):
                for f in range(fields):
                    value = jnp.where(lane < cuts[t], temp[fields + f, t - 1, k], temp[fields + f, t, k])
                    natural[f, t - 1, pl.ds(k, ROWS8, stride=number), :] = value

            over(number, join, most)
            finished(t - 1)


def one_step(old, new, east_vel, north_vel, depth_east, depth_north):
    width, number = east_vel.shape[:2]
    cols = range(width)
    for c in cols:
        old[c, number] = pltpu.roll(old[c, 0], ROWS8 - 1, 0)
    end = number - 1
    south = [pltpu.roll(north_vel[c, end] + depth_north[c, end] * (old[c, number] - old[c, end]), 1, 0) for c in cols]
    for k in range(number):
        height = [old[c, k] for c in cols]
        height_e = height[1:] + [pltpu.roll(height[0], LANES - 1, 1)]
        east = [None] * width
        for c in [width - 1] + list(range(width - 1)):
            east[c] = east_vel[c, k] + depth_east[c, k] * (height_e[c] - height[c])
        west = [pltpu.roll(east[-1], 1, 1)] + east[:-1]
        north = [None] * width
        for c in cols:
            north[c] = north_vel[c, k] + depth_north[c, k] * (old[c, k + 1] - height[c])
            new[c, k] = height[c] + (east[c] - west[c]) + (north[c] - south[c])
            east_vel[c, k] = east[c]
            north_vel[c, k] = north[c]
        south = north


def steps(number, height, other, *rest):
    def two(_, carry):
        one_step(height, other, *rest)
        one_step(other, height, *rest)
        return carry

    lax.fori_loop(0, number // 2, two, 0)


def route_kernel(dims, state, depth, innov_in, weight_in, tile_in, count_in, row_in, col_in, fields_out, recv,
                 fields, height, east_vel, north_vel, depth_east, depth_north,
                 innov, weight, tile_row, count_row, obs_row, obs_col, spots, cells, ordered, temp, send, east_pack, west_pack, east_got, west_got,
                 load_sem, small_sem, row_sem, pack_sem, corner_sem, a2a_sem, own_sem, store_sem):
    rows, cols, lat, lon, blocks = dims
    tiles = cols // LANES
    ext = rows + 2 * HALO
    number = ext // ROWS8
    my_lat, my_lon = lax.axis_index("lat"), lax.axis_index("lon")
    east, west = lax.rem(my_lon + 1, lon), lax.rem(my_lon + lon - 1, lon)
    has_north, has_south = my_lat < lat - 1, my_lat > 0

    small = [pltpu.make_async_copy(source, target, small_sem.at[i]) for i, (source, target) in enumerate((
        (tile_in, tile_row), (count_in, count_row), (innov_in, innov), (weight_in, weight), (row_in, obs_row), (col_in, obs_col)))]
    for load in small:
        load.start()
    loads = []
    for t in range(tiles):
        span = pl.ds(t * LANES, LANES)
        for source, start, some in ((state, 0, 3), (depth, 3, 2)):
            loads.append(pltpu.make_async_copy(
                source.at[:, :, span], fields.at[pl.ds(start, some), t, pl.ds(HALO, rows), :], load_sem.at[len(loads)]))
    for load in loads:
        load.start()

    barrier = pltpu.get_barrier_semaphore()

    def greet(index, carry):
        pl.semaphore_signal(barrier, inc=1, device_id=(my_lat, shift_to(my_lon, index, lon)), device_id_type=MESH)
        return carry

    for has, where in ((has_north, my_lat + 1), (has_south, my_lat - 1)):
        @pl.when(has)
        def _():
            for column in (west, my_lon, east):
                pl.semaphore_signal(barrier, inc=1, device_id=(where, column), device_id_type=MESH)
    lax.fori_loop(1, lon, greet, 0, unroll=max(d for d in range(1, 10) if (lon - 1) % d == 0))

    for load in small:
        load.wait()
    slots = innov.shape[1]
    square = (blocks, blocks)
    diagonal = lax.broadcasted_iota(I32, square, 0) == lane_ids(square)
    tile = jnp.sum(jnp.where(diagonal, tile_row[...].astype(F32), 0.0), axis=1, keepdims=True)
    count = jnp.sum(jnp.where(diagonal, count_row[...].astype(F32), 0.0), axis=1, keepdims=True)
    live = lane_ids((blocks, slots)).astype(F32) < count
    bin_rows, bin_cols = rows // ROW_BINS, cols // COL_BINS
    row_at, col_at = obs_row[...], obs_col[...]
    bin_at = row_at // bin_rows * COL_BINS + col_at // bin_cols
    cell = (bin_at * bin_rows + row_at % bin_rows) * bin_cols + col_at % bin_cols + 1
    member = [jnp.where(jnp.logical_and(live, bin_at == b), 1.0, 0.0) for b in range(BINS)]
    to_left = jnp.where(lax.broadcasted_iota(I32, (slots, slots), 0) < lane_ids((slots, slots)), 1.0, 0.0).astype(BF16)
    ahead = jnp.dot(jnp.concatenate(member, axis=0).astype(BF16), to_left, preferred_element_type=F32)
    begin = jnp.ones((blocks, 1), F32)
    spot = jnp.zeros((blocks, slots), F32)
    for b in range(BINS):
        spot += member[b] * (ahead[b * blocks:(b + 1) * blocks] + begin)
        begin += jnp.sum(member[b], axis=1, keepdims=True)
    spots[...] = spot
    innov[...] = jnp.where(live, innov[...], 0.0)
    cells[...] = jnp.where(live, cell, 0).astype(F32)
    ranks = (lax.broadcasted_iota(I32, (slots, slots), 0) + 1).astype(F32)
    sub = lax.broadcasted_iota(I32, (ROWS8 - 4, slots), 0)

    def order(b, carry):
        move = jnp.where(ranks == spots[pl.ds(b, 1), :], 1.0, 0.0).astype(BF16)
        values = weight[b] * innov[pl.ds(b, 1), :]
        data = jnp.concatenate([values, jnp.where(sub == 0, cells[pl.ds(b, 1), :], 0.0)], axis=0)
        high = data.astype(BF16).astype(F32)
        mid = (data - high).astype(BF16).astype(F32)
        parts = jnp.concatenate([high, mid, data - high - mid], axis=0).astype(BF16)
        moved = lax.dot_general(parts, move, (((1,), (1,)), ((), ())), preferred_element_type=F32)
        ordered[pl.ds(pl.multiple_of(b * ROWS8, ROWS8), ROWS8), :] = moved[:ROWS8] + moved[ROWS8:2 * ROWS8] + moved[2 * ROWS8:]
        return carry

    lax.fori_loop(0, blocks, order, 0, unroll=max(d for d in range(1, 17) if blocks % d == 0))
    named = jnp.where(tile == lane_ids((blocks, lon)).astype(F32), 1.0, 0.0)
    earlier = jnp.where(lax.broadcasted_iota(I32, square, 0) > lane_ids(square), 1.0, 0.0)
    before = jnp.dot(earlier.astype(BF16), named.astype(BF16), preferred_element_type=F32)
    rank = jnp.sum(before * named, axis=1, keepdims=True)
    place = tile * CAP + rank
    wide = (blocks, ROWS8 * blocks)
    ids = lane_ids(wide)
    row_of = jnp.where(lax.broadcasted_iota(I32, wide, 0) == ids // ROWS8, place * ROWS8 + (ids % ROWS8).astype(F32), 0.0)
    row_of = jnp.sum(row_of, axis=0, keepdims=True)
    pick = lax.broadcasted_iota(I32, (CAP * lon * ROWS8, ROWS8 * blocks), 0).astype(F32) == row_of
    pick = jnp.where(pick, 1.0, 0.0).astype(BF16)
    data = ordered[...]
    high = data.astype(BF16)
    rest = data - high.astype(F32)
    mid = rest.astype(BF16)
    low = (rest - mid.astype(F32)).astype(BF16)
    sent = (jnp.dot(pick, high, preferred_element_type=F32) + jnp.dot(pick, mid, preferred_element_type=F32)
            + jnp.dot(pick, low, preferred_element_type=F32))
    send[...] = sent.reshape(CAP * lon, ROWS8, slots)[:, :PIECES, :]

    zero_rows = jnp.zeros((5, tiles, HALO, LANES), F32)

    @pl.when(jnp.logical_not(has_south))
    def _():
        fields[:, pl.ds(0, tiles), pl.ds(0, HALO), :] = zero_rows
        east_got[pl.ds(0, HALO), :] = zero_rows[0, 0]
        west_got[pl.ds(0, HALO), :] = zero_rows[0, 0]

    @pl.when(jnp.logical_not(has_north))
    def _():
        fields[:, pl.ds(0, tiles), pl.ds(HALO + rows, HALO), :] = zero_rows
        east_got[pl.ds(HALO + rows, HALO), :] = zero_rows[0, 0]
        west_got[pl.ds(HALO + rows, HALO), :] = zero_rows[0, 0]

    for load in loads:
        load.wait()

    @pl.when(jnp.logical_not(has_north))
    def _():
        wall = pl.ds(HALO + rows - ROWS8, ROWS8)
        keep = lax.broadcasted_iota(I32, (tiles, ROWS8, LANES), 1) < ROWS8 - 1
        fields[4, pl.ds(0, tiles), wall, :] = jnp.where(keep, fields[4, pl.ds(0, tiles), wall, :], 0.0)

    lane = lane_ids((ROWS8, LANES))

    def pack(index, carry):
        base = pl.multiple_of(index * ROWS8, ROWS8)
        here = pl.ds(HALO + base, ROWS8)
        to_west = jnp.zeros((ROWS8, LANES), F32)
        to_east = to_west
        for f in range(5):
            first = HALO * f
            inside = jnp.logical_and(lane >= first, lane < first + HALO)
            to_west = jnp.where(inside, pltpu.roll(fields[f, 0, here, :], first, 1) if f else fields[f, 0, here, :], to_west)
            first = (LANES - HALO + HALO * f) % LANES
            inside = jnp.logical_and(lane >= first, lane < first + HALO)
            value = fields[f, tiles - 1, here, :]
            to_east = jnp.where(inside, pltpu.roll(value, HALO * f, 1) if f else value, to_east)
        west_pack[pl.ds(base, ROWS8), :] = to_west
        east_pack[pl.ds(base, ROWS8), :] = to_east
        return carry

    lax.fori_loop(0, rows // ROWS8, pack, 0, unroll=8)

    pl.semaphore_wait(barrier, lon - 1 + 3 * has_north.astype(I32) + 3 * has_south.astype(I32))

    def remote(source, target, sems, where):
        return pltpu.make_async_remote_copy(src_ref=source, dst_ref=target, send_sem=sems.at[0], recv_sem=sems.at[1],
                                            device_id=where, device_id_type=MESH)

    main = pl.ds(HALO, rows)
    low_rows, high_rows = pl.ds(0, HALO), pl.ds(HALO + rows, HALO)
    inner = pl.ds(0, tiles)
    to_north = remote(fields.at[:, inner, pl.ds(rows, HALO), :], fields.at[:, inner, low_rows, :], row_sem.at[0], (my_lat + 1, my_lon))
    to_south = remote(fields.at[:, inner, pl.ds(HALO, HALO), :], fields.at[:, inner, high_rows, :], row_sem.at[1], (my_lat - 1, my_lon))
    to_east = remote(east_pack, west_got.at[main], pack_sem.at[0], (my_lat, east))
    to_west = remote(west_pack, east_got.at[main], pack_sem.at[1], (my_lat, west))
    tail = pl.ds(rows - HALO, HALO)
    north_east = remote(east_pack.at[tail], west_got.at[low_rows], corner_sem.at[0], (my_lat + 1, east))
    north_west = remote(west_pack.at[tail], east_got.at[low_rows], corner_sem.at[1], (my_lat + 1, west))
    south_east = remote(east_pack.at[low_rows], west_got.at[high_rows], corner_sem.at[2], (my_lat - 1, east))
    south_west = remote(west_pack.at[low_rows], east_got.at[high_rows], corner_sem.at[3], (my_lat - 1, west))
    northward, southward = (to_north, north_east, north_west), (to_south, south_east, south_west)

    @pl.when(has_north)
    def _():
        for copy in northward:
            copy.start()

    @pl.when(has_south)
    def _():
        for copy in southward:
            copy.start()

    to_east.start()
    to_west.start()

    def block_copy(index):
        where = shift_to(my_lon, index, lon)
        return remote(send.at[pl.ds(CAP * where, CAP)], recv.at[pl.ds(CAP * my_lon, CAP)], a2a_sem, (my_lat, where))

    def send_blocks(index, carry):
        block_copy(index).start()
        return carry

    lax.fori_loop(1, lon, send_blocks, 0, unroll=max(d for d in range(1, 10) if (lon - 1) % d == 0))
    mine = pl.ds(CAP * my_lon, CAP)
    own = pltpu.make_async_copy(send.at[mine], recv.at[mine], own_sem)
    own.start()

    @pl.when(has_south)
    def _():
        for copy in northward:
            copy.wait_recv()

    @pl.when(has_north)
    def _():
        for copy in southward:
            copy.wait_recv()

    to_east.wait_recv()
    to_west.wait_recv()

    def unpack(index):
        here = pl.ds(pl.multiple_of(index * ROWS8, ROWS8), ROWS8)
        from_east, from_west = east_got[here, :], west_got[here, :]
        for f in range(5):
            first = HALO * f
            right = jnp.logical_and(lane >= first, lane < first + HALO)
            first = (LANES - HALO + HALO * f) % LANES
            left = jnp.logical_and(lane >= first, lane < first + HALO)
            both = jnp.where(right, from_east, jnp.where(left, from_west, 0.0))
            fields[f, tiles, here, :] = pltpu.roll(both, LANES - HALO * f, 1) if f else both

    over(ext // ROWS8, unpack, 19)

    @pl.when(has_north)
    def _():
        for copy in northward:
            copy.wait_send()

    @pl.when(has_south)
    def _():
        for copy in southward:
            copy.wait_send()

    to_east.wait_send()
    to_west.wait_send()

    refs = (height, east_vel, north_vel, depth_east, depth_north)
    maps = columns_at(tiles + 1)

    def keep(f, c, k, value):
        refs[f][c, k] = value

    to_runs(maps, [fields.at[f] for f in range(5)], temp, number, keep)
    inner = pl.ds(0, number)
    stores = [pltpu.make_async_copy(ref.at[:, inner], fields_out.at[f], store_sem.at[f]) for f, ref in enumerate(refs)]
    for store in stores:
        store.start()

    own.wait()
    others = pl.ds(0, CAP * (lon - 1))
    every = pltpu.make_async_remote_copy(src_ref=send.at[others], dst_ref=recv.at[others], send_sem=a2a_sem.at[0],
                                         recv_sem=a2a_sem.at[1], device_id=(my_lat, east), device_id_type=MESH)
    every.wait_recv()
    every.wait_send()
    for store in stores:
        store.wait()


def spread_kernel(dims, recv, out, counts, found, packed, total, left_a, left_b, right_a, right_b, load_sem):
    rows, cols, lat, lon, blocks = dims
    tiles = cols // LANES
    segments = CAP * lon
    bin_rows, bin_cols = rows // ROW_BINS, cols // COL_BINS
    bins = ROW_BINS * COL_BINS
    padded = left_a.shape[0] // 2
    depth = GROUP * LANES
    room = segments + GROUP
    cell = recv[:, PIECES - 1, :]
    ones = jnp.ones((ROWS8, LANES), BF16)
    area = float(bin_rows * bin_cols)
    for b in range(bins):
        within = jnp.logical_and(cell > b * area, cell <= (b + 1) * area)
        live_of = lax.dot_general(ones, jnp.where(within, 1.0, 0.0).astype(BF16), (((1,), (1,)), ((), ())), preferred_element_type=F32)
        found[pl.ds(b, 1), :] = live_of[:1].astype(I32)
    found[pl.ds(bins, ROWS8 - bins), :] = jnp.zeros((ROWS8 - bins, segments), I32)
    load = pltpu.make_async_copy(found, counts, load_sem)
    load.start()
    total[...] = jnp.zeros_like(total)
    load.wait()
    lane = lane_ids((PIECES, LANES))
    zero = jnp.zeros((PIECES, LANES), F32)

    def append(segment, carry):
        block = recv[segment]
        begin = 0
        after = []
        for b, (fill, current) in enumerate(carry):
            number = counts[b, segment]
            chunk = lax.shift_right_logical(fill, 7)
            turned = pltpu.roll(block, (fill - begin) & (LANES - 1), 1)
            current = jnp.where(lane >= (fill & (LANES - 1)), turned, current)
            packed[chunk + b * room] = current
            begin = begin + number
            fill = fill + number
            after.append((fill, jnp.where(lax.shift_right_logical(fill, 7) > chunk, turned, current)))
        return tuple(after)

    filled = lax.fori_loop(0, segments, append, ((jnp.int32(0), zero),) * bins, unroll=min(UNROLL, segments))
    jobs, starts = [], [0]
    for b, (fill, current) in enumerate(filled):
        chunk = lax.shift_right_logical(fill, 7) + b * room
        packed[chunk] = jnp.where(lane < (fill & (LANES - 1)), current, 0.0)
        for extra in range(1, GROUP):
            packed[chunk + extra] = zero
        starts.append(starts[-1] + (fill + depth - 1) // depth)
    for extra in range(GROUP):
        packed[bins * room + extra] = zero
    count = starts[-1]

    def place(job):
        which = 0
        begin = 0
        for b in range(1, bins):
            past = job >= starts[b]
            which = jnp.where(past, b, which)
            begin = jnp.where(past, starts[b], begin)
        chunk = which * room + (job - begin) * GROUP
        return jnp.where(job < count, chunk, bins * room), jnp.where(job < count, which, 0)

    row_ids = lax.broadcasted_iota(IDS, (padded, depth), 0)
    col_ids = lax.broadcasted_iota(IDS, (bin_cols, depth), 0)
    one, none = jnp.array(1, BF16), jnp.array(0, BF16)

    def build(job, left, right):
        chunk, which = place(job)
        both = jnp.concatenate([packed[chunk + j] for j in range(GROUP)], axis=1)
        cell = both[4:5, :].astype(I32) - 1 - which * (bin_rows * bin_cols)
        row_at = cell // bin_cols if bin_cols & (bin_cols - 1) else lax.shift_right_arithmetic(cell, bin_cols.bit_length() - 1)
        col_at = cell - row_at * bin_cols

        def wide(value, kind, number):
            return jnp.broadcast_to(value, (number, depth)).astype(kind)

        here = row_ids == wide(row_at, IDS, padded)
        past = row_ids == wide(row_at + 1, IDS, padded)
        column = jnp.where(col_ids == wide(col_at, IDS, bin_cols), one, none)
        right[:, :depth] = column
        right[:, depth:] = column
        high = both[:4, :].astype(BF16).astype(F32)
        for part, values in enumerate((high, both[:4, :] - high)):
            for side in range(2):
                at = wide(values[side:side + 1, :], BF16, padded)
                above = wide(values[side + 2:side + 3, :], BF16, padded)
                left[pl.ds(side * padded, padded), pl.ds(part * depth, depth)] = jnp.where(here, at, jnp.where(past, above, none))

    def add(job, left, right):
        _, which = place(job)
        total[which] += lax.dot_general(left[...], right[...], (((1,), (1,)), ((), ())), preferred_element_type=F32)

    build(0, left_a, right_a)

    def pair(index, carry):
        build(2 * index + 1, left_b, right_b)
        add(2 * index, left_a, right_a)
        build(2 * index + 2, left_a, right_a)
        add(2 * index + 1, left_b, right_b)
        return carry

    lax.fori_loop(0, (count + 1) // 2, pair, 0)

    bin_tiles = bin_cols // LANES
    lane = lane_ids((bin_rows, LANES))
    for i in range(ROW_BINS):
        if i:
            for j in range(COL_BINS):
                for at in (0, padded):
                    total[i * COL_BINS + j, pl.ds(at, ROWS8), :] += total[(i - 1) * COL_BINS + j, pl.ds(at + bin_rows, ROWS8), :]
        before = jnp.zeros((bin_rows, LANES), F32)
        for t in range(tiles):
            which, span = i * COL_BINS + t // bin_tiles, pl.ds(t % bin_tiles * LANES, LANES)
            turned = pltpu.roll(total[which, pl.ds(padded, bin_rows), span], 1, 1)
            out[t, pl.ds(i * bin_rows, bin_rows), :] = total[which, pl.ds(0, bin_rows), span] + jnp.where(lane == 0, before, turned)
            before = turned


def finish_kernel(dims, fields_in, forcing_in, out, forcing, height, other, east_vel, north_vel, depth_east, depth_north, temp, done,
                  east_pack, west_pack, east_got, west_got, load_sem, row_sem, pack_sem, corner_sem, store_sem):
    rows, cols, lat, lon, blocks = dims
    tiles = cols // LANES
    ext = rows + 2 * HALO
    number = ext // ROWS8
    my_lat, my_lon = lax.axis_index("lat"), lax.axis_index("lon")
    east, west = lax.rem(my_lon + 1, lon), lax.rem(my_lon + lon - 1, lon)
    has_north, has_south = my_lat < lat - 1, my_lat > 0
    refs = (height, east_vel, north_vel, depth_east, depth_north)
    inner = pl.ds(0, number)
    loads = [pltpu.make_async_copy(forcing_in, forcing.at[pl.ds(0, tiles), pl.ds(HALO, rows), :], load_sem.at[5])]
    loads += [pltpu.make_async_copy(fields_in.at[f], ref.at[:, inner], load_sem.at[f]) for f, ref in enumerate(refs)]
    for load in loads:
        load.start()
    barrier = pltpu.get_barrier_semaphore()
    for has, where in ((has_north, my_lat + 1), (has_south, my_lat - 1)):
        @pl.when(has)
        def _():
            for column in (west, my_lon, east):
                pl.semaphore_signal(barrier, inc=1, device_id=(where, column), device_id_type=MESH)
    for column in (west, east):
        pl.semaphore_signal(barrier, inc=1, device_id=(my_lat, column), device_id_type=MESH)

    beyond = HALO - FRINGE
    for at in (0, ext - beyond):
        forcing[:, pl.ds(at, beyond), :] = jnp.zeros((tiles + 1, beyond, LANES), F32)
    for has, at in ((has_south, beyond), (has_north, HALO + rows)):
        @pl.when(jnp.logical_not(has))
        def _():
            forcing[:, pl.ds(at, FRINGE), :] = jnp.zeros((tiles + 1, FRINGE, LANES), F32)

    loads[0].wait()
    run = rows // 8
    lane = lane_ids((run, LANES))
    to_west = jnp.zeros((run, LANES), F32)
    to_east = to_west
    for g in range(8):
        here = pl.ds(HALO + run * g, run)
        inside = lane // FRINGE == g
        value = forcing[0, here, :]
        to_west = jnp.where(inside, pltpu.roll(value, FRINGE * g, 1) if g else value, to_west)
        value = forcing[tiles - 1, here, :]
        to_east = jnp.where(inside, pltpu.roll(value, (FRINGE * (g + 1)) % LANES, 1) if g < 7 else value, to_east)
    west_pack[pl.ds(0, run), :] = to_west
    east_pack[pl.ds(0, run), :] = to_east
    ends = (pl.ds(HALO, FRINGE), pl.ds(HALO + rows - FRINGE, FRINGE))
    outer = (pl.ds(HALO - FRINGE, FRINGE), pl.ds(HALO + rows, FRINGE))
    for at, here in zip((run, run + FRINGE), ends):
        west_pack[pl.ds(at, FRINGE), :] = forcing[0, here, :]
        east_pack[pl.ds(at, FRINGE), :] = forcing[tiles - 1, here, :]

    pl.semaphore_wait(barrier, 2 + 3 * has_north.astype(I32) + 3 * has_south.astype(I32))

    def remote(source, target, sems, where):
        return pltpu.make_async_remote_copy(src_ref=source, dst_ref=target, send_sem=sems.at[0], recv_sem=sems.at[1],
                                            device_id=where, device_id_type=MESH)

    main = pl.ds(0, tiles)
    strip, low_end, high_end = pl.ds(0, run), pl.ds(run, FRINGE), pl.ds(run + FRINGE, FRINGE)
    to_north = remote(forcing.at[main, ends[1], :], forcing.at[main, outer[0], :], row_sem.at[0], (my_lat + 1, my_lon))
    to_south = remote(forcing.at[main, ends[0], :], forcing.at[main, outer[1], :], row_sem.at[1], (my_lat - 1, my_lon))
    go_east = remote(east_pack.at[strip], west_got.at[strip], pack_sem.at[0], (my_lat, east))
    go_west = remote(west_pack.at[strip], east_got.at[strip], pack_sem.at[1], (my_lat, west))
    north_east = remote(east_pack.at[high_end], west_got.at[low_end], corner_sem.at[0], (my_lat + 1, east))
    north_west = remote(west_pack.at[high_end], east_got.at[low_end], corner_sem.at[1], (my_lat + 1, west))
    south_east = remote(east_pack.at[low_end], west_got.at[high_end], corner_sem.at[2], (my_lat - 1, east))
    south_west = remote(west_pack.at[low_end], east_got.at[high_end], corner_sem.at[3], (my_lat - 1, west))
    northward, southward = (to_north, north_east, north_west), (to_south, south_east, south_west)

    @pl.when(has_north)
    def _():
        for copy in northward:
            copy.start()

    @pl.when(has_south)
    def _():
        for copy in southward:
            copy.start()

    go_east.start()
    go_west.start()

    for load in loads[1:]:
        load.wait()
    steps(HALF, height, other, *refs[1:])

    @pl.when(has_south)
    def _():
        for copy in northward:
            copy.wait_recv()

    @pl.when(has_north)
    def _():
        for copy in southward:
            copy.wait_recv()

    go_east.wait_recv()
    go_west.wait_recv()
    right = lane < FRINGE
    left = lane >= LANES - FRINGE
    from_east, from_west = east_got[strip, :], west_got[strip, :]
    for g in range(8):
        here = pl.ds(HALO + run * g, run)
        one = pltpu.roll(from_east, (LANES - FRINGE * g) % LANES, 1) if g else from_east
        two = pltpu.roll(from_west, (LANES - FRINGE * (g + 1)) % LANES, 1) if g < 7 else from_west
        forcing[tiles, here, :] = jnp.where(right, one, jnp.where(left, two, 0.0))
    lane = lane_ids((FRINGE, LANES))
    right = lane < FRINGE
    left = lane >= LANES - FRINGE
    for has, end, at in ((has_south, low_end, HALO - FRINGE), (has_north, high_end, HALO + rows)):
        @pl.when(has)
        def _():
            forcing[tiles, pl.ds(at, FRINGE), :] = jnp.where(right, east_got[end, :], jnp.where(left, west_got[end, :], 0.0))

    maps = columns_at(tiles + 1)

    def keep(f, c, k, value):
        height[c, k] += value

    to_runs(maps, [forcing], temp, number, keep)
    steps(HALF, height, other, *refs[1:])
    stores = []

    def finished(t):
        store = pltpu.make_async_copy(done.at[:, t, pl.ds(HALO, rows), :], out.at[:, :, pl.ds(t * LANES, LANES)], store_sem.at[t])
        store.start()
        stores.append(store)

    from_runs(maps, refs[:3], temp, number, done, finished)

    @pl.when(has_north)
    def _():
        for copy in northward:
            copy.wait_send()

    @pl.when(has_south)
    def _():
        for copy in southward:
            copy.wait_send()

    go_east.wait_send()
    go_west.wait_send()
    for store in stores:
        store.wait()


def per_device(lat, lon, adjoint_state, face_depth, innovation, interp_weight, block_tile, block_count, obs_row, obs_col):
    rows, cols = adjoint_state.shape[1:]
    blocks, slots = innovation.shape
    tiles = cols // LANES
    dims = (rows, cols, lat, lon, blocks)
    ext = rows + 2 * HALO
    segments = CAP * lon
    vmem = pl.BlockSpec(memory_space=pltpu.VMEM)
    anywhere = pl.BlockSpec(memory_space=pl.ANY)
    dma = pltpu.SemaphoreType.DMA
    number = ext // ROWS8
    natural = pltpu.VMEM((5, tiles + 1, ext, LANES), F32)
    runs = [pltpu.VMEM((tiles + 1, number + 1, ROWS8, LANES), F32)] * 2 + [pltpu.VMEM((tiles + 1, number, ROWS8, LANES), F32)] * 4
    params = functools.partial(pltpu.CompilerParams, has_side_effects=True)
    fields, recv = pl.pallas_call(
        functools.partial(route_kernel, dims),
        name="route",
        out_shape=(
            jax.ShapeDtypeStruct((5, tiles + 1, number, ROWS8, LANES), F32),
            jax.ShapeDtypeStruct((segments, PIECES, slots), F32),
        ),
        in_specs=[anywhere] * 8,
        out_specs=(anywhere, anywhere),
        scratch_shapes=[
            natural, *runs[1:],
            pltpu.VMEM((blocks, slots), F32),
            pltpu.VMEM((blocks, 4, slots), F32),
            pltpu.VMEM((1, blocks), I32),
            pltpu.VMEM((1, blocks), I32),
            pltpu.VMEM((blocks, slots), I32),
            pltpu.VMEM((blocks, slots), I32),
            pltpu.VMEM((blocks, slots), F32),
            pltpu.VMEM((blocks, slots), F32),
            pltpu.VMEM((ROWS8 * blocks, slots), F32),
            pltpu.VMEM((5, tiles + 1, number, ROWS8, LANES), F32),
            pltpu.VMEM((segments, PIECES, slots), F32),
            pltpu.VMEM((rows, LANES), F32),
            pltpu.VMEM((rows, LANES), F32),
            pltpu.VMEM((ext, LANES), F32),
            pltpu.VMEM((ext, LANES), F32),
            dma((2 * tiles,)), dma((6,)), dma((2, 2)), dma((2, 2)), dma((4, 2)), dma((2,)), dma, dma((5,)),
        ],
        compiler_params=params(collective_id=0, vmem_limit_bytes=56 << 20),
    )(adjoint_state, face_depth, innovation, interp_weight, block_tile.reshape(1, blocks), block_count.reshape(1, blocks),
      obs_row, obs_col)
    padded = rows if ROW_BINS == 1 else rows // ROW_BINS + 16
    forcing = pl.pallas_call(
        functools.partial(spread_kernel, dims),
        name="spread",
        out_shape=jax.ShapeDtypeStruct((tiles, rows, LANES), F32),
        in_specs=[vmem],
        out_specs=vmem,
        scratch_shapes=[
            pltpu.SMEM((ROWS8, segments), I32),
            pltpu.VMEM((ROWS8, segments), I32),
            pltpu.VMEM((BINS * (segments + GROUP) + GROUP, PIECES, LANES), F32),
            pltpu.VMEM((BINS, 2 * padded, cols // COL_BINS), F32),
            *[pltpu.VMEM((2 * padded, 2 * GROUP * LANES), BF16)] * 2,
            *[pltpu.VMEM((cols // COL_BINS, 2 * GROUP * LANES), BF16)] * 2,
            dma,
        ],
        compiler_params=pltpu.CompilerParams(vmem_limit_bytes=24 << 20),
    )(recv)
    run = rows // 8 + 2 * FRINGE
    return pl.pallas_call(
        functools.partial(finish_kernel, dims),
        name="finish",
        out_shape=jax.ShapeDtypeStruct((3, rows, cols), F32),
        in_specs=[anywhere] * 2,
        out_specs=anywhere,
        scratch_shapes=[
            pltpu.VMEM((tiles + 1, ext, LANES), F32),
            *runs,
            pltpu.VMEM((6, tiles + 1, number, ROWS8, LANES), F32),
            pltpu.VMEM((3, tiles, ext, LANES), F32),
            pltpu.VMEM((run, LANES), F32),
            pltpu.VMEM((run, LANES), F32),
            pltpu.VMEM((run, LANES), F32),
            pltpu.VMEM((run, LANES), F32),
            dma((6,)), dma((2, 2)), dma((2, 2)), dma((4, 2)), dma((tiles,)),
        ],
        compiler_params=params(collective_id=1, vmem_limit_bytes=50 << 20),
    )(fields, forcing)


def solution(mesh):
    return jax.shard_map(
        functools.partial(per_device, mesh.shape["lat"], mesh.shape["lon"]),
        mesh=mesh,
        in_specs=(
            P(None, "lat", "lon"),
            P(None, "lat", "lon"),
            P(("lat", "lon"), None),
            P(("lat", "lon"), None, None),
            P(("lat", "lon"), None),
            P(("lat", "lon"), None),
            P(("lat", "lon"), None),
            P(("lat", "lon"), None),
        ),
        out_specs=P(None, "lat", "lon"),
        check_vma=False,
    )
```

```python
import functools

import jax
import jax.numpy as jnp
from jax import lax
from jax.experimental import pallas as pl
from jax.experimental.pallas import tpu as pltpu
from jax.sharding import PartitionSpec as P

WIN = 6
WINDOWS = 4
CAP = 2
LANES = 128
ROWS8 = 8
HALO = WIN * WINDOWS
HALF = HALO // 2
FRINGE = 16
PIECES = 5
GROUP = 8
ROW_BINS = 1
COL_BINS = 2
BINS = ROW_BINS * COL_BINS
UNROLL = 32
IDS = jnp.int16
MESH = pl.DeviceIdType.MESH
F32 = jnp.float32
BF16 = jnp.bfloat16
I32 = jnp.int32


def lane_ids(shape):
    return lax.broadcasted_iota(I32, shape, len(shape) - 1)


def shift_to(me, index, lon):
    where = me + index
    return jnp.where(where >= lon, where - lon, where)


def columns_at(width):
    part = LANES // width
    lane = lane_ids((ROWS8, LANES))
    part_of, inside = lane // part, lane % part
    cuts = [(width * part * t - HALO) % LANES for t in range(width)]
    into = [(width * part * t - HALO + LANES + width * inside + (part_of + width - t) % width) % LANES for t in range(width)]
    turn = [part * ((part_of + c) % width) + inside for c in range(width)]
    back = [part * ((part_of + width - c) % width) + inside for c in range(width)]
    out = []
    for t in range(width):
        along = (lane + LANES - cuts[t]) % LANES
        out.append(jnp.minimum(part * ((along + t) % width) + along // width, LANES - 1))
    return lane, part_of, cuts, into, turn, back, out


def take(values, index):
    return jnp.take_along_axis(values, index, axis=1)


def by_part(part_of, choices):
    value = choices[-1]
    for p in range(len(choices) - 1):
        value = jnp.where(part_of == p, choices[p], value)
    return value


def over(number, body, most):
    size = max(d for d in range(1, number + 1) if number % d == 0 and d <= max(most, 1))

    def one(p, carry):
        for j in range(size):
            body(p * size + j)
        return carry

    lax.fori_loop(0, number // size, one, 0)


def to_runs(maps, natural, temp, number, keep, finished=None):
    lane, part_of, cuts, into, turn, back, out = maps
    width = len(cuts)
    most = 200 // len(natural)
    for t in range(width):
        def sort(k):
            rows = pl.ds(k, ROWS8, stride=number)
            for f, ref in enumerate(natural):
                temp[f, t, k] = take(jnp.where(lane >= cuts[t], ref[(t - 1) % width, rows, :], ref[t, rows, :]), into[t])

        over(number, sort, most)
    for c in range(width):
        def mix(k):
            for f in range(len(natural)):
                value = by_part(part_of, [temp[f, (p - c) % width, k] for p in range(width)])
                keep(f, c, k, take(value, turn[c]) if c else value)

        over(number, mix, most)
        if finished is not None:
            finished(c)


def from_runs(maps, refs, temp, number, natural, finished):
    lane, part_of, cuts, into, turn, back, out = maps
    width, fields = len(cuts), len(refs)
    most = 120 // fields
    for c in range(1, width):
        def unmix(k):
            for f in range(fields):
                temp[f, c, k] = take(refs[f][c, k], back[c])

        over(number, unmix, most)
    for t in range(width):
        def unsort(k):
            for f in range(fields):
                parts = [(p - t) % width for p in range(width)]
                value = by_part(part_of, [temp[f, c, k] if c else refs[f][0, k] for c in parts])
                temp[fields + f, t, k] = take(value, out[t])

        over(number, unsort, most)
        if t:
            def join(k):
                for f in range(fields):
                    value = jnp.where(lane < cuts[t], temp[fields + f, t - 1, k], temp[fields + f, t, k])
                    natural[f, t - 1, pl.ds(k, ROWS8, stride=number), :] = value

            over(number, join, most)
            finished(t - 1)


def one_step(old, new, east_vel, north_vel, depth_east, depth_north):
    width, number = east_vel.shape[:2]
    cols = range(width)
    for c in cols:
        old[c, number] = pltpu.roll(old[c, 0], ROWS8 - 1, 0)
    end = number - 1
    south = [pltpu.roll(north_vel[c, end] + depth_north[c, end] * (old[c, number] - old[c, end]), 1, 0) for c in cols]
    for k in range(number):
        height = [old[c, k] for c in cols]
        height_e = height[1:] + [pltpu.roll(height[0], LANES - 1, 1)]
        east = [None] * width
        for c in [width - 1] + list(range(width - 1)):
            east[c] = east_vel[c, k] + depth_east[c, k] * (height_e[c] - height[c])
        west = [pltpu.roll(east[-1], 1, 1)] + east[:-1]
        north = [None] * width
        for c in cols:
            north[c] = north_vel[c, k] + depth_north[c, k] * (old[c, k + 1] - height[c])
            new[c, k] = height[c] + (east[c] - west[c]) + (north[c] - south[c])
            east_vel[c, k] = east[c]
            north_vel[c, k] = north[c]
        south = north


def steps(number, height, other, *rest):
    def two(_, carry):
        one_step(height, other, *rest)
        one_step(other, height, *rest)
        return carry

    lax.fori_loop(0, number // 2, two, 0)


def route_kernel(dims, state, depth, innov_in, weight_in, tile_in, count_in, row_in, col_in, fields_out, recv,
                 fields, height, east_vel, north_vel, depth_east, depth_north,
                 innov, weight, tile_row, count_row, obs_row, obs_col, spots, cells, ordered, temp, send, east_pack, west_pack, east_got, west_got,
                 load_sem, small_sem, row_sem, pack_sem, corner_sem, a2a_sem, own_sem, store_sem):
    rows, cols, lat, lon, blocks = dims
    tiles = cols // LANES
    ext = rows + 2 * HALO
    number = ext // ROWS8
    my_lat, my_lon = lax.axis_index("lat"), lax.axis_index("lon")
    east, west = lax.rem(my_lon + 1, lon), lax.rem(my_lon + lon - 1, lon)
    has_north, has_south = my_lat < lat - 1, my_lat > 0

    small = [pltpu.make_async_copy(source, target, small_sem.at[i]) for i, (source, target) in enumerate((
        (tile_in, tile_row), (count_in, count_row), (innov_in, innov), (weight_in, weight), (row_in, obs_row), (col_in, obs_col)))]
    for load in small:
        load.start()
    loads = []
    for t in range(tiles):
        span = pl.ds(t * LANES, LANES)
        for source, start, some in ((state, 0, 3), (depth, 3, 2)):
            loads.append(pltpu.make_async_copy(
                source.at[:, :, span], fields.at[pl.ds(start, some), t, pl.ds(HALO, rows), :], load_sem.at[len(loads)]))
    for load in loads:
        load.start()

    barrier = pltpu.get_barrier_semaphore()

    def greet(index, carry):
        pl.semaphore_signal(barrier, inc=1, device_id=(my_lat, shift_to(my_lon, index, lon)), device_id_type=MESH)
        return carry

    for has, where in ((has_north, my_lat + 1), (has_south, my_lat - 1)):
        @pl.when(has)
        def _():
            for column in (west, my_lon, east):
                pl.semaphore_signal(barrier, inc=1, device_id=(where, column), device_id_type=MESH)
    lax.fori_loop(1, lon, greet, 0, unroll=max(d for d in range(1, 10) if (lon - 1) % d == 0))

    for load in small:
        load.wait()
    slots = innov.shape[1]
    square = (blocks, blocks)
    diagonal = lax.broadcasted_iota(I32, square, 0) == lane_ids(square)
    tile = jnp.sum(jnp.where(diagonal, tile_row[...].astype(F32), 0.0), axis=1, keepdims=True)
    count = jnp.sum(jnp.where(diagonal, count_row[...].astype(F32), 0.0), axis=1, keepdims=True)
    live = lane_ids((blocks, slots)).astype(F32) < count
    bin_rows, bin_cols = rows // ROW_BINS, cols // COL_BINS
    row_at, col_at = obs_row[...], obs_col[...]
    bin_at = row_at // bin_rows * COL_BINS + col_at // bin_cols
    cell = (bin_at * bin_rows + row_at % bin_rows) * bin_cols + col_at % bin_cols + 1
    member = [jnp.where(jnp.logical_and(live, bin_at == b), 1.0, 0.0) for b in range(BINS)]
    to_left = jnp.where(lax.broadcasted_iota(I32, (slots, slots), 0) < lane_ids((slots, slots)), 1.0, 0.0).astype(BF16)
    ahead = jnp.dot(jnp.concatenate(member, axis=0).astype(BF16), to_left, preferred_element_type=F32)
    begin = jnp.ones((blocks, 1), F32)
    spot = jnp.zeros((blocks, slots), F32)
    for b in range(BINS):
        spot += member[b] * (ahead[b * blocks:(b + 1) * blocks] + begin)
        begin += jnp.sum(member[b], axis=1, keepdims=True)
    spots[...] = spot
    innov[...] = jnp.where(live, innov[...], 0.0)
    cells[...] = jnp.where(live, cell, 0).astype(F32)
    ranks = (lax.broadcasted_iota(I32, (slots, slots), 0) + 1).astype(F32)
    sub = lax.broadcasted_iota(I32, (ROWS8 - 4, slots), 0)

    def order(b, carry):
        move = jnp.where(ranks == spots[pl.ds(b, 1), :], 1.0, 0.0).astype(BF16)
        values = weight[b] * innov[pl.ds(b, 1), :]
        data = jnp.concatenate([values, jnp.where(sub == 0, cells[pl.ds(b, 1), :], 0.0)], axis=0)
        high = data.astype(BF16).astype(F32)
        mid = (data - high).astype(BF16).astype(F32)
        parts = jnp.concatenate([high, mid, data - high - mid], axis=0).astype(BF16)
        moved = lax.dot_general(parts, move, (((1,), (1,)), ((), ())), preferred_element_type=F32)
        ordered[pl.ds(pl.multiple_of(b * ROWS8, ROWS8), ROWS8), :] = moved[:ROWS8] + moved[ROWS8:2 * ROWS8] + moved[2 * ROWS8:]
        return carry

    lax.fori_loop(0, blocks, order, 0, unroll=max(d for d in range(1, 17) if blocks % d == 0))
    named = jnp.where(tile == lane_ids((blocks, lon)).astype(F32), 1.0, 0.0)
    earlier = jnp.where(lax.broadcasted_iota(I32, square, 0) > lane_ids(square), 1.0, 0.0)
    before = jnp.dot(earlier.astype(BF16), named.astype(BF16), preferred_element_type=F32)
    rank = jnp.sum(before * named, axis=1, keepdims=True)
    place = tile * CAP + rank
    wide = (blocks, ROWS8 * blocks)
    ids = lane_ids(wide)
    row_of = jnp.where(lax.broadcasted_iota(I32, wide, 0) == ids // ROWS8, place * ROWS8 + (ids % ROWS8).astype(F32), 0.0)
    row_of = jnp.sum(row_of, axis=0, keepdims=True)
    pick = lax.broadcasted_iota(I32, (CAP * lon * ROWS8, ROWS8 * blocks), 0).astype(F32) == row_of
    pick = jnp.where(pick, 1.0, 0.0).astype(BF16)
    data = ordered[...]
    high = data.astype(BF16)
    rest = data - high.astype(F32)
    mid = rest.astype(BF16)
    low = (rest - mid.astype(F32)).astype(BF16)
    sent = (jnp.dot(pick, high, preferred_element_type=F32) + jnp.dot(pick, mid, preferred_element_type=F32)
            + jnp.dot(pick, low, preferred_element_type=F32))
    send[...] = sent.reshape(CAP * lon, ROWS8, slots)[:, :PIECES, :]

    zero_rows = jnp.zeros((5, tiles, HALO, LANES), F32)

    @pl.when(jnp.logical_not(has_south))
    def _():
        fields[:, pl.ds(0, tiles), pl.ds(0, HALO), :] = zero_rows
        east_got[pl.ds(0, HALO), :] = zero_rows[0, 0]
        west_got[pl.ds(0, HALO), :] = zero_rows[0, 0]

    @pl.when(jnp.logical_not(has_north))
    def _():
        fields[:, pl.ds(0, tiles), pl.ds(HALO + rows, HALO), :] = zero_rows
        east_got[pl.ds(HALO + rows, HALO), :] = zero_rows[0, 0]
        west_got[pl.ds(HALO + rows, HALO), :] = zero_rows[0, 0]

    for load in loads:
        load.wait()

    @pl.when(jnp.logical_not(has_north))
    def _():
        wall = pl.ds(HALO + rows - ROWS8, ROWS8)
        keep = lax.broadcasted_iota(I32, (tiles, ROWS8, LANES), 1) < ROWS8 - 1
        fields[4, pl.ds(0, tiles), wall, :] = jnp.where(keep, fields[4, pl.ds(0, tiles), wall, :], 0.0)

    lane = lane_ids((ROWS8, LANES))

    def pack(index, carry):
        base = pl.multiple_of(index * ROWS8, ROWS8)
        here = pl.ds(HALO + base, ROWS8)
        to_west = jnp.zeros((ROWS8, LANES), F32)
        to_east = to_west
        for f in range(5):
            first = HALO * f
            inside = jnp.logical_and(lane >= first, lane < first + HALO)
            to_west = jnp.where(inside, pltpu.roll(fields[f, 0, here, :], first, 1) if f else fields[f, 0, here, :], to_west)
            first = (LANES - HALO + HALO * f) % LANES
            inside = jnp.logical_and(lane >= first, lane < first + HALO)
            value = fields[f, tiles - 1, here, :]
            to_east = jnp.where(inside, pltpu.roll(value, HALO * f, 1) if f else value, to_east)
        west_pack[pl.ds(base, ROWS8), :] = to_west
        east_pack[pl.ds(base, ROWS8), :] = to_east
        return carry

    lax.fori_loop(0, rows // ROWS8, pack, 0, unroll=8)

    pl.semaphore_wait(barrier, lon - 1 + 3 * has_north.astype(I32) + 3 * has_south.astype(I32))

    def remote(source, target, sems, where):
        return pltpu.make_async_remote_copy(src_ref=source, dst_ref=target, send_sem=sems.at[0], recv_sem=sems.at[1],
                                            device_id=where, device_id_type=MESH)

    main = pl.ds(HALO, rows)
    low_rows, high_rows = pl.ds(0, HALO), pl.ds(HALO + rows, HALO)
    inner = pl.ds(0, tiles)
    to_north = remote(fields.at[:, inner, pl.ds(rows, HALO), :], fields.at[:, inner, low_rows, :], row_sem.at[0], (my_lat + 1, my_lon))
    to_south = remote(fields.at[:, inner, pl.ds(HALO, HALO), :], fields.at[:, inner, high_rows, :], row_sem.at[1], (my_lat - 1, my_lon))
    to_east = remote(east_pack, west_got.at[main], pack_sem.at[0], (my_lat, east))
    to_west = remote(west_pack, east_got.at[main], pack_sem.at[1], (my_lat, west))
    tail = pl.ds(rows - HALO, HALO)
    north_east = remote(east_pack.at[tail], west_got.at[low_rows], corner_sem.at[0], (my_lat + 1, east))
    north_west = remote(west_pack.at[tail], east_got.at[low_rows], corner_sem.at[1], (my_lat + 1, west))
    south_east = remote(east_pack.at[low_rows], west_got.at[high_rows], corner_sem.at[2], (my_lat - 1, east))
    south_west = remote(west_pack.at[low_rows], east_got.at[high_rows], corner_sem.at[3], (my_lat - 1, west))
    northward, southward = (to_north, north_east, north_west), (to_south, south_east, south_west)

    @pl.when(has_north)
    def _():
        for copy in northward:
            copy.start()

    @pl.when(has_south)
    def _():
        for copy in southward:
            copy.start()

    to_east.start()
    to_west.start()

    def block_copy(index):
        where = shift_to(my_lon, index, lon)
        return remote(send.at[pl.ds(CAP * where, CAP)], recv.at[pl.ds(CAP * my_lon, CAP)], a2a_sem, (my_lat, where))

    def send_blocks(index, carry):
        block_copy(index).start()
        return carry

    lax.fori_loop(1, lon, send_blocks, 0, unroll=max(d for d in range(1, 10) if (lon - 1) % d == 0))
    mine = pl.ds(CAP * my_lon, CAP)
    own = pltpu.make_async_copy(send.at[mine], recv.at[mine], own_sem)
    own.start()

    @pl.when(has_south)
    def _():
        for copy in northward:
            copy.wait_recv()

    @pl.when(has_north)
    def _():
        for copy in southward:
            copy.wait_recv()

    to_east.wait_recv()
    to_west.wait_recv()

    def unpack(index):
        here = pl.ds(pl.multiple_of(index * ROWS8, ROWS8), ROWS8)
        from_east, from_west = east_got[here, :], west_got[here, :]
        for f in range(5):
            first = HALO * f
            right = jnp.logical_and(lane >= first, lane < first + HALO)
            first = (LANES - HALO + HALO * f) % LANES
            left = jnp.logical_and(lane >= first, lane < first + HALO)
            both = jnp.where(right, from_east, jnp.where(left, from_west, 0.0))
            fields[f, tiles, here, :] = pltpu.roll(both, LANES - HALO * f, 1) if f else both

    over(ext // ROWS8, unpack, 19)

    @pl.when(has_north)
    def _():
        for copy in northward:
            copy.wait_send()

    @pl.when(has_south)
    def _():
        for copy in southward:
            copy.wait_send()

    to_east.wait_send()
    to_west.wait_send()

    refs = (height, east_vel, north_vel, depth_east, depth_north)
    maps = columns_at(tiles + 1)

    stores = []

    def keep(f, c, k, value):
        refs[f][c, k] = value

    def finished(c):
        for f, ref in enumerate(refs):
            stores.append(pltpu.make_async_copy(ref.at[c, pl.ds(0, number)], fields_out.at[f, c], store_sem.at[f, c]))
            stores[-1].start()

    to_runs(maps, [fields.at[f] for f in range(5)], temp, number, keep, finished)
    own.wait()
    others = pl.ds(0, CAP * (lon - 1))
    every = pltpu.make_async_remote_copy(src_ref=send.at[others], dst_ref=recv.at[others], send_sem=a2a_sem.at[0],
                                         recv_sem=a2a_sem.at[1], device_id=(my_lat, east), device_id_type=MESH)
    every.wait_recv()
    every.wait_send()
    for store in stores:
        store.wait()


def spread_kernel(dims, recv, out, counts, found, packed, total, left_a, left_b, right_a, right_b, load_sem):
    rows, cols, lat, lon, blocks = dims
    tiles = cols // LANES
    segments = CAP * lon
    bin_rows, bin_cols = rows // ROW_BINS, cols // COL_BINS
    bins = ROW_BINS * COL_BINS
    padded = left_a.shape[0] // 2
    depth = GROUP * LANES
    room = segments + GROUP
    cell = recv[:, PIECES - 1, :]
    ones = jnp.ones((ROWS8, LANES), BF16)
    area = float(bin_rows * bin_cols)
    for b in range(bins):
        within = jnp.logical_and(cell > b * area, cell <= (b + 1) * area)
        live_of = lax.dot_general(ones, jnp.where(within, 1.0, 0.0).astype(BF16), (((1,), (1,)), ((), ())), preferred_element_type=F32)
        found[pl.ds(b, 1), :] = live_of[:1].astype(I32)
    found[pl.ds(bins, ROWS8 - bins), :] = jnp.zeros((ROWS8 - bins, segments), I32)
    load = pltpu.make_async_copy(found, counts, load_sem)
    load.start()
    total[...] = jnp.zeros_like(total)
    load.wait()
    lane = lane_ids((PIECES, LANES))
    zero = jnp.zeros((PIECES, LANES), F32)

    def append(segment, carry):
        block = recv[segment]
        begin = 0
        after = []
        for b, (fill, current) in enumerate(carry):
            number = counts[b, segment]
            chunk = lax.shift_right_logical(fill, 7)
            turned = pltpu.roll(block, (fill - begin) & (LANES - 1), 1)
            current = jnp.where(lane >= (fill & (LANES - 1)), turned, current)
            packed[chunk + b * room] = current
            begin = begin + number
            fill = fill + number
            after.append((fill, jnp.where(lax.shift_right_logical(fill, 7) > chunk, turned, current)))
        return tuple(after)

    filled = lax.fori_loop(0, segments, append, ((jnp.int32(0), zero),) * bins, unroll=min(UNROLL, segments))
    jobs, starts = [], [0]
    for b, (fill, current) in enumerate(filled):
        chunk = lax.shift_right_logical(fill, 7) + b * room
        packed[chunk] = jnp.where(lane < (fill & (LANES - 1)), current, 0.0)
        for extra in range(1, GROUP):
            packed[chunk + extra] = zero
        starts.append(starts[-1] + (fill + depth - 1) // depth)
    for extra in range(GROUP):
        packed[bins * room + extra] = zero
    count = starts[-1]

    def place(job):
        which = 0
        begin = 0
        for b in range(1, bins):
            past = job >= starts[b]
            which = jnp.where(past, b, which)
            begin = jnp.where(past, starts[b], begin)
        chunk = which * room + (job - begin) * GROUP
        return jnp.where(job < count, chunk, bins * room), jnp.where(job < count, which, 0)

    row_ids = lax.broadcasted_iota(IDS, (padded, depth), 0)
    col_ids = lax.broadcasted_iota(IDS, (bin_cols, depth), 0)
    one, none = jnp.array(1, BF16), jnp.array(0, BF16)

    def build(job, left, right):
        chunk, which = place(job)
        both = jnp.concatenate([packed[chunk + j] for j in range(GROUP)], axis=1)
        cell = both[4:5, :].astype(I32) - 1 - which * (bin_rows * bin_cols)
        row_at = cell // bin_cols if bin_cols & (bin_cols - 1) else lax.shift_right_arithmetic(cell, bin_cols.bit_length() - 1)
        col_at = cell - row_at * bin_cols

        def wide(value, kind, number):
            return jnp.broadcast_to(value, (number, depth)).astype(kind)

        here = row_ids == wide(row_at, IDS, padded)
        past = row_ids == wide(row_at + 1, IDS, padded)
        column = jnp.where(col_ids == wide(col_at, IDS, bin_cols), one, none)
        right[:, :depth] = column
        right[:, depth:] = column
        high = both[:4, :].astype(BF16).astype(F32)
        for part, values in enumerate((high, both[:4, :] - high)):
            for side in range(2):
                at = wide(values[side:side + 1, :], BF16, padded)
                above = wide(values[side + 2:side + 3, :], BF16, padded)
                left[pl.ds(side * padded, padded), pl.ds(part * depth, depth)] = jnp.where(here, at, jnp.where(past, above, none))

    def add(job, left, right):
        _, which = place(job)
        total[which] += lax.dot_general(left[...], right[...], (((1,), (1,)), ((), ())), preferred_element_type=F32)

    build(0, left_a, right_a)

    def pair(index, carry):
        build(2 * index + 1, left_b, right_b)
        add(2 * index, left_a, right_a)
        build(2 * index + 2, left_a, right_a)
        add(2 * index + 1, left_b, right_b)
        return carry

    lax.fori_loop(0, (count + 1) // 2, pair, 0)

    bin_tiles = bin_cols // LANES
    lane = lane_ids((bin_rows, LANES))
    for i in range(ROW_BINS):
        if i:
            for j in range(COL_BINS):
                for at in (0, padded):
                    total[i * COL_BINS + j, pl.ds(at, ROWS8), :] += total[(i - 1) * COL_BINS + j, pl.ds(at + bin_rows, ROWS8), :]
        before = jnp.zeros((bin_rows, LANES), F32)
        for t in range(tiles):
            which, span = i * COL_BINS + t // bin_tiles, pl.ds(t % bin_tiles * LANES, LANES)
            turned = pltpu.roll(total[which, pl.ds(padded, bin_rows), span], 1, 1)
            out[t, pl.ds(i * bin_rows, bin_rows), :] = total[which, pl.ds(0, bin_rows), span] + jnp.where(lane == 0, before, turned)
            before = turned


def finish_kernel(dims, fields_in, forcing_in, out, forcing, height, other, east_vel, north_vel, depth_east, depth_north, temp, done,
                  east_pack, west_pack, east_got, west_got, load_sem, row_sem, pack_sem, corner_sem, store_sem):
    rows, cols, lat, lon, blocks = dims
    tiles = cols // LANES
    ext = rows + 2 * HALO
    number = ext // ROWS8
    my_lat, my_lon = lax.axis_index("lat"), lax.axis_index("lon")
    east, west = lax.rem(my_lon + 1, lon), lax.rem(my_lon + lon - 1, lon)
    has_north, has_south = my_lat < lat - 1, my_lat > 0
    refs = (height, east_vel, north_vel, depth_east, depth_north)
    inner = pl.ds(0, number)
    loads = [pltpu.make_async_copy(forcing_in, forcing.at[pl.ds(0, tiles), pl.ds(HALO, rows), :], load_sem.at[5])]
    loads += [pltpu.make_async_copy(fields_in.at[f], ref.at[:, inner], load_sem.at[f]) for f, ref in enumerate(refs)]
    for load in loads:
        load.start()
    barrier = pltpu.get_barrier_semaphore()
    for has, where in ((has_north, my_lat + 1), (has_south, my_lat - 1)):
        @pl.when(has)
        def _():
            for column in (west, my_lon, east):
                pl.semaphore_signal(barrier, inc=1, device_id=(where, column), device_id_type=MESH)
    for column in (west, east):
        pl.semaphore_signal(barrier, inc=1, device_id=(my_lat, column), device_id_type=MESH)

    beyond = HALO - FRINGE
    for at in (0, ext - beyond):
        forcing[:, pl.ds(at, beyond), :] = jnp.zeros((tiles + 1, beyond, LANES), F32)
    for has, at in ((has_south, beyond), (has_north, HALO + rows)):
        @pl.when(jnp.logical_not(has))
        def _():
            forcing[:, pl.ds(at, FRINGE), :] = jnp.zeros((tiles + 1, FRINGE, LANES), F32)

    loads[0].wait()
    run = rows // 8
    lane = lane_ids((run, LANES))
    to_west = jnp.zeros((run, LANES), F32)
    to_east = to_west
    for g in range(8):
        here = pl.ds(HALO + run * g, run)
        inside = lane // FRINGE == g
        value = forcing[0, here, :]
        to_west = jnp.where(inside, pltpu.roll(value, FRINGE * g, 1) if g else value, to_west)
        value = forcing[tiles - 1, here, :]
        to_east = jnp.where(inside, pltpu.roll(value, (FRINGE * (g + 1)) % LANES, 1) if g < 7 else value, to_east)
    west_pack[pl.ds(0, run), :] = to_west
    east_pack[pl.ds(0, run), :] = to_east
    ends = (pl.ds(HALO, FRINGE), pl.ds(HALO + rows - FRINGE, FRINGE))
    outer = (pl.ds(HALO - FRINGE, FRINGE), pl.ds(HALO + rows, FRINGE))
    for at, here in zip((run, run + FRINGE), ends):
        west_pack[pl.ds(at, FRINGE), :] = forcing[0, here, :]
        east_pack[pl.ds(at, FRINGE), :] = forcing[tiles - 1, here, :]

    pl.semaphore_wait(barrier, 2 + 3 * has_north.astype(I32) + 3 * has_south.astype(I32))

    def remote(source, target, sems, where):
        return pltpu.make_async_remote_copy(src_ref=source, dst_ref=target, send_sem=sems.at[0], recv_sem=sems.at[1],
                                            device_id=where, device_id_type=MESH)

    main = pl.ds(0, tiles)
    strip, low_end, high_end = pl.ds(0, run), pl.ds(run, FRINGE), pl.ds(run + FRINGE, FRINGE)
    to_north = remote(forcing.at[main, ends[1], :], forcing.at[main, outer[0], :], row_sem.at[0], (my_lat + 1, my_lon))
    to_south = remote(forcing.at[main, ends[0], :], forcing.at[main, outer[1], :], row_sem.at[1], (my_lat - 1, my_lon))
    go_east = remote(east_pack.at[strip], west_got.at[strip], pack_sem.at[0], (my_lat, east))
    go_west = remote(west_pack.at[strip], east_got.at[strip], pack_sem.at[1], (my_lat, west))
    north_east = remote(east_pack.at[high_end], west_got.at[low_end], corner_sem.at[0], (my_lat + 1, east))
    north_west = remote(west_pack.at[high_end], east_got.at[low_end], corner_sem.at[1], (my_lat + 1, west))
    south_east = remote(east_pack.at[low_end], west_got.at[high_end], corner_sem.at[2], (my_lat - 1, east))
    south_west = remote(west_pack.at[low_end], east_got.at[high_end], corner_sem.at[3], (my_lat - 1, west))
    northward, southward = (to_north, north_east, north_west), (to_south, south_east, south_west)

    @pl.when(has_north)
    def _():
        for copy in northward:
            copy.start()

    @pl.when(has_south)
    def _():
        for copy in southward:
            copy.start()

    go_east.start()
    go_west.start()

    for load in loads[1:]:
        load.wait()
    steps(HALF, height, other, *refs[1:])

    @pl.when(has_south)
    def _():
        for copy in northward:
            copy.wait_recv()

    @pl.when(has_north)
    def _():
        for copy in southward:
            copy.wait_recv()

    go_east.wait_recv()
    go_west.wait_recv()
    right = lane < FRINGE
    left = lane >= LANES - FRINGE
    from_east, from_west = east_got[strip, :], west_got[strip, :]
    for g in range(8):
        here = pl.ds(HALO + run * g, run)
        one = pltpu.roll(from_east, (LANES - FRINGE * g) % LANES, 1) if g else from_east
        two = pltpu.roll(from_west, (LANES - FRINGE * (g + 1)) % LANES, 1) if g < 7 else from_west
        forcing[tiles, here, :] = jnp.where(right, one, jnp.where(left, two, 0.0))
    lane = lane_ids((FRINGE, LANES))
    right = lane < FRINGE
    left = lane >= LANES - FRINGE
    for has, end, at in ((has_south, low_end, HALO - FRINGE), (has_north, high_end, HALO + rows)):
        @pl.when(has)
        def _():
            forcing[tiles, pl.ds(at, FRINGE), :] = jnp.where(right, east_got[end, :], jnp.where(left, west_got[end, :], 0.0))

    maps = columns_at(tiles + 1)

    def keep(f, c, k, value):
        height[c, k] += value

    to_runs(maps, [forcing], temp, number, keep)
    steps(HALF, height, other, *refs[1:])
    stores = []

    def finished(t):
        store = pltpu.make_async_copy(done.at[:, t, pl.ds(HALO, rows), :], out.at[:, :, pl.ds(t * LANES, LANES)], store_sem.at[t])
        store.start()
        stores.append(store)

    from_runs(maps, refs[:3], temp, number, done, finished)

    @pl.when(has_north)
    def _():
        for copy in northward:
            copy.wait_send()

    @pl.when(has_south)
    def _():
        for copy in southward:
            copy.wait_send()

    go_east.wait_send()
    go_west.wait_send()
    for store in stores:
        store.wait()


def per_device(lat, lon, adjoint_state, face_depth, innovation, interp_weight, block_tile, block_count, obs_row, obs_col):
    rows, cols = adjoint_state.shape[1:]
    blocks, slots = innovation.shape
    tiles = cols // LANES
    dims = (rows, cols, lat, lon, blocks)
    ext = rows + 2 * HALO
    segments = CAP * lon
    vmem = pl.BlockSpec(memory_space=pltpu.VMEM)
    anywhere = pl.BlockSpec(memory_space=pl.ANY)
    dma = pltpu.SemaphoreType.DMA
    number = ext // ROWS8
    natural = pltpu.VMEM((5, tiles + 1, ext, LANES), F32)
    runs = [pltpu.VMEM((tiles + 1, number + 1, ROWS8, LANES), F32)] * 2 + [pltpu.VMEM((tiles + 1, number, ROWS8, LANES), F32)] * 4
    params = functools.partial(pltpu.CompilerParams, has_side_effects=True)
    fields, recv = pl.pallas_call(
        functools.partial(route_kernel, dims),
        name="route",
        out_shape=(
            jax.ShapeDtypeStruct((5, tiles + 1, number, ROWS8, LANES), F32),
            jax.ShapeDtypeStruct((segments, PIECES, slots), F32),
        ),
        in_specs=[anywhere] * 8,
        out_specs=(anywhere, anywhere),
        scratch_shapes=[
            natural, *runs[1:],
            pltpu.VMEM((blocks, slots), F32),
            pltpu.VMEM((blocks, 4, slots), F32),
            pltpu.VMEM((1, blocks), I32),
            pltpu.VMEM((1, blocks), I32),
            pltpu.VMEM((blocks, slots), I32),
            pltpu.VMEM((blocks, slots), I32),
            pltpu.VMEM((blocks, slots), F32),
            pltpu.VMEM((blocks, slots), F32),
            pltpu.VMEM((ROWS8 * blocks, slots), F32),
            pltpu.VMEM((5, tiles + 1, number, ROWS8, LANES), F32),
            pltpu.VMEM((segments, PIECES, slots), F32),
            pltpu.VMEM((rows, LANES), F32),
            pltpu.VMEM((rows, LANES), F32),
            pltpu.VMEM((ext, LANES), F32),
            pltpu.VMEM((ext, LANES), F32),
            dma((2 * tiles,)), dma((6,)), dma((2, 2)), dma((2, 2)), dma((4, 2)), dma((2,)), dma, dma((5, tiles + 1)),
        ],
        compiler_params=params(collective_id=0, vmem_limit_bytes=56 << 20),
    )(adjoint_state, face_depth, innovation, interp_weight, block_tile.reshape(1, blocks), block_count.reshape(1, blocks),
      obs_row, obs_col)
    padded = rows if ROW_BINS == 1 else rows // ROW_BINS + 16
    forcing = pl.pallas_call(
        functools.partial(spread_kernel, dims),
        name="spread",
        out_shape=jax.ShapeDtypeStruct((tiles, rows, LANES), F32),
        in_specs=[vmem],
        out_specs=vmem,
        scratch_shapes=[
            pltpu.SMEM((ROWS8, segments), I32),
            pltpu.VMEM((ROWS8, segments), I32),
            pltpu.VMEM((BINS * (segments + GROUP) + GROUP, PIECES, LANES), F32),
            pltpu.VMEM((BINS, 2 * padded, cols // COL_BINS), F32),
            *[pltpu.VMEM((2 * padded, 2 * GROUP * LANES), BF16)] * 2,
            *[pltpu.VMEM((cols // COL_BINS, 2 * GROUP * LANES), BF16)] * 2,
            dma,
        ],
        compiler_params=pltpu.CompilerParams(vmem_limit_bytes=24 << 20),
    )(recv)
    run = rows // 8 + 2 * FRINGE
    return pl.pallas_call(
        functools.partial(finish_kernel, dims),
        name="finish",
        out_shape=jax.ShapeDtypeStruct((3, rows, cols), F32),
        in_specs=[anywhere] * 2,
        out_specs=anywhere,
        scratch_shapes=[
            pltpu.VMEM((tiles + 1, ext, LANES), F32),
            *runs,
            pltpu.VMEM((6, tiles + 1, number, ROWS8, LANES), F32),
            pltpu.VMEM((3, tiles, ext, LANES), F32),
            pltpu.VMEM((run, LANES), F32),
            pltpu.VMEM((run, LANES), F32),
            pltpu.VMEM((run, LANES), F32),
            pltpu.VMEM((run, LANES), F32),
            dma((6,)), dma((2, 2)), dma((2, 2)), dma((4, 2)), dma((tiles,)),
        ],
        compiler_params=params(collective_id=1, vmem_limit_bytes=50 << 20),
    )(fields, forcing)


def solution(mesh):
    return jax.shard_map(
        functools.partial(per_device, mesh.shape["lat"], mesh.shape["lon"]),
        mesh=mesh,
        in_specs=(
            P(None, "lat", "lon"),
            P(None, "lat", "lon"),
            P(("lat", "lon"), None),
            P(("lat", "lon"), None, None),
            P(("lat", "lon"), None),
            P(("lat", "lon"), None),
            P(("lat", "lon"), None),
            P(("lat", "lon"), None),
        ),
        out_specs=P(None, "lat", "lon"),
        check_vma=False,
    )
```
